32 devices in a mesh: seq: 8 (over y, x, core), batch: 4 (over z).
Axes of the slice: x: 2, y: 2, z: 4, core: 2. Of those that a mesh axis runs over, the one named last changes fastest.
Arguments:
- frames_in: bfloat16 [4, 3072, 1024], P('batch', 'seq'), may hold values from -6 to 6
- skip_in: bfloat16 [4, 3072, 1024], P('batch', 'seq'), may hold values from -6 to 6
- time_table: bfloat16 [32, 1024], P(None, ('seq', 'batch')), may hold values from -6 to 6
- timestep: int32 [4, 3], P('batch'), may hold values from 0 to 31
- lengths: int32 [4, 3], P('batch'), may hold values from 1 to 2690, as said below
- span_start: int32 [4, 3], P('batch'), may hold values from 0 to 807, as said below
- span_len: int32 [4, 3], P('batch'), may hold values from 1 to 1883, as said below
- skip_proj: bfloat16 [2048, 1024], P(('seq', 'batch')), may hold values from -0.125 to 0.125
- mod_proj: bfloat16 [1024, 4096], P(('seq', 'batch')), may hold values from -0.1875 to 0.1875
- mod_bias: bfloat16 [4096], P(('seq', 'batch')), may hold values from -1.796875 to 1.796875
- qkv_proj: bfloat16 [1024, 3072], P(('seq', 'batch')), may hold values from -0.1875 to 0.1875
- out_proj: bfloat16 [1024, 1024], P(('seq', 'batch')), may hold values from -0.75 to 0.75
- up_proj: bfloat16 [1024, 4096], P(('seq', 'batch')), may hold values from -0.1875 to 0.1875
- up_bias: bfloat16 [4096], P(('seq', 'batch')), may hold values from -3 to 3
- down_proj: bfloat16 [4096, 1024], P(('seq', 'batch')), may hold values from -0.09375 to 0.09375
- cotangent: bfloat16 [4, 3072, 1024], P('batch', 'seq'), may hold values from -6 to 6
Outputs:
- block_out: bfloat16 [4, 3072, 1024], P('batch', 'seq')
- grad_frames: bfloat16 [4, 3072, 1024], P('batch', 'seq')
- grad_skip: bfloat16 [4, 3072, 1024], P('batch', 'seq')
- grad_time: float32 [32, 1024], P(None, ('seq', 'batch'))
- grad_skip_proj: float32 [2048, 1024], P(('seq', 'batch'))
- grad_mod_proj: float32 [1024, 4096], P(('seq', 'batch'))
- grad_mod_bias: float32 [4096], P(('seq', 'batch'))
- grad_qkv_proj: float32 [1024, 3072], P(('seq', 'batch'))
- grad_out_proj: float32 [1024, 1024], P(('seq', 'batch'))
- grad_up_proj: float32 [1024, 4096], P(('seq', 'batch'))
- grad_up_bias: float32 [4096], P(('seq', 'batch'))
- grad_down_proj: float32 [4096, 1024], P(('seq', 'batch'))
The draws below stay inside these ranges and needn't reach their ends.
Inputs may be any that keep to these rules, and one draw needn't show every extreme that they name: In each group the 3 lengths sum to 3072; the longest utterance starts before frame 384 of its group and ends after frame 3072 - 384. span_start + span_len is at most the utterance's length. `span_len`: at least 70 percent of the utterance's length, rounded down, and at least 1.
All inputs are finite; a program needn't handle non-finite values.
Results may differ from the reference program's by a relative error of at most 0.018.
The reference program's roundings to bfloat16 on the way count: a program that leaves them out, or rounds other values in their place, can miss the bound.
Values may be sent and summed in bfloat16 or wider, within the bound.
No kernel may reach another device: no remote copies, remote signals or barrier semaphores. Data moves between devices by JAX's collectives and lax.ppermute only.
A program may use at most 320 MiB of HBM per device.

```python
import math
import jax
import jax.numpy as jnp
from jax import lax

D = 1024
HEADS = 16
FF = 4096
TOK_DEV = 384
UTT = 3
NSTEP = 32
FRAMES = 3072
GROUPS = 4


def plan_lengths(key):
    offset_key, place_key = jax.random.split(key)
    middle = max((TOK_DEV - 1) // (UTT - 1), 1)
    reach = (middle - 1) // 2
    offsets = jax.random.randint(offset_key, (GROUPS, UTT - 1), 0, reach + 1, dtype=jnp.int32)
    shorts = (middle + offsets - jnp.roll(offsets, -1, axis=1)).astype(jnp.int32)
    place = jax.random.randint(place_key, (GROUPS, 1), 0, UTT, dtype=jnp.int32)
    slot_ids = jnp.arange(UTT, dtype=jnp.int32)[None, :]
    source = jnp.clip(slot_ids - (slot_ids > place).astype(jnp.int32), 0, UTT - 2)
    picked = jnp.take_along_axis(shorts, source, axis=1)
    longest = FRAMES - (UTT - 1) * middle
    is_long = slot_ids == place
    return (jnp.where(is_long, longest, picked).astype(jnp.int32), is_long)


def plan_spans(key):
    utt_lengths, is_long = plan_lengths(key)
    share_key, start_key = jax.random.split(jax.random.fold_in(key, 7))
    share = jax.random.randint(share_key, (GROUPS, UTT), 70, 101, dtype=jnp.int32)
    share = jnp.where(is_long, 70, share)
    span_sizes = jnp.maximum(utt_lengths * share // 100, 1).astype(jnp.int32)
    span_begins = jax.random.randint(start_key, (GROUPS, UTT), 0, utt_lengths - span_sizes + 1, dtype=jnp.int32)
    span_begins = jnp.where(is_long, utt_lengths - span_sizes, span_begins).astype(jnp.int32)
    return (span_begins, span_sizes)


def draw_lengths(key, part):
    return plan_lengths(key)[0]


def draw_span_start(key, part):
    return plan_spans(key)[0]


def draw_span_len(key, part):
    return plan_spans(key)[1]


def plant(array, key, least, top_value):
    spot = [jax.random.randint(jax.random.fold_in(key, axis), (), 0, length) for axis, length in enumerate(array.shape)]
    widest = array.shape.index(max(array.shape))
    next_to = spot[:widest] + [(spot[widest] + 1) % array.shape[widest]] + spot[widest + 1:]
    return array.at[tuple(spot)].set(least).at[tuple(next_to)].set(top_value)


def level_of(stream_key, extent, shards, low, top_value):
    def one(axis_at, parts):
        heights = jax.random.uniform(jax.random.fold_in(jax.random.fold_in(stream_key, 6), axis_at), (parts,), jnp.float32, low / len(shards), top_value / len(shards))
        return jnp.repeat(jnp.exp(heights), extent[axis_at] // parts).reshape((-1,) + (1,) * (len(extent) - axis_at - 1))

    loudness = one(*shards[0])
    for cut in shards[1:]:
        loudness = loudness * one(*cut)
    return loudness


def noise(rng, shape, scale, bound, cuts=(), held_as=jnp.bfloat16):
    entries = scale * jax.random.normal(rng, shape, jnp.float32)
    if cuts:
        entries = entries * level_of(rng, shape, cuts, -0.22, 0.18)
    return jnp.clip(entries, -bound, bound).astype(held_as)


def setup_inputs(seed: int = 0) -> dict:
    keys = jax.random.split(jax.random.key(seed), 17)
    return {
        "frames_in": noise(keys[0], (GROUPS, FRAMES, D), 1.0, 6.0, ((0, 4), (1, 8))),
        "skip_in": noise(keys[1], (GROUPS, FRAMES, D), 1.0, 6.0, ((0, 4), (1, 8))),
        "time_table": noise(keys[2], (NSTEP, D), 1.0, 6.0, ((1, 32),)),
        "timestep": plant(jax.random.randint(keys[3], (GROUPS, UTT), 0, NSTEP), jax.random.fold_in(keys[3], 1), 0, NSTEP - 1).astype(jnp.int32),
        "lengths": draw_lengths(jax.random.fold_in(keys[16], 71), 0),
        "span_start": draw_span_start(jax.random.fold_in(keys[16], 71), 0),
        "span_len": draw_span_len(jax.random.fold_in(keys[16], 71), 0),
        "skip_proj": noise(keys[7], (2 * D, D), (2 * D) ** -0.5, 0.125, ((0, 32),)),
        "mod_proj": noise(keys[8], (D, 4 * D), D ** -0.5, 0.1875, ((0, 32),)),
        "mod_bias": noise(keys[9], (4 * D,), 0.3, 1.796875, ((0, 32),)),
        "qkv_proj": noise(keys[10], (D, 3 * D), D ** -0.5, 0.1875, ((0, 32),)),
        "out_proj": noise(keys[11], (D, D), (D // 16) ** -0.5, 0.75, ((0, 32),)),
        "up_proj": noise(keys[12], (D, FF), D ** -0.5, 0.1875, ((0, 32),)),
        "up_bias": noise(keys[13], (FF,), 0.5, 3.0, ((0, 32),)),
        "down_proj": noise(keys[14], (FF, D), FF ** -0.5, 0.09375, ((0, 32),)),
        "cotangent": noise(keys[15], (GROUPS, FRAMES, D), 1.0, 6.0, ((0, 4), (1, 8))),
    }


highest = lax.Precision.HIGHEST
norm_eps = 1e-06

@jax.custom_vjp
def low(v):
    return lax.optimization_barrier(v.astype(jnp.bfloat16)).astype(jnp.float32)

@jax.custom_vjp
def low_back(v):
    return v

def low_keep(v):
    return (low(v), None)

def low_pass(kept, grad):
    return (grad,)

def back_keep(v):
    return (v, None)

def back_low(kept, grad):
    return (low(grad),)
low.defvjp(low_keep, low_pass)
low_back.defvjp(back_keep, back_low)

def matmul(first_op, second_op):
    return jnp.dot(first_op, second_op, precision=highest)

def frame_plan(utt_lengths, span_begins, span_sizes, frame_ids):
    utt_ends = jnp.cumsum(utt_lengths).astype(jnp.int32)
    starts = (utt_ends - utt_lengths).astype(jnp.int32)
    member = (frame_ids[:, None] >= starts[None, :]) & (frame_ids[:, None] < utt_ends[None, :])
    member_int = member.astype(jnp.int32)
    slot_ids = jnp.arange(utt_lengths.shape[0], dtype=jnp.int32)
    utterance = lax.optimization_barrier(jnp.sum(member_int * slot_ids[None, :], axis=1)).astype(jnp.int32)
    utt_begin = lax.optimization_barrier(jnp.sum(member_int * starts[None, :], axis=1)).astype(jnp.int32)
    position = (frame_ids - utt_begin).astype(jnp.int32)
    span_first = lax.optimization_barrier(jnp.sum(member_int * span_begins[None, :], axis=1)).astype(jnp.int32)
    span_after = (span_first + lax.optimization_barrier(jnp.sum(member_int * span_sizes[None, :], axis=1))).astype(jnp.int32)
    in_span = (position >= span_first) & (position < span_after)
    return (member, utterance, position, in_span)

def layer_norm(hidden):
    centred = hidden - lax.optimization_barrier(jnp.mean(hidden, axis=-1, keepdims=True))
    return centred * lax.rsqrt(lax.optimization_barrier(jnp.mean(centred * centred, axis=-1, keepdims=True)) + norm_eps)

def rotary(values, position):
    half_size = values.shape[-1] // 2
    freq_rates = jnp.exp(jnp.arange(half_size, dtype=jnp.float32) * (-math.log(10000.0) / half_size))
    angles = position.astype(jnp.float32)[:, None] * freq_rates[None, :]
    cosine = jnp.cos(angles)[:, None, :]
    sine_part = jnp.sin(angles)[:, None, :]
    first_half = values[..., :half_size]
    second_half = values[..., half_size:]
    return jnp.concatenate([first_half * cosine - second_half * sine_part, second_half * cosine + first_half * sine_part], axis=-1)

def head_attend(query_head, key_head, value_head, same_utt):
    scores = low_back(matmul(query_head, key_head.T))
    scores = jnp.where(same_utt, scores, -1e+30)
    row_max = lax.optimization_barrier(jnp.max(scores, axis=-1, keepdims=True))
    weights = jnp.exp(scores - row_max)
    row_probs = weights / lax.optimization_barrier(jnp.sum(weights, axis=-1, keepdims=True))
    return matmul(low(row_probs), value_head)

def layer(frames_here, skip_here, params, member_rows, step_pick, utterance, position):
    skip_proj, mod_proj, mod_bias, qkv_proj, out_proj, up_proj, up_bias, down_proj, time_table = params
    frames = frames_here.shape[0]
    model_width = frames_here.shape[1]
    head_depth = model_width // HEADS
    time_rows = matmul(step_pick, time_table)
    time_vec = low(jax.nn.silu(time_rows))
    modulation = matmul(time_vec, mod_proj) + mod_bias
    per_frame = matmul(member_rows, modulation)
    scale_one = per_frame[:, :model_width]
    shift_one = per_frame[:, model_width:2 * model_width]
    scale_two = per_frame[:, 2 * model_width:3 * model_width]
    shift_two = per_frame[:, 3 * model_width:]
    stream_in = low_back(matmul(jnp.concatenate([frames_here, skip_here], axis=1), skip_proj))
    normed_one = low(layer_norm(stream_in) * (1.0 + scale_one) + shift_one)
    projected = low_back(matmul(normed_one, qkv_proj)).reshape(frames, 3, HEADS, head_depth)
    query = low(rotary(projected[:, 0], position) * head_depth ** (-0.5))
    key = low(rotary(projected[:, 1], position))
    value = low(projected[:, 2])
    same_utt = utterance[:, None] == utterance[None, :]

    def one_head(operands):
        return head_attend(operands[0], operands[1], operands[2], same_utt)
    heads_out = lax.map(jax.checkpoint(one_head), (query.transpose(1, 0, 2), key.transpose(1, 0, 2), value.transpose(1, 0, 2)))
    attended = low(low_back(heads_out)).transpose(1, 0, 2).reshape(frames, model_width)
    stream_mid = stream_in + low_back(matmul(attended, out_proj))
    normed_two = low(layer_norm(stream_mid) * (1.0 + scale_two) + shift_two)
    pre_act = low_back(matmul(normed_two, up_proj) + up_bias)
    activated = low(jax.nn.gelu(pre_act, approximate=True))
    return stream_mid + low_back(matmul(activated, down_proj))

def add_pair(first_op, second_op):
    return first_op + second_op

def reference(frames_in, skip_in, time_table, timestep, lengths, span_start, span_len, skip_proj, mod_proj, mod_bias, qkv_proj, out_proj, up_proj, up_bias, down_proj, cotangent):
    params = tuple((weight.astype(jnp.float32) for weight in (skip_proj, mod_proj, mod_bias, qkv_proj, out_proj, up_proj, up_bias, down_proj, time_table)))
    frame_ids = jnp.arange(FRAMES, dtype=jnp.int32)
    step_range = jnp.arange(NSTEP, dtype=jnp.int32)

    def group_step(running, operands):
        frames_group, skip_group, cot_group, step_group, utt_lengths, span_begins, span_sizes = operands
        member, utterance, position, in_span = frame_plan(utt_lengths, span_begins, span_sizes, frame_ids)
        member_rows = member.astype(jnp.float32)
        step_pick = (step_group[:, None] == step_range[None, :]).astype(jnp.float32)

        def forward(frames_here, skip_here, weights):
            return layer(frames_here, skip_here, weights, member_rows, step_pick, utterance, position)
        layer_out, pullback = jax.vjp(forward, frames_group.astype(jnp.float32), skip_group.astype(jnp.float32), params)
        masked_cot = cot_group.astype(jnp.float32) * in_span[:, None].astype(jnp.float32)
        grad_here, grad_skip_here, grad_params = pullback(masked_cot)
        running = jax.tree.map(add_pair, running, grad_params)
        return (running, (layer_out.astype(jnp.bfloat16), grad_here.astype(jnp.bfloat16), grad_skip_here.astype(jnp.bfloat16)))
    zero_grads = jax.tree.map(jnp.zeros_like, params)
    running, results = lax.scan(group_step, zero_grads, (frames_in, skip_in, cotangent, timestep, lengths, span_start, span_len))
    block_out, grad_frames, grad_skip = results
    grad_skip_proj, grad_mod_proj, grad_mod_bias, grad_qkv_proj, grad_out_proj, grad_up_proj, grad_up_bias, grad_down_proj, grad_time = running
    return (block_out, grad_frames, grad_skip, grad_time, grad_skip_proj, grad_mod_proj, grad_mod_bias, grad_qkv_proj, grad_out_proj, grad_up_proj, grad_up_bias, grad_down_proj)
```

```python
import functools
import math

import jax
import jax.numpy as jnp
from jax import lax
from jax.experimental import pallas as pl
from jax.experimental.pallas import tpu as pltpu
from jax.sharding import PartitionSpec as P

HEADS = 16
HD = 64
LANES = 128
MASKED = -(2.0 ** 100)
NORM_EPS = 1e-06
BOTH = ("seq", "batch")
NT = (((1,), (1,)), ((), ()))
NN = (((1,), (0,)), ((), ()))
TN = (((0,), (0,)), ((), ()))
highest = lax.Precision.HIGHEST


def mm(a, b, dims):
    return lax.dot_general(a, b, dims, preferred_element_type=jnp.float32)


def utt_of(ends_ref, rows, utts):
    found = jnp.zeros_like(rows)
    for u in range(utts - 1):
        found = found + (rows >= ends_ref[u]).astype(jnp.int32)
    return found


def key_range(ends_ref, first, last, utts, frames):
    low = 0
    high = frames
    for u in range(utts - 1):
        low = jnp.where(first >= ends_ref[u], ends_ref[u], low)
    for u in reversed(range(utts - 1)):
        high = jnp.where(last < ends_ref[u], ends_ref[u], high)
    return low, high


def split3(x):
    a = x.astype(jnp.bfloat16).astype(jnp.float32)
    b = (x - a).astype(jnp.bfloat16).astype(jnp.float32)
    return a, b, x - a - b


def fwd_kernel(ends_ref, qkv_ref, out_ref, lse_ref, q_s, k_s, v_s, m_s, acc_s, *, heads, utts, bq, bk):
    sources, _, rows, _ = qkv_ref.shape
    frames = sources * rows

    def build(src, carry):
        at = pl.multiple_of(src * rows, rows)
        lane = lax.broadcasted_iota(jnp.int32, (rows, LANES), 1)
        row = lax.broadcasted_iota(jnp.int32, (rows, LANES), 0) + at
        utt = utt_of(ends_ref, row, utts)
        for h in range(heads):
            spare = (1 - h) * HD
            mine = (lane >= HD) if h else (lane < HD)
            slot = lane - spare
            is_slot = (slot >= 0) & (slot < utts)
            qf = jnp.where(is_slot & (slot != utt), MASKED, 0.0)
            kf = jnp.where(slot == utt, 1.0, 0.0)
            vf = jnp.where(slot == 0, 1.0, 0.0)
            for part, feat, dst in ((0, qf, q_s), (1, kf, k_s), (2, vf, v_s)):
                x = qkv_ref[src, part].astype(jnp.float32)
                dst[h, pl.ds(at, rows), :] = jnp.where(mine, x, feat).astype(jnp.bfloat16)
        return carry

    lax.fori_loop(0, sources, build, 0)

    def q_block(i, carry):
        at = pl.multiple_of(i * bq, bq)
        low, high = key_range(ends_ref, at, at + bq - 1, utts, frames)
        m_s[...] = jnp.full(m_s.shape, -3.0e38, jnp.float32)
        acc_s[...] = jnp.zeros(acc_s.shape, jnp.float32)

        def k_block(j, inner):
            kat = pl.multiple_of(j * bk, bk)
            for h in range(heads):
                s = mm(q_s[h, pl.ds(at, bq), :], k_s[h, pl.ds(kat, bk), :], NT)
                old = m_s[h]
                top = jnp.maximum(old, jnp.max(s, axis=1, keepdims=True))
                alpha = jnp.exp(old - top)
                p = jnp.exp(s - top[:, :1]).astype(jnp.bfloat16)
                acc_s[h] = acc_s[h] * alpha + mm(p, v_s[h, pl.ds(kat, bk), :], NN)
                m_s[h] = top
            return inner

        lax.fori_loop(low // bk, (high + bk - 1) // bk, k_block, 0)
        lane = lax.broadcasted_iota(jnp.int32, (bq, LANES), 1)
        out = None
        lse = None
        for h in range(heads):
            spare = (1 - h) * HD
            acc = acc_s[h]
            total = acc[:, spare : spare + 1]
            o = acc / total
            l = m_s[h] + jnp.log(total)
            out = o if out is None else jnp.where(lane < HD, out, o)
            lse = l if lse is None else jnp.where(lane < HD, lse, l)
        out_ref[pl.ds(at, bq), :] = out.astype(jnp.bfloat16)
        lse_ref[pl.ds(at, bq), :] = lse
        return carry

    lax.fori_loop(0, frames // bq, q_block, 0)


def attend(qkv, ends, heads, bq, bk):
    sources, _, rows, _ = qkv.shape
    frames = sources * rows
    utts = ends.shape[0]
    return pl.pallas_call(
        functools.partial(fwd_kernel, heads=heads, utts=utts, bq=bq, bk=bk),
        out_shape=(
            jax.ShapeDtypeStruct((frames, LANES), jnp.bfloat16),
            jax.ShapeDtypeStruct((frames, LANES), jnp.float32),
        ),
        in_specs=[pl.BlockSpec(memory_space=pltpu.SMEM), pl.BlockSpec(memory_space=pltpu.VMEM)],
        out_specs=(pl.BlockSpec(memory_space=pltpu.VMEM), pl.BlockSpec(memory_space=pltpu.VMEM)),
        scratch_shapes=[pltpu.VMEM((heads, frames, LANES), jnp.bfloat16)] * 3
        + [pltpu.VMEM((heads, bq, LANES), jnp.float32)] * 2,
        compiler_params=pltpu.CompilerParams(vmem_limit_bytes=56 * 1024 * 1024),
        cost_estimate=pl.CostEstimate(
            flops=40 * heads * frames * frames * HD, bytes_accessed=frames * LANES * 12,
            transcendentals=heads * frames * frames,
        ),
        name="attend",
    )(ends, qkv)


def bwd_kernel(ends_ref, qkv_ref, da_ref, out_ref, lse_ref, cos_ref, sin_ref, grad_ref,
               q_s, k_s, v_s, d_s, gq_s, gk_s, gv_s, *, heads, utts, bq, bk):
    sources, _, rows, _ = qkv_ref.shape
    frames = sources * rows

    def build(src, carry):
        at = pl.multiple_of(src * rows, rows)
        lane = lax.broadcasted_iota(jnp.int32, (rows, LANES), 1)
        row = lax.broadcasted_iota(jnp.int32, (rows, LANES), 0) + at
        utt = utt_of(ends_ref, row, utts)
        da = da_ref[pl.ds(at, rows), :].astype(jnp.float32)
        prod = da * out_ref[pl.ds(at, rows), :].astype(jnp.float32)
        lse = lse_ref[pl.ds(at, rows), :]
        for h in range(heads):
            spare = (1 - h) * HD
            mine = (lane >= HD) if h else (lane < HD)
            slot = lane - spare
            is_slot = (slot >= 0) & (slot < utts)
            delta = jnp.sum(jnp.where(mine, prod, 0.0), axis=1, keepdims=True)
            l3 = split3(-lse[:, h * HD : h * HD + 1])
            d3 = split3(-delta)
            qf = jnp.where(is_slot & (slot != utt), MASKED, 0.0)
            df = jnp.zeros_like(qf)
            for n in range(3):
                qf = jnp.where(slot == utts + n, l3[n], qf)
                df = jnp.where(slot == n, d3[n], df)
            kf = jnp.where((slot == utt) | ((slot >= utts) & (slot < utts + 3)), 1.0, 0.0)
            vf = jnp.where((slot >= 0) & (slot < 3), 1.0, 0.0)
            for x, feat, dst in (
                (qkv_ref[src, 0], qf, q_s), (qkv_ref[src, 1], kf, k_s), (qkv_ref[src, 2], vf, v_s),
            ):
                dst[h, pl.ds(at, rows), :] = jnp.where(mine, x.astype(jnp.float32), feat).astype(jnp.bfloat16)
            d_s[h, pl.ds(at, rows), :] = jnp.where(mine, da, df).astype(jnp.bfloat16)
        gq_s[:, pl.ds(at, rows), :] = jnp.zeros((heads, rows, LANES), jnp.float32)
        return carry

    lax.fori_loop(0, sources, build, 0)

    def k_block(j, carry):
        kat = pl.multiple_of(j * bk, bk)
        low, high = key_range(ends_ref, kat, kat + bk - 1, utts, frames)
        gk_s[:, pl.ds(kat, bk), :] = jnp.zeros((heads, bk, LANES), jnp.float32)
        gv_s[:, pl.ds(kat, bk), :] = jnp.zeros((heads, bk, LANES), jnp.float32)

        def q_block(i, inner):
            at = pl.multiple_of(i * bq, bq)
            for h in range(heads):
                q = q_s[h, pl.ds(at, bq), :]
                d = d_s[h, pl.ds(at, bq), :]
                k = k_s[h, pl.ds(kat, bk), :]
                p = jnp.exp(mm(k, q, NT))
                ds = (p * mm(v_s[h, pl.ds(kat, bk), :], d, NT)).astype(jnp.bfloat16)
                gv_s[h, pl.ds(kat, bk), :] += mm(p.astype(jnp.bfloat16), d, NN)
                gk_s[h, pl.ds(kat, bk), :] += mm(ds, q, NN)
                gq_s[h, pl.ds(at, bq), :] += mm(ds, k, TN)
            return inner

        lax.fori_loop(low // bq, (high + bq - 1) // bq, q_block, 0)
        return carry

    lax.fori_loop(0, frames // bk, k_block, 0)

    def finish(src, carry):
        at = pl.multiple_of(src * rows, rows)
        lane = lax.broadcasted_iota(jnp.int32, (rows, LANES), 1)
        first = (lane % HD) < HD // 2
        cos = cos_ref[pl.ds(at, rows), :]
        sin = sin_ref[pl.ds(at, rows), :]

        def both(ref):
            x = ref[0, pl.ds(at, rows), :]
            return jnp.where(lane < HD, x, ref[1, pl.ds(at, rows), :]) if heads == 2 else x

        def unturn(x):
            partner = jnp.where(first, pltpu.roll(x, LANES - HD // 2, 1), pltpu.roll(x, HD // 2, 1))
            return x * cos - partner * sin

        grad_ref[src, 0] = (unturn(both(gq_s)) * HD ** -0.5).astype(jnp.bfloat16)
        grad_ref[src, 1] = unturn(both(gk_s)).astype(jnp.bfloat16)
        grad_ref[src, 2] = both(gv_s).astype(jnp.bfloat16)
        return carry

    lax.fori_loop(0, sources, finish, 0)


def attend_back(qkv, grad_out, out, lse, cos, sin, ends, heads, bq, bk):
    sources, _, rows, _ = qkv.shape
    frames = sources * rows
    utts = ends.shape[0]
    vmem = pl.BlockSpec(memory_space=pltpu.VMEM)
    return pl.pallas_call(
        functools.partial(bwd_kernel, heads=heads, utts=utts, bq=bq, bk=bk),
        out_shape=jax.ShapeDtypeStruct(qkv.shape, jnp.bfloat16),
        in_specs=[pl.BlockSpec(memory_space=pltpu.SMEM)] + [vmem] * 6,
        out_specs=vmem,
        scratch_shapes=[pltpu.VMEM((heads, frames, LANES), jnp.bfloat16)] * 4
        + [pltpu.VMEM((heads, frames, LANES), jnp.float32)] * 3,
        compiler_params=pltpu.CompilerParams(vmem_limit_bytes=60 * 1024 * 1024),
        cost_estimate=pl.CostEstimate(
            flops=64 * heads * frames * frames * HD, bytes_accessed=frames * LANES * 24,
            transcendentals=heads * frames * frames,
        ),
        name="attend_back",
    )(ends, qkv, grad_out, out, lse, cos, sin)


def project_kernel(normed_ref, weight_ref, cos_ref, sin_ref, out_ref):
    part = pl.program_id(0)
    weight = weight_ref[...].reshape(-1, weight_ref.shape[-1])
    turned = mm(normed_ref[...], weight, NN)
    lane = lax.broadcasted_iota(jnp.int32, (turned.shape[0], LANES), 1)
    first = (lane % HD) < HD // 2
    scale = jnp.where(part == 0, HD ** -0.5, 1.0)
    for at in range(out_ref.shape[0]):
        x = turned[:, at * LANES : (at + 1) * LANES]
        partner = jnp.where(first, pltpu.roll(x, LANES - HD // 2, 1), pltpu.roll(x, HD // 2, 1))
        rotated = (x * cos_ref[...] + partner * sin_ref[...]) * scale
        out_ref[at, 0] = jnp.where(part == 2, x, rotated).astype(jnp.bfloat16)


def project(normed, gathered, first_row, rows_each, cos, sin):
    rows, width = normed.shape
    devices = gathered.shape[0]
    targets = width // LANES
    each = 2
    at = first_row // rows_each
    return pl.pallas_call(
        project_kernel,
        grid=(3, targets // each),
        out_shape=jax.ShapeDtypeStruct((targets, 3, rows, LANES), jnp.bfloat16),
        in_specs=[
            pl.BlockSpec((rows, width), lambda p, t: (0, 0)),
            pl.BlockSpec((devices, rows_each, each * LANES), lambda p, t: (0, at + p, t)),
            pl.BlockSpec((rows, LANES), lambda p, t: (0, 0)),
            pl.BlockSpec((rows, LANES), lambda p, t: (0, 0)),
        ],
        out_specs=pl.BlockSpec((each, 1, rows, LANES), lambda p, t: (t, p, 0, 0)),
        compiler_params=pltpu.CompilerParams(vmem_limit_bytes=40 * 1024 * 1024),
        cost_estimate=pl.CostEstimate(
            flops=6 * rows * width * width, bytes_accessed=8 * width * width, transcendentals=0
        ),
        name="project",
    )(normed, gathered, cos, sin)


def rows_of(first_op, second_op):
    return lax.dot_general(first_op, second_op, TN, preferred_element_type=jnp.float32)


def times(first_op, second_op):
    return lax.dot_general(first_op, second_op, NN, preferred_element_type=jnp.float32)


def times_transpose(first_op, second_op):
    return lax.dot_general(first_op, second_op, NT, preferred_element_type=jnp.float32)


def swap(value, bit):
    size = lax.axis_size("seq")
    return lax.ppermute(value, "seq", [(i, i ^ bit) for i in range(size)])


def ahead(value, step):
    size = lax.axis_size("batch")
    return lax.ppermute(value, "batch", [(i, (i + step) % size) for i in range(size)])


def column_blocks(value, starts, width):
    return jnp.concatenate(
        [lax.dynamic_slice_in_dim(value, s, width, axis=1) for s in starts], axis=1
    )


def scatter_sum(first_op, second_op, bits):
    seq = lax.axis_size("seq")
    batch = lax.axis_size("batch")
    me = lax.axis_index("seq")
    rows_total = first_op.shape[1]
    block = rows_total // seq
    core = me & 1

    def starts(keep_of):
        return [(2 * i + keep_of(i)) * block for i in range(seq // 2)]

    other = swap(column_blocks(first_op, starts(lambda i: 1 - core), block), 1)
    second_other = swap(second_op, 1)
    mine = column_blocks(first_op, starts(lambda i: core), block)
    left = jnp.concatenate([mine, other], axis=0)
    right = jnp.concatenate([second_op, second_other], axis=0)
    high_bits = [seq >> (i + 1) for i in range(seq.bit_length() - 2)]
    bit = bits[0]
    shift = bit.bit_length() - 1
    value = (me >> shift) & 1
    chosen = [i for i in range(seq // 2) if not (2 * i) & bit]
    keep_at = [(i + value * (bit // 2)) * block for i in chosen]
    send_at = [(i + (1 - value) * (bit // 2)) * block for i in chosen]
    sent = rows_of(column_blocks(left, send_at, block), right).astype(jnp.bfloat16)
    came = swap(sent, bit)
    total = rows_of(column_blocks(left, keep_at, block), right) + came.astype(jnp.float32)
    left_bits = [b for b in high_bits if b != bit]
    total = total.astype(jnp.bfloat16).reshape(
        (2,) * len(left_bits) + (batch, block // batch, second_op.shape[1])
    )
    for bit in bits[1:]:
        axis = left_bits.index(bit)
        value = (me >> (bit.bit_length() - 1)) & 1
        came = swap(lax.dynamic_index_in_dim(total, 1 - value, axis, keepdims=False), bit)
        kept = lax.dynamic_index_in_dim(total, value, axis, keepdims=False)
        total = (kept.astype(jnp.float32) + came.astype(jnp.float32)).astype(jnp.bfloat16)
        left_bits.remove(bit)
    place = lax.axis_index("batch")
    result = lax.dynamic_index_in_dim(total, place, 0, keepdims=False).astype(jnp.float32)
    for step in range(1, batch):
        piece = lax.dynamic_index_in_dim(total, (place + step) % batch, 0, keepdims=False)
        result = result + ahead(piece, step).astype(jnp.float32)
    return result


def normalise(hidden):
    centred = hidden - jnp.mean(hidden, axis=-1, keepdims=True)
    inverse = lax.rsqrt(jnp.mean(centred * centred, axis=-1, keepdims=True) + NORM_EPS)
    return centred * inverse, inverse


def normalise_back(grad, normed, inverse):
    return inverse * (
        grad
        - jnp.mean(grad, axis=-1, keepdims=True)
        - normed * jnp.mean(grad * normed, axis=-1, keepdims=True)
    )


def per_row(member, table):
    total = member[:, 0:1] * table[0:1]
    for u in range(1, table.shape[0]):
        total = total + member[:, u : u + 1] * table[u : u + 1]
    return total


def gelu_parts(x):
    rate = math.sqrt(2.0 / math.pi)
    inner = jnp.tanh(rate * (x + 0.044715 * x * x * x))
    value = 0.5 * x * (1.0 + inner)
    slope = 0.5 * (1.0 + inner) + 0.5 * x * (1.0 - inner * inner) * rate * (
        1.0 + 3 * 0.044715 * x * x
    )
    return value, slope


def turn_tables(position):
    half = HD // 2
    lane = jnp.arange(LANES, dtype=jnp.int32)
    rates = jnp.exp((lane % half).astype(jnp.float32) * (-math.log(10000.0) / half))
    angles = position.astype(jnp.float32)[:, None] * rates[None, :]
    side = jnp.where((lane % HD) < half, -1.0, 1.0).astype(jnp.float32)
    return jnp.cos(angles), jnp.sin(angles) * side[None, :]


def all_pieces(value):
    batch = lax.axis_size("batch")
    place = lax.axis_index("batch")
    out = jnp.zeros((batch,) + value.shape, value.dtype)
    out = lax.dynamic_update_index_in_dim(out, value, place, 0)
    for step in range(1, batch):
        out = lax.dynamic_update_index_in_dim(
            out, ahead(value, step), (place - step) % batch, 0
        )
    return out


def seq_total(value):
    bit = 1
    while bit < lax.axis_size("seq"):
        value = value + swap(value, bit)
        bit *= 2
    return value


def shards(
    frames_in,
    skip_in,
    time_table,
    timestep,
    lengths,
    span_start,
    span_len,
    skip_proj,
    mod_proj,
    mod_bias,
    qkv_proj,
    out_proj,
    up_proj,
    up_bias,
    down_proj,
    cotangent,
):
    seq = lax.axis_size("seq")
    batch = lax.axis_size("batch")
    seq_at = lax.axis_index("seq")
    batch_at = lax.axis_index("batch")
    device = seq_at * batch + batch_at
    devices = seq * batch
    inputs = frames_in[0]
    skip_rows = skip_in[0]
    rows, width = inputs.shape
    hidden = up_proj.shape[1]
    frames = rows * seq
    heads = HEADS // seq
    utts = lengths.shape[1]

    early = jnp.concatenate(
        [skip_proj] + [qkv_proj[:, p * width : (p + 1) * width] for p in range(3)], axis=0
    )
    late = jnp.concatenate(
        [down_proj, out_proj]
        + [up_proj[:, p * width : (p + 1) * width] for p in range(hidden // width)],
        axis=0,
    )
    early = lax.all_gather(early, BOTH, axis=0, tiled=False)
    late = lax.all_gather(late, BOTH, axis=0, tiled=False)
    skip_each, qkv_each, out_each, up_each, down_each = (
        skip_proj.shape[0],
        qkv_proj.shape[0],
        out_proj.shape[0],
        up_proj.shape[0],
        down_proj.shape[0],
    )
    full_skip = early[:, :skip_each].reshape(2 * width, width)
    full_qkv = [
        early[:, skip_each + p * qkv_each : skip_each + (p + 1) * qkv_each].reshape(width, width)
        for p in range(3)
    ]
    full_down = late[:, :down_each].reshape(hidden, width)
    full_out = late[:, down_each : down_each + out_each].reshape(width, width)
    full_up = (
        late[:, down_each + out_each :]
        .reshape(devices, hidden // width, up_each, width)
        .transpose(0, 2, 1, 3)
        .reshape(width, hidden)
    )

    utt_lengths = lengths[0]
    ends = jnp.cumsum(utt_lengths).astype(jnp.int32)
    starts = ends - utt_lengths
    frame_ids = seq_at * rows + jnp.arange(rows, dtype=jnp.int32)
    group_ids = jnp.arange(frames, dtype=jnp.int32)

    def members(ids):
        return (ids[:, None] >= starts[None, :]) & (ids[:, None] < ends[None, :])

    member = members(frame_ids)
    member_int = member.astype(jnp.int32)
    position = frame_ids - jnp.sum(member_int * starts[None, :], axis=1)
    span_first = jnp.sum(member_int * span_start[0][None, :], axis=1)
    span_after = span_first + jnp.sum(member_int * span_len[0][None, :], axis=1)
    in_span = ((position >= span_first) & (position < span_after)).astype(jnp.float32)
    member_rows = member.astype(jnp.float32)
    group_position = group_ids - jnp.sum(members(group_ids).astype(jnp.int32) * starts[None, :], axis=1)
    cos, sin = turn_tables(position)
    group_cos, group_sin = turn_tables(group_position)

    steps = all_pieces(timestep[0]).reshape(-1)
    step_pick = (
        steps[:, None] == jnp.arange(time_table.shape[0], dtype=jnp.int32)[None, :]
    ).astype(jnp.float32)
    time_rows = jnp.dot(step_pick, time_table.astype(jnp.float32), precision=highest)
    silu_value, silu_pull = jax.vjp(jax.nn.silu, time_rows)
    time_vec = silu_value.astype(jnp.bfloat16)
    terms = times(time_vec, mod_proj)
    bias_terms = lax.dynamic_update_slice(
        jnp.zeros((4 * width,), jnp.float32),
        mod_bias.astype(jnp.float32),
        (device * mod_bias.shape[0],),
    )
    terms = (terms + bias_terms[None, :]).reshape(batch, utts, 4 * width)
    modulation = lax.dynamic_index_in_dim(terms, batch_at, 0, keepdims=False)
    for step in range(1, batch):
        modulation = modulation + ahead(
            lax.dynamic_index_in_dim(terms, (batch_at + step) % batch, 0, keepdims=False), step
        )
    modulation = seq_total(modulation)
    scale_one = per_row(member_rows, 1.0 + modulation[:, :width])
    shift_one = per_row(member_rows, modulation[:, width : 2 * width])
    scale_two = per_row(member_rows, 1.0 + modulation[:, 2 * width : 3 * width])
    shift_two = per_row(member_rows, modulation[:, 3 * width :])
    full_bup = all_gather_bias(up_bias)

    joined = jnp.concatenate([inputs, skip_rows], axis=1)
    stream_in = times(joined, full_skip)
    unit_one, inverse_one = normalise(stream_in)
    normed_one = (unit_one * scale_one + shift_one).astype(jnp.bfloat16)
    sent = project(normed_one, early, skip_each, qkv_each, cos, sin)
    per_device = width // seq
    if per_device < LANES:
        sent = sent.reshape(-1, 3, rows, 2, per_device).transpose(0, 3, 1, 2, 4)
        sent = sent.reshape(seq, 3, rows, per_device)
        sent = jnp.pad(sent, ((0, 0), (0, 0), (0, 0), (0, LANES - per_device)))
    held = lax.all_to_all(sent, "seq", 0, 0, tiled=True)
    head_out, log_sums = attend(held, ends, heads, 1024, 512)
    attended = lax.all_to_all(
        head_out.reshape(seq, rows, LANES)[:, :, :per_device], "seq", 0, 0, tiled=True
    )
    attended = attended.transpose(1, 0, 2).reshape(rows, width)
    stream_mid = stream_in + times(attended, full_out)
    unit_two, inverse_two = normalise(stream_mid)
    normed_two = (unit_two * scale_two + shift_two).astype(jnp.bfloat16)
    pre_act = times(normed_two, full_up) + full_bup[None, :]
    act_value, act_slope = gelu_parts(pre_act)
    activated = act_value.astype(jnp.bfloat16)
    result = (stream_mid + times(activated, full_down)).astype(jnp.bfloat16)

    grad_result = cotangent[0].astype(jnp.float32) * in_span[:, None]
    grad_branch = grad_result.astype(jnp.bfloat16)
    grad_pre = (times_transpose(grad_branch, full_down) * act_slope).astype(jnp.bfloat16)
    grad_normed = times_transpose(grad_pre, full_up)
    grad_mid = grad_result + normalise_back(grad_normed * scale_two, unit_two, inverse_two)
    grad_attn_out = grad_mid.astype(jnp.bfloat16)
    grad_attended = times_transpose(grad_attn_out, full_out).astype(jnp.bfloat16)
    high = [seq >> (i + 1) for i in range(seq.bit_length() - 2)]
    low = high[::-1]
    grad_down = scatter_sum(activated, grad_branch, low)
    grad_up = scatter_sum(normed_two, grad_pre, high)
    grad_out_w = scatter_sum(attended, grad_attn_out, high)
    mod_two = jnp.concatenate(
        [
            jnp.dot(member_rows.T, grad_normed * unit_two, precision=highest),
            jnp.dot(member_rows.T, grad_normed, precision=highest),
        ],
        axis=1,
    )

    back = grad_attended.reshape(rows, seq, per_device).transpose(1, 0, 2)
    if per_device < LANES:
        back = jnp.pad(back, ((0, 0), (0, 0), (0, LANES - per_device)))
    back = lax.all_to_all(back, "seq", 0, 0, tiled=True).reshape(frames, LANES)
    grad_held = attend_back(
        held, back, head_out, log_sums, group_cos, group_sin, ends, heads, 1024, 512
    )
    grad_projected = lax.all_to_all(grad_held[..., :per_device], "seq", 0, 0, tiled=True)
    grad_projected = grad_projected.transpose(2, 1, 0, 3).reshape(rows, 3 * width)
    grad_qkv_w = scatter_sum(normed_one, grad_projected, low)
    grad_normed_one = sum(
        times_transpose(grad_projected[:, p * width : (p + 1) * width], full_qkv[p])
        for p in range(3)
    )
    grad_stream = (
        grad_mid + normalise_back(grad_normed_one * scale_one, unit_one, inverse_one)
    ).astype(jnp.bfloat16)
    grad_skip_w = scatter_sum(joined, grad_stream, high)
    grad_joined = times_transpose(grad_stream, full_skip)
    grad_inputs = grad_joined[:, :width].astype(jnp.bfloat16)
    grad_skip_rows = grad_joined[:, width:].astype(jnp.bfloat16)

    mod_one = jnp.concatenate(
        [
            jnp.dot(member_rows.T, grad_normed_one * unit_one, precision=highest),
            jnp.dot(member_rows.T, grad_normed_one, precision=highest),
        ],
        axis=1,
    )
    grad_modulation = all_pieces(seq_total(jnp.concatenate([mod_one, mod_two], axis=1)))
    grad_modulation = grad_modulation.reshape(batch * utts, 4 * width)
    grad_bmod = lax.dynamic_slice_in_dim(
        jnp.sum(grad_modulation, axis=0), device * mod_bias.shape[0], mod_bias.shape[0]
    )
    grad_mod_w = jnp.dot(time_vec.astype(jnp.float32).T, grad_modulation, precision=highest)
    grad_time_vec = jnp.dot(grad_modulation, mod_proj.astype(jnp.float32).T, precision=highest)
    grad_table = jnp.dot(step_pick.T, silu_pull(grad_time_vec)[0], precision=highest)
    grad_bup = bias_total(jnp.sum(grad_pre.astype(jnp.float32), axis=0))
    return (
        result[None],
        grad_inputs[None],
        grad_skip_rows[None],
        grad_table,
        grad_skip_w,
        grad_mod_w,
        grad_bmod,
        grad_qkv_w,
        grad_out_w,
        grad_up,
        grad_bup,
        grad_down,
    )


def all_gather_bias(bias):
    seq = lax.axis_size("seq")
    pieces = all_pieces(bias.astype(jnp.float32)).reshape(1, -1)
    bit = 1
    out = jnp.zeros((seq, pieces.shape[1]), jnp.float32)
    out = lax.dynamic_update_slice(out, pieces, (lax.axis_index("seq"), 0))
    return seq_total(out).reshape(-1)


def bias_total(terms):
    batch = lax.axis_size("batch")
    place = lax.axis_index("batch")
    size = terms.shape[0] // (lax.axis_size("seq") * batch)
    terms = seq_total(terms.reshape(-1, size))
    total = lax.dynamic_slice_in_dim(terms, lax.axis_index("seq") * batch, batch, axis=0)
    result = lax.dynamic_index_in_dim(total, place, 0, keepdims=False)
    for step in range(1, batch):
        result = result + ahead(
            lax.dynamic_index_in_dim(total, (place + step) % batch, 0, keepdims=False), step
        )
    return result


def solution(mesh):
    return jax.shard_map(
        shards,
        mesh=mesh,
        in_specs=(
            P("batch", "seq", None),
            P("batch", "seq", None),
            P(None, BOTH),
            P("batch", None),
            P("batch", None),
            P("batch", None),
            P("batch", None),
            P(BOTH, None),
            P(BOTH, None),
            P(BOTH),
            P(BOTH, None),
            P(BOTH, None),
            P(BOTH, None),
            P(BOTH),
            P(BOTH, None),
            P("batch", "seq", None),
        ),
        out_specs=(
            P("batch", "seq", None),
            P("batch", "seq", None),
            P("batch", "seq", None),
            P(None, BOTH),
            P(BOTH, None),
            P(BOTH, None),
            P(BOTH),
            P(BOTH, None),
            P(BOTH, None),
            P(BOTH, None),
            P(BOTH),
            P(BOTH, None),
        ),
        check_vma=False,
    )
```

```python
import functools
import math

import jax
import jax.numpy as jnp
from jax import lax
from jax.experimental import pallas as pl
from jax.experimental.pallas import tpu as pltpu
from jax.sharding import PartitionSpec as P

HEADS = 16
HD = 64
LANES = 128
MASKED = -(2.0 ** 100)
NORM_EPS = 1e-06
VMEM = 60 * 1024 * 1024
BOTH = ("seq", "batch")
NT = (((1,), (1,)), ((), ()))
NN = (((1,), (0,)), ((), ()))
TN = (((0,), (0,)), ((), ()))
highest = lax.Precision.HIGHEST


def mm(a, b, dims):
    return lax.dot_general(a, b, dims, preferred_element_type=jnp.float32)


def utt_of(ends_ref, rows, utts):
    found = jnp.zeros_like(rows)
    for u in range(utts - 1):
        found = found + (rows >= ends_ref[u]).astype(jnp.int32)
    return found


def key_range(ends_ref, first, last, utts, frames):
    low = 0
    high = frames
    for u in range(utts - 1):
        low = jnp.where(first >= ends_ref[u], ends_ref[u], low)
    for u in reversed(range(utts - 1)):
        high = jnp.where(last < ends_ref[u], ends_ref[u], high)
    return low, high


def split3(x):
    a = x.astype(jnp.bfloat16).astype(jnp.float32)
    b = (x - a).astype(jnp.bfloat16).astype(jnp.float32)
    return a, b, x - a - b


def fwd_kernel(ends_ref, qkv_ref, out_ref, lse_ref, q_s, k_s, v_s, m_s, acc_s, *, heads, utts, bq, bk):
    sources, _, rows, _ = qkv_ref.shape
    frames = sources * rows

    def build(src, carry):
        at = pl.multiple_of(src * rows, rows)
        lane = lax.broadcasted_iota(jnp.int32, (rows, LANES), 1)
        row = lax.broadcasted_iota(jnp.int32, (rows, LANES), 0) + at
        utt = utt_of(ends_ref, row, utts)
        for h in range(heads):
            spare = (1 - h) * HD
            mine = (lane >= HD) if h else (lane < HD)
            slot = lane - spare
            is_slot = (slot >= 0) & (slot < utts)
            qf = jnp.where(is_slot & (slot != utt), MASKED, 0.0)
            kf = jnp.where(slot == utt, 1.0, 0.0)
            vf = jnp.where(slot == 0, 1.0, 0.0)
            for part, feat, dst in ((0, qf, q_s), (1, kf, k_s), (2, vf, v_s)):
                x = qkv_ref[src, part].astype(jnp.float32)
                dst[h, pl.ds(at, rows), :] = jnp.where(mine, x, feat).astype(jnp.bfloat16)
        return carry

    lax.fori_loop(0, sources, build, 0)

    def q_block(i, carry):
        at = pl.multiple_of(i * bq, bq)
        low, high = key_range(ends_ref, at, at + bq - 1, utts, frames)
        m_s[...] = jnp.full(m_s.shape, -3.0e38, jnp.float32)
        acc_s[...] = jnp.zeros(acc_s.shape, jnp.float32)

        def k_block(j, inner):
            kat = pl.multiple_of(j * bk, bk)
            for h in range(heads):
                s = mm(q_s[h, pl.ds(at, bq), :], k_s[h, pl.ds(kat, bk), :], NT)
                old = m_s[h]
                top = jnp.maximum(old, jnp.max(s, axis=1, keepdims=True))
                alpha = jnp.exp(old - top)
                p = jnp.exp(s - top[:, :1]).astype(jnp.bfloat16)
                acc_s[h] = acc_s[h] * alpha + mm(p, v_s[h, pl.ds(kat, bk), :], NN)
                m_s[h] = top
            return inner

        lax.fori_loop(low // bk, (high + bk - 1) // bk, k_block, 0)
        lane = lax.broadcasted_iota(jnp.int32, (bq, LANES), 1)
        out = None
        lse = None
        for h in range(heads):
            spare = (1 - h) * HD
            acc = acc_s[h]
            total = acc[:, spare : spare + 1]
            o = acc / total
            l = m_s[h] + jnp.log(total)
            out = o if out is None else jnp.where(lane < HD, out, o)
            lse = l if lse is None else jnp.where(lane < HD, lse, l)
        out_ref[pl.ds(at, bq), :] = out.astype(jnp.bfloat16)
        lse_ref[pl.ds(at, bq), :] = lse
        return carry

    lax.fori_loop(0, frames // bq, q_block, 0)


def attend(qkv, ends, heads, bq, bk):
    sources, _, rows, _ = qkv.shape
    frames = sources * rows
    utts = ends.shape[0]
    return pl.pallas_call(
        functools.partial(fwd_kernel, heads=heads, utts=utts, bq=bq, bk=bk),
        out_shape=(
            jax.ShapeDtypeStruct((frames, LANES), jnp.bfloat16),
            jax.ShapeDtypeStruct((frames, LANES), jnp.float32),
        ),
        in_specs=[pl.BlockSpec(memory_space=pltpu.SMEM), pl.BlockSpec(memory_space=pltpu.VMEM)],
        out_specs=(pl.BlockSpec(memory_space=pltpu.VMEM), pl.BlockSpec(memory_space=pltpu.VMEM)),
        scratch_shapes=[pltpu.VMEM((heads, frames, LANES), jnp.bfloat16)] * 3
        + [pltpu.VMEM((heads, bq, LANES), jnp.float32)] * 2,
        compiler_params=pltpu.CompilerParams(vmem_limit_bytes=VMEM),
        cost_estimate=pl.CostEstimate(
            flops=40 * heads * frames * frames * HD, bytes_accessed=frames * LANES * 12,
            transcendentals=heads * frames * frames,
        ),
        name="attend",
    )(ends, qkv)


def bwd_kernel(
    ends_ref, qkv_ref, da_ref, out_ref, lse_ref, cos_ref, sin_ref, *rest, heads, utts, bq, bk
):
    grad_ref, q_s, k_s, v_s, d_s, gq_s, gk_s, gv_s = rest[-8:]
    sources, _, rows, _ = qkv_ref.shape
    frames = sources * rows

    def build(src, carry):
        at = pl.multiple_of(src * rows, rows)
        lane = lax.broadcasted_iota(jnp.int32, (rows, LANES), 1)
        row = lax.broadcasted_iota(jnp.int32, (rows, LANES), 0) + at
        utt = utt_of(ends_ref, row, utts)
        da = da_ref[pl.ds(at, rows), :].astype(jnp.float32)
        prod = da * out_ref[pl.ds(at, rows), :].astype(jnp.float32)
        lse = lse_ref[pl.ds(at, rows), :]
        for h in range(heads):
            spare = (1 - h) * HD
            mine = (lane >= HD) if h else (lane < HD)
            slot = lane - spare
            is_slot = (slot >= 0) & (slot < utts)
            delta = jnp.sum(jnp.where(mine, prod, 0.0), axis=1, keepdims=True)
            l3 = split3(-lse[:, h * HD : h * HD + 1])
            d3 = split3(-delta)
            qf = jnp.where(is_slot & (slot != utt), MASKED, 0.0)
            df = jnp.zeros_like(qf)
            for n in range(3):
                qf = jnp.where(slot == utts + n, l3[n], qf)
                df = jnp.where(slot == n, d3[n], df)
            kf = jnp.where((slot == utt) | ((slot >= utts) & (slot < utts + 3)), 1.0, 0.0)
            vf = jnp.where((slot >= 0) & (slot < 3), 1.0, 0.0)
            for x, feat, dst in (
                (qkv_ref[src, 0], qf, q_s), (qkv_ref[src, 1], kf, k_s), (qkv_ref[src, 2], vf, v_s),
            ):
                dst[h, pl.ds(at, rows), :] = jnp.where(mine, x.astype(jnp.float32), feat).astype(jnp.bfloat16)
            d_s[h, pl.ds(at, rows), :] = jnp.where(mine, da, df).astype(jnp.bfloat16)
        gq_s[:, pl.ds(at, rows), :] = jnp.zeros((heads, rows, LANES), jnp.float32)
        return carry

    lax.fori_loop(0, sources, build, 0)

    def k_block(j, carry):
        kat = pl.multiple_of(j * bk, bk)
        low, high = key_range(ends_ref, kat, kat + bk - 1, utts, frames)
        gk_s[:, pl.ds(kat, bk), :] = jnp.zeros((heads, bk, LANES), jnp.float32)
        gv_s[:, pl.ds(kat, bk), :] = jnp.zeros((heads, bk, LANES), jnp.float32)

        def q_block(i, inner):
            at = pl.multiple_of(i * bq, bq)
            for h in range(heads):
                q = q_s[h, pl.ds(at, bq), :]
                d = d_s[h, pl.ds(at, bq), :]
                k = k_s[h, pl.ds(kat, bk), :]
                p = jnp.exp(mm(k, q, NT))
                ds = (p * mm(v_s[h, pl.ds(kat, bk), :], d, NT)).astype(jnp.bfloat16)
                gv_s[h, pl.ds(kat, bk), :] += mm(p.astype(jnp.bfloat16), d, NN)
                gk_s[h, pl.ds(kat, bk), :] += mm(ds, q, NN)
                gq_s[h, pl.ds(at, bq), :] += mm(ds, k, TN)
            return inner

        lax.fori_loop(low // bq, (high + bq - 1) // bq, q_block, 0)
        return carry

    lax.fori_loop(0, frames // bk, k_block, 0)

    def finish(src, carry):
        at = pl.multiple_of(src * rows, rows)
        lane = lax.broadcasted_iota(jnp.int32, (rows, LANES), 1)
        first = (lane % HD) < HD // 2
        cos = cos_ref[pl.ds(at, rows), :]
        sin = sin_ref[pl.ds(at, rows), :]

        def both(ref):
            x = ref[0, pl.ds(at, rows), :]
            return jnp.where(lane < HD, x, ref[1, pl.ds(at, rows), :]) if heads == 2 else x

        def unturn(x):
            partner = jnp.where(first, pltpu.roll(x, LANES - HD // 2, 1), pltpu.roll(x, HD // 2, 1))
            return x * cos - partner * sin

        grad_ref[src, 0] = (unturn(both(gq_s)) * HD ** -0.5).astype(jnp.bfloat16)
        grad_ref[src, 1] = unturn(both(gk_s)).astype(jnp.bfloat16)
        grad_ref[src, 2] = both(gv_s).astype(jnp.bfloat16)
        return carry

    lax.fori_loop(0, sources, finish, 0)


def attend_back(qkv, grad_out, out, lse, cos, sin, ends, heads, after, bq, bk):
    sources, _, rows, _ = qkv.shape
    frames = sources * rows
    utts = ends.shape[0]
    vmem = pl.BlockSpec(memory_space=pltpu.VMEM)
    return pl.pallas_call(
        functools.partial(bwd_kernel, heads=heads, utts=utts, bq=bq, bk=bk),
        out_shape=jax.ShapeDtypeStruct(qkv.shape, jnp.bfloat16),
        in_specs=[pl.BlockSpec(memory_space=pltpu.SMEM)]
        + [vmem] * 6
        + [pl.BlockSpec(memory_space=pl.ANY)] * len(after),
        out_specs=vmem,
        scratch_shapes=[pltpu.VMEM((heads, frames, LANES), jnp.bfloat16)] * 4
        + [pltpu.VMEM((heads, frames, LANES), jnp.float32)] * 3,
        compiler_params=pltpu.CompilerParams(vmem_limit_bytes=VMEM),
        cost_estimate=pl.CostEstimate(
            flops=64 * heads * frames * frames * HD, bytes_accessed=frames * LANES * 24,
            transcendentals=heads * frames * frames,
        ),
        name="attend_back",
    )(ends, qkv, grad_out, out, lse, cos, sin, *after)


def unjoin_kernel(grad_ref, weight_ref, *rest):
    width = grad_ref.shape[1]
    i = pl.program_id(0)
    made = mm(grad_ref[...], weight_ref[...].reshape(-1, width), NT).astype(jnp.bfloat16)

    @pl.when(i < 2)
    def _():
        rest[-2][...] = made

    @pl.when(i >= 2)
    def _():
        rest[-1][...] = made


def unjoin(grad, early, skip_each, after):
    rows, width = grad.shape
    devices = early.shape[0]
    half = width // 2
    return pl.pallas_call(
        unjoin_kernel,
        grid=(4,),
        out_shape=[jax.ShapeDtypeStruct((rows, width), jnp.bfloat16)] * 2,
        in_specs=[
            pl.BlockSpec((rows, width), lambda i: (0, 0)),
            pl.BlockSpec((devices // 4, skip_each, width), lambda i: (i, 0, 0)),
        ]
        + [pl.BlockSpec(memory_space=pl.ANY)] * len(after),
        out_specs=[
            pl.BlockSpec((rows, half), lambda i: (0, jnp.minimum(i, 1))),
            pl.BlockSpec((rows, half), lambda i: (0, jnp.maximum(i - 2, 0))),
        ],
        cost_estimate=pl.CostEstimate(
            flops=4 * rows * width * width, bytes_accessed=6 * width * width, transcendentals=0
        ),
        compiler_params=pltpu.CompilerParams(vmem_limit_bytes=VMEM),
        name="unjoin",
    )(grad, early, *after)


def normalise(hidden):
    centred = hidden - jnp.mean(hidden, axis=-1, keepdims=True)
    inverse = lax.rsqrt(jnp.mean(centred * centred, axis=-1, keepdims=True) + NORM_EPS)
    return centred * inverse, inverse


def normalise_back(grad, normed, inverse):
    return inverse * (
        grad
        - jnp.mean(grad, axis=-1, keepdims=True)
        - normed * jnp.mean(grad * normed, axis=-1, keepdims=True)
    )


def per_row(info, table, utts):
    total = info[:, 0:1] * table[0:1]
    for u in range(1, utts):
        total = total + info[:, u : u + 1] * table[u : u + 1]
    return total


def sums_by_utt(ref, at, info, value, utts):
    width = value.shape[1]
    for u in range(utts):
        ref[u : u + 1, at : at + width] = jnp.sum(info[:, u : u + 1] * value, axis=0, keepdims=True)


def gelu_parts(x):
    rate = math.sqrt(2.0 / math.pi)
    square = x * x
    inner = jnp.tanh(x * (rate + rate * 0.044715 * square))
    half = 0.5 + 0.5 * inner
    value = x * half
    slope = half + 0.5 * x * (1.0 - inner * inner) * (rate + 3 * rate * 0.044715 * square)
    return value, slope


def front_kernel(frames_ref, skip_ref, info_ref, mod_ref, wskip_ref, wqkv_ref, cos_ref, sin_ref,
                 *rest, utts, steps, parts):
    stream_ref, out_ref, flipped_ref, normed_ref = rest[-4:]
    i = pl.program_id(0)
    width = stream_ref.shape[1]
    weight = wskip_ref[...].reshape(-1, width)
    depth = weight.shape[0]

    for n in range(steps):
        @pl.when(i == n)
        def _(n=n):
            at = n * depth
            source = frames_ref if at < width else skip_ref
            at = at % width
            term = mm(source[:, at : at + depth], weight, NN)
            stream_ref[...] = term if n == 0 else stream_ref[...] + term

    @pl.when(i == steps - 1)
    def _():
        info = info_ref[...]
        unit, _unused = normalise(stream_ref[...])
        scale = per_row(info, 1.0 + mod_ref[:, :width], utts)
        shift = per_row(info, mod_ref[:, width : 2 * width], utts)
        normed = (unit * scale + shift).astype(jnp.bfloat16)
        normed_ref[...] = normed
        flipped_ref[...] = normed.T

    @pl.when(i >= steps)
    def _():
        part = (i - steps) // parts
        w = wqkv_ref[...].reshape(width, -1)
        turned = mm(normed_ref[...], w, NN)
        lane = lax.broadcasted_iota(jnp.int32, (turned.shape[0], LANES), 1)
        first = (lane % HD) < HD // 2
        scale = jnp.where(part == 0, HD ** -0.5, 1.0)
        for at in range(out_ref.shape[0]):
            x = turned[:, at * LANES : (at + 1) * LANES]
            partner = jnp.where(first, pltpu.roll(x, LANES - HD // 2, 1), pltpu.roll(x, HD // 2, 1))
            rotated = (x * cos_ref[...] + partner * sin_ref[...]) * scale
            out_ref[at, 0] = jnp.where(part == 2, x, rotated).astype(jnp.bfloat16)


def front(frames, skip, info, modulation, early, skip_each, qkv_each, cos, sin, utts, after):
    rows, width = frames.shape
    devices = early.shape[0]
    steps, parts = 4, 4
    targets = width // LANES
    each = targets // parts
    first = skip_each // qkv_each

    def fixed(*shape):
        return pl.BlockSpec(shape, lambda i: (0,) * len(shape))

    def later(i):
        return jnp.maximum(i - steps, 0)

    return pl.pallas_call(
        functools.partial(front_kernel, utts=utts, steps=steps, parts=parts),
        grid=(steps + 3 * parts,),
        out_shape=(
            jax.ShapeDtypeStruct((rows, width), jnp.float32),
            jax.ShapeDtypeStruct((targets, 3, rows, LANES), jnp.bfloat16),
            jax.ShapeDtypeStruct((width, rows), jnp.bfloat16),
        ),
        in_specs=[
            fixed(rows, width),
            fixed(rows, width),
            fixed(rows, LANES),
            fixed(utts, 4 * width),
            pl.BlockSpec((devices // steps, skip_each, width), lambda i: (jnp.minimum(i, steps - 1), 0, 0)),
            pl.BlockSpec(
                (devices, qkv_each, each * LANES),
                lambda i: (0, first + later(i) // parts, later(i) % parts),
            ),
            fixed(rows, LANES),
            fixed(rows, LANES),
        ]
        + [pl.BlockSpec(memory_space=pl.ANY)] * len(after),
        out_specs=(
            fixed(rows, width),
            pl.BlockSpec((each, 1, rows, LANES), lambda i: (later(i) % parts, later(i) // parts, 0, 0)),
            fixed(width, rows),
        ),
        scratch_shapes=[pltpu.VMEM((rows, width), jnp.bfloat16)],
        compiler_params=pltpu.CompilerParams(vmem_limit_bytes=VMEM),
        cost_estimate=pl.CostEstimate(
            flops=16 * rows * width * width, bytes_accessed=20 * width * width, transcendentals=0
        ),
        name="front",
    )(frames, skip, info, modulation, early, early, cos, sin, *after)


def middle_kernel(att_ref, stream_ref, info_ref, mod_ref, branch_ref, wout_ref, wup_ref, wdown_ref, bias_ref,
                  result_ref, attended_ref, normed_ref, act_ref, pre_ref, grad_ref, grad_low_ref,
                  back_ref, sums_ref, bup_ref,
                  mid_s, unit_s, inv_s, total_s, gn_s, att_s, normed_s, *, utts, blocks):
    b = pl.program_id(0)
    rows, width = stream_ref.shape
    groups = att_ref.shape[0]

    @pl.when(b == 0)
    def _():
        for s in range(groups):
            att_s[:, s * LANES : (s + 1) * LANES] = att_ref[s]
            attended_ref[s * LANES : (s + 1) * LANES, :] = att_ref[s].T
        mid = stream_ref[...] + mm(att_s[...], wout_ref[...].reshape(width, width), NN)
        mid_s[...] = mid
        unit, inverse = normalise(mid)
        unit_s[...] = unit
        inv_s[...] = jnp.broadcast_to(inverse, inv_s.shape)
        info = info_ref[...]
        scale = per_row(info, 1.0 + mod_ref[:, 2 * width : 3 * width], utts)
        shift = per_row(info, mod_ref[:, 3 * width :], utts)
        normed = (unit * scale + shift).astype(jnp.bfloat16)
        normed_s[...] = normed
        normed_ref[...] = normed.T

    up = wup_ref[...].reshape(width, -1)
    down = wdown_ref[...].reshape(-1, width)
    value, slope = gelu_parts(mm(normed_s[...], up, NN) + bias_ref[...])
    act = value.astype(jnp.bfloat16)
    act_ref[...] = act.T
    term = mm(act, down, NN)
    pre = (mm(branch_ref[...], down, NT) * slope).astype(jnp.bfloat16)
    pre_ref[...] = pre
    bup_ref[...] = jnp.sum(pre.astype(jnp.float32), axis=0, keepdims=True)
    grad_term = mm(pre, up, NT)

    @pl.when(b == 0)
    def _():
        total_s[...] = mid_s[...] + term
        gn_s[...] = grad_term

    @pl.when(b > 0)
    def _():
        total_s[...] += term
        gn_s[...] += grad_term

    @pl.when(b == blocks - 1)
    def _():
        result_ref[...] = total_s[...].astype(jnp.bfloat16)
        info = info_ref[...]
        scale = per_row(info, 1.0 + mod_ref[:, 2 * width : 3 * width], utts)
        gn = gn_s[...]
        unit = unit_s[...]
        grad = branch_ref[...].astype(jnp.float32) + normalise_back(gn * scale, unit, inv_s[:, :1])
        grad_ref[...] = grad
        low = grad.astype(jnp.bfloat16)
        grad_low_ref[...] = low
        back = mm(low, wout_ref[...].reshape(width, width), NT).astype(jnp.bfloat16)
        for s in range(groups):
            back_ref[s] = back[:, s * LANES : (s + 1) * LANES]
        sums_by_utt(sums_ref, 0, info, gn * unit, utts)
        sums_by_utt(sums_ref, width, info, gn, utts)


def middle(att, stream, info, modulation, cot, late, down_each, out_each, up_each, bias, utts):
    rows, width = stream.shape
    devices = late.shape[0]
    hidden = down_each * devices
    block = 512
    blocks = hidden // block
    halves = width // block
    groups = width // LANES
    out_at = down_each // out_each
    up_at = (down_each + out_each) // up_each

    def fixed(*shape):
        return pl.BlockSpec(shape, lambda b: (0,) * len(shape))

    def whole(*shape, dtype=jnp.bfloat16):
        return jax.ShapeDtypeStruct(shape, dtype)

    f32 = jnp.float32
    return pl.pallas_call(
        functools.partial(middle_kernel, utts=utts, blocks=blocks),
        grid=(blocks,),
        out_shape=(
            whole(rows, width),
            whole(width, rows),
            whole(width, rows),
            whole(hidden, rows),
            whole(rows, hidden),
            whole(rows, width, dtype=f32),
            whole(rows, width),
            whole(groups, rows, LANES),
            whole(utts, 2 * width, dtype=f32),
            whole(1, hidden, dtype=f32),
        ),
        in_specs=[
            fixed(groups, rows, LANES),
            fixed(rows, width),
            fixed(rows, LANES),
            fixed(utts, 4 * width),
            fixed(rows, width),
            pl.BlockSpec((devices, out_each, width), lambda b: (0, out_at, 0)),
            pl.BlockSpec((devices, up_each, block), lambda b: (0, up_at + b // halves, b % halves)),
            pl.BlockSpec((devices // blocks, down_each, width), lambda b: (b, 0, 0)),
            pl.BlockSpec((1, block), lambda b: (0, b)),
        ],
        out_specs=(
            fixed(rows, width),
            fixed(width, rows),
            fixed(width, rows),
            pl.BlockSpec((block, rows), lambda b: (b, 0)),
            pl.BlockSpec((rows, block), lambda b: (0, b)),
            fixed(rows, width),
            fixed(rows, width),
            fixed(groups, rows, LANES),
            fixed(utts, 2 * width),
            pl.BlockSpec((1, block), lambda b: (0, b)),
        ),
        scratch_shapes=[
            pltpu.VMEM((rows, width), f32),
            pltpu.VMEM((rows, width), f32),
            pltpu.VMEM((rows, LANES), f32),
            pltpu.VMEM((rows, width), f32),
            pltpu.VMEM((rows, width), f32),
            pltpu.VMEM((rows, width), jnp.bfloat16),
            pltpu.VMEM((rows, width), jnp.bfloat16),
        ],
        compiler_params=pltpu.CompilerParams(vmem_limit_bytes=VMEM),
        cost_estimate=pl.CostEstimate(
            flops=12 * rows * hidden * width, bytes_accessed=20 * width * width,
            transcendentals=rows * hidden,
        ),
        name="middle",
    )(att, stream, info, modulation, cot, late, late, late, bias)


def tail_kernel(held_ref, stream_ref, info_ref, mod_ref, mid_ref, w_ref, two_ref, bup_ref,
                *rest, utts):
    proj_ref, out_ref, sums_ref, gn_s = rest[-4:]
    p = pl.program_id(0)
    rows, width = stream_ref.shape
    groups = held_ref.shape[0]
    for s in range(groups):
        proj_ref[:, s * LANES : (s + 1) * LANES] = held_ref[s, 0]
    term = mm(proj_ref[...], w_ref[...].reshape(width, width), NT)

    @pl.when(p == 0)
    def _():
        gn_s[...] = term

    @pl.when(p > 0)
    def _():
        gn_s[...] += term

    @pl.when(p == 2)
    def _():
        info = info_ref[...]
        unit, inverse = normalise(stream_ref[...])
        scale = per_row(info, 1.0 + mod_ref[:, :width], utts)
        gn = gn_s[...]
        out_ref[...] = (mid_ref[...] + normalise_back(gn * scale, unit, inverse)).astype(jnp.bfloat16)
        sums_ref[0:utts, 2 * width :] = two_ref[...]
        sums_ref[utts : utts + 1, :] = bup_ref[...]
        sums_by_utt(sums_ref, 0, info, gn * unit, utts)
        sums_by_utt(sums_ref, width, info, gn, utts)


def tail(held, stream, info, modulation, mid, early, skip_each, qkv_each, two, bup, utts, after):
    rows, width = stream.shape
    devices = early.shape[0]
    groups = held.shape[0]
    first = skip_each // qkv_each

    def fixed(*shape):
        return pl.BlockSpec(shape, lambda p: (0,) * len(shape))

    return pl.pallas_call(
        functools.partial(tail_kernel, utts=utts),
        grid=(3,),
        out_shape=(
            jax.ShapeDtypeStruct((rows, 3 * width), jnp.bfloat16),
            jax.ShapeDtypeStruct((rows, width), jnp.bfloat16),
            jax.ShapeDtypeStruct((utts + 1, 4 * width), jnp.float32),
        ),
        in_specs=[
            pl.BlockSpec((groups, 1, rows, LANES), lambda p: (0, p, 0, 0)),
            fixed(rows, width),
            fixed(rows, LANES),
            fixed(utts, 4 * width),
            fixed(rows, width),
            pl.BlockSpec((devices, qkv_each, width), lambda p: (0, first + p, 0)),
            fixed(utts, 2 * width),
            fixed(1, 4 * width),
        ]
        + [pl.BlockSpec(memory_space=pl.ANY)] * len(after),
        out_specs=(
            pl.BlockSpec((rows, width), lambda p: (0, p)),
            fixed(rows, width),
            fixed(utts + 1, 4 * width),
        ),
        scratch_shapes=[pltpu.VMEM((rows, width), jnp.float32)],
        compiler_params=pltpu.CompilerParams(vmem_limit_bytes=VMEM),
        cost_estimate=pl.CostEstimate(
            flops=6 * rows * width * width, bytes_accessed=14 * width * width, transcendentals=0
        ),
        name="tail",
    )(held, stream, info, modulation, mid, early, two, bup, *after)


def outer_kernel(pick_ref, *refs, sizes, counts, batch, chosen, adds, extra):
    u = pl.program_id(0)
    out_refs = refs[len(refs) - chosen :] if adds else [refs[-1].at[n] for n in range(chosen)]
    came = refs[len(refs) - chosen - extra - 1] if adds else None
    at = 0
    start = 0
    row = 0
    for each, count in zip(sizes, counts):
        own = refs[at : at + chosen]
        other = refs[at + chosen : at + 2 * chosen]
        second, second_other = refs[at + 2 * chosen : at + 2 * chosen + 2]
        for j in range(count):
            @pl.when(u == start + j)
            def _(own=own, other=other, second=second, second_other=second_other, each=each, row=row):
                left = jnp.concatenate(
                    [
                        jnp.concatenate([one[...] for one in own], axis=0),
                        jnp.concatenate([one[...] for one in other], axis=0),
                    ],
                    axis=1,
                )
                right = jnp.concatenate([second[...], second_other[...]], axis=0)
                total = mm(left, right, NN)
                for n in range(chosen):
                    for z in range(batch):
                        low = (n * batch + z) * each
                        part = total[low : low + each]
                        if adds:
                            part = part + came[n, z, row : row + each, :].astype(jnp.float32)
                        out_refs[n][z, row : row + each, :] = part.astype(jnp.bfloat16)
            row += each
        start += count
        at += 2 * chosen + 2


def outer_plain(weights, picks, half, batch, wide, add):
    made = []
    for first, first_other, second, second_other in weights:
        block = first.shape[0] // lax.axis_size("seq")
        columns = second.shape[1] // 2
        total = 0.0
        for one, two in ((first, second), (first_other, second_other)):
            chosen = [
                lax.dynamic_slice_in_dim(one, picks[n] * block, block, axis=0)
                for n in range(picks.shape[0])
            ]
            total = total + mm(
                jnp.concatenate(chosen, axis=0), two[:, half * columns : (half + 1) * columns], NN
            )
        total = total.reshape(picks.shape[0], batch, block // batch, columns // wide, wide)
        total = total.transpose(0, 1, 3, 2, 4)
        made.append(total.reshape(picks.shape[0], batch, -1, wide))
    made = jnp.concatenate(made, axis=2)
    if add is None:
        return made.astype(jnp.bfloat16)
    return list((made + add.astype(jnp.float32)).astype(jnp.bfloat16))


def outer(weights, picks, half, batch, wide, add=None, after=()):
    chosen = picks.shape[0]
    seq = lax.axis_size("seq")
    blocks = [first.shape[0] // seq for first, _, _, _ in weights]
    sizes = [block // batch for block in blocks]
    counts = [second.shape[1] // 2 // wide for _, _, second, _ in weights]
    if any(block % LANES for block in blocks):
        return outer_plain(weights, picks, half, batch, wide, add)
    tokens = weights[0][0].shape[1]
    height = sum(e * c for e, c in zip(sizes, counts))
    shape = (batch, height, wide)
    specs = []
    operands = []
    start = 0
    flops = 0
    for (first, first_other, second, second_other), block, count in zip(weights, blocks, counts):
        def rows_at(n, block=block):
            return pl.BlockSpec((block, tokens), lambda u, pick: (pick[n], 0))

        def column_at(u, pick, start=start, count=count):
            return (0, half * count + jnp.clip(u - start, 0, count - 1))

        specs += [rows_at(n) for n in range(chosen)] * 2
        specs += [pl.BlockSpec((tokens, wide), column_at)] * 2
        operands += [first] * chosen + [first_other] * chosen + [second, second_other]
        start += count
        flops += 4 * tokens * chosen * block * count * wide
    whole = pl.BlockSpec(shape, lambda u, pick: (0, 0, 0))
    stacked = pl.BlockSpec((chosen,) + shape, lambda u, pick: (0, 0, 0, 0))
    made = jax.ShapeDtypeStruct((chosen,) + shape, jnp.bfloat16)
    return pl.pallas_call(
        functools.partial(
            outer_kernel, sizes=sizes, counts=counts, batch=batch, chosen=chosen,
            adds=add is not None, extra=len(after),
        ),
        grid_spec=pltpu.PrefetchScalarGridSpec(
            num_scalar_prefetch=1,
            grid=(sum(counts),),
            in_specs=specs
            + ([] if add is None else [stacked])
            + [pl.BlockSpec(memory_space=pl.ANY)] * len(after),
            out_specs=stacked if add is None else [whole] * chosen,
        ),
        out_shape=made if add is None else [jax.ShapeDtypeStruct(shape, jnp.bfloat16)] * chosen,
        compiler_params=pltpu.CompilerParams(vmem_limit_bytes=VMEM),
        cost_estimate=pl.CostEstimate(flops=2 * flops, bytes_accessed=flops // 300, transcendentals=0),
        name="outer",
    )(picks, *operands, *(() if add is None else (add,)), *after)


def merge_kernel(at_ref, *refs, sums, count):
    outs = refs[len(refs) - count :]
    for n in range(count):
        z = lax.rem(at_ref[0] + n, count)
        for h in range(sums):
            total = refs[2 * h][z].astype(jnp.float32) + refs[2 * h + 1][z].astype(jnp.float32)
            outs[n][h] = total.astype(jnp.bfloat16)


def merge(pairs, after):
    batch, height, wide = pairs[0][0].shape
    at = lax.axis_index("batch").reshape(1).astype(jnp.int32)
    vmem = pl.BlockSpec(memory_space=pltpu.VMEM)
    sums = len(pairs)
    size = sums * batch * height * wide
    return list(pl.pallas_call(
        functools.partial(merge_kernel, sums=sums, count=batch),
        out_shape=[jax.ShapeDtypeStruct((sums, height, wide), jnp.bfloat16)] * batch,
        in_specs=[pl.BlockSpec(memory_space=pltpu.SMEM)]
        + [vmem] * (2 * sums)
        + [pl.BlockSpec(memory_space=pl.ANY)] * len(after),
        out_specs=[vmem] * batch,
        cost_estimate=pl.CostEstimate(flops=size, bytes_accessed=6 * size, transcendentals=0),
        compiler_params=pltpu.CompilerParams(vmem_limit_bytes=VMEM // 2),
        name="merge",
    )(at, *[one for pair in pairs for one in pair], *after))


def finish_kernel(own_ref, *rest, count):
    total = own_ref[...].astype(jnp.float32)
    for n in range(count):
        total = total + rest[n][...].astype(jnp.float32)
    rest[-1][...] = total


def finish(own, came, after):
    vmem = pl.BlockSpec(memory_space=pltpu.VMEM)
    return pl.pallas_call(
        functools.partial(finish_kernel, count=len(came)),
        out_shape=jax.ShapeDtypeStruct(own.shape, jnp.float32),
        in_specs=[vmem] * (1 + len(came)) + [pl.BlockSpec(memory_space=pl.ANY)] * len(after),
        out_specs=vmem,
        cost_estimate=pl.CostEstimate(
            flops=4 * own.size, bytes_accessed=12 * own.size, transcendentals=0
        ),
        name="finish",
    )(own, *came, *after)


def tie_kernel(*refs):
    pass


def tie(value, after):
    anywhere = pl.BlockSpec(memory_space=pl.ANY)
    return pl.pallas_call(
        tie_kernel,
        out_shape=jax.ShapeDtypeStruct(value.shape, value.dtype),
        in_specs=[anywhere] * (1 + len(after)),
        out_specs=anywhere,
        input_output_aliases={0: 0},
        name="tie",
    )(value, *after)


def times(first_op, second_op):
    return lax.dot_general(first_op, second_op, NN, preferred_element_type=jnp.float32)


def swap(value, bit):
    size = lax.axis_size("seq")
    return lax.ppermute(value, "seq", [(i, i ^ bit) for i in range(size)])


def ahead(value, step):
    size = lax.axis_size("batch")
    return lax.ppermute(value, "batch", [(i, (i + step) % size) for i in range(size)])


class Sum:
    wide = 512

    def __init__(self, weights, half, bits):
        self.weights, self.half, self.bits = weights, half, bits
        self.seq = lax.axis_size("seq")
        self.batch = lax.axis_size("batch")
        self.next = 1

    def picks(self, sent):
        me = lax.axis_index("seq")
        first = me ^ self.bits[0] if sent else me
        found = [0]
        for bit in self.bits[:0:-1]:
            found = found + [f | bit for f in found]
        return (jnp.array(found, jnp.int32) ^ first).astype(jnp.int32)

    def send(self, after=()):
        sent = outer(self.weights, self.picks(True), self.half, self.batch, self.wide, None, after)
        self.came = swap(sent, self.bits[0])
        return [sent]

    def keep(self, after=()):
        self.total = list(
            outer(self.weights, self.picks(False), self.half, self.batch, self.wide, self.came, after)
        )

    def pass_on(self):
        count = len(self.total) // 2
        sent = self.total[count:]
        self.total = self.total[:count]
        self.came = [swap(one, self.bits[self.next]) for one in sent]
        self.next += 1
        return sent

    def take(self):
        self.total = [
            (a.astype(jnp.float32) + b.astype(jnp.float32)).astype(jnp.bfloat16)
            for a, b in zip(self.total, self.came)
        ]


class Sums:
    def __init__(self, weights, orders):
        self.weights = weights
        self.halves = [Sum(weights, half, bits) for half, bits in enumerate(orders)]

    def send(self, after=()):
        return sum([one.send(after) for one in self.halves], [])

    def came(self):
        return [one.came for one in self.halves]

    def keep(self, after=()):
        for one in self.halves:
            one.keep(after)
        return sum([one.pass_on() for one in self.halves], [])

    def spread(self, after=()):
        for one in self.halves:
            while one.next < len(one.bits):
                one.take()
                one.pass_on()
        pieces = merge([(one.total[0], one.came[0]) for one in self.halves], tuple(after))
        self.own = pieces[0]
        self.pieces = [ahead(piece, step) for step, piece in enumerate(pieces) if step]
        return pieces[1:]

    def result(self, after=()):
        total = finish(self.own, self.pieces, tuple(after))
        devices = lax.axis_size("seq") * lax.axis_size("batch")
        made = []
        at = 0
        for first, _, second, _ in self.weights:
            each = first.shape[0] // devices
            columns = second.shape[1] // 2
            count = columns // Sum.wide
            piece = total[:, at : at + each * count].reshape(2, count, each, Sum.wide)
            made.append(piece.transpose(2, 0, 1, 3).reshape(each, 2 * columns))
            at += each * count
        return made


def turn_tables(position):
    half = HD // 2
    lane = jnp.arange(LANES, dtype=jnp.int32)
    rates = jnp.exp((lane % half).astype(jnp.float32) * (-math.log(10000.0) / half))
    angles = position.astype(jnp.float32)[:, None] * rates[None, :]
    side = jnp.where((lane % HD) < half, -1.0, 1.0).astype(jnp.float32)
    return jnp.cos(angles), jnp.sin(angles) * side[None, :]


def all_pieces(value):
    batch = lax.axis_size("batch")
    place = lax.axis_index("batch")
    out = jnp.zeros((batch,) + value.shape, value.dtype)
    out = lax.dynamic_update_index_in_dim(out, value, place, 0)
    for step in range(1, batch):
        out = lax.dynamic_update_index_in_dim(
            out, ahead(value, step), (place - step) % batch, 0
        )
    return out


def seq_total(value):
    bit = 1
    while bit < lax.axis_size("seq"):
        value = value + swap(value, bit)
        bit *= 2
    return value


def shards(
    frames_in,
    skip_in,
    time_table,
    timestep,
    lengths,
    span_start,
    span_len,
    skip_proj,
    mod_proj,
    mod_bias,
    qkv_proj,
    out_proj,
    up_proj,
    up_bias,
    down_proj,
    cotangent,
):
    seq = lax.axis_size("seq")
    batch = lax.axis_size("batch")
    seq_at = lax.axis_index("seq")
    batch_at = lax.axis_index("batch")
    device = seq_at * batch + batch_at
    devices = seq * batch
    inputs = frames_in[0]
    skip_rows = skip_in[0]
    rows, width = inputs.shape
    hidden = up_proj.shape[1]
    frames = rows * seq
    heads = HEADS // seq
    utts = lengths.shape[1]

    early = jnp.concatenate(
        [skip_proj] + [qkv_proj[:, p * width : (p + 1) * width] for p in range(3)], axis=0
    )
    late = jnp.concatenate(
        [down_proj, out_proj]
        + [up_proj[:, p * width : (p + 1) * width] for p in range(hidden // width)],
        axis=0,
    )
    early = lax.all_gather(early, BOTH, axis=0, tiled=False)
    late = lax.all_gather(late, BOTH, axis=0, tiled=False)
    skip_each, qkv_each, out_each, up_each, down_each = (
        skip_proj.shape[0],
        qkv_proj.shape[0],
        out_proj.shape[0],
        up_proj.shape[0],
        down_proj.shape[0],
    )
    utt_lengths = lengths[0]
    ends = jnp.cumsum(utt_lengths).astype(jnp.int32)
    starts = ends - utt_lengths
    frame_ids = seq_at * rows + jnp.arange(rows, dtype=jnp.int32)
    group_ids = jnp.arange(frames, dtype=jnp.int32)

    def members(ids):
        return (ids[:, None] >= starts[None, :]) & (ids[:, None] < ends[None, :])

    member = members(frame_ids)
    member_int = member.astype(jnp.int32)
    position = frame_ids - jnp.sum(member_int * starts[None, :], axis=1)
    span_first = jnp.sum(member_int * span_start[0][None, :], axis=1)
    span_after = span_first + jnp.sum(member_int * span_len[0][None, :], axis=1)
    in_span = ((position >= span_first) & (position < span_after)).astype(jnp.float32)
    member_rows = member.astype(jnp.float32)
    group_position = group_ids - jnp.sum(members(group_ids).astype(jnp.int32) * starts[None, :], axis=1)
    cos, sin = turn_tables(position)
    group_cos, group_sin = turn_tables(group_position)

    steps = all_pieces(timestep[0]).reshape(-1)
    step_pick = (
        steps[:, None] == jnp.arange(time_table.shape[0], dtype=jnp.int32)[None, :]
    ).astype(jnp.float32)
    time_rows = jnp.dot(step_pick, time_table.astype(jnp.float32), precision=highest)
    silu_value, silu_pull = jax.vjp(jax.nn.silu, time_rows)
    time_vec = silu_value.astype(jnp.bfloat16)
    terms = times(time_vec, mod_proj)
    def placed(bias):
        return lax.dynamic_update_slice(
            jnp.zeros((4 * width,), jnp.float32), bias.astype(jnp.float32), (device * bias.shape[0],)
        )

    terms = (terms + placed(mod_bias)[None, :]).reshape(batch, utts, 4 * width)
    up_terms = jnp.broadcast_to(placed(up_bias), (batch, 1, 4 * width))
    terms = jnp.concatenate([terms, up_terms], axis=1)
    modulation = lax.dynamic_index_in_dim(terms, batch_at, 0, keepdims=False)
    for step in range(1, batch):
        modulation = modulation + ahead(
            lax.dynamic_index_in_dim(terms, (batch_at + step) % batch, 0, keepdims=False), step
        )
    modulation = seq_total(modulation)
    full_bup = modulation[utts:]
    modulation = modulation[:utts]
    info = jnp.pad(member_rows, ((0, 0), (0, LANES - utts)))
    branch = (cotangent[0].astype(jnp.float32) * in_span[:, None]).astype(jnp.bfloat16)
    joined = jnp.concatenate([inputs.T, skip_rows.T], axis=0)
    branch_pair = (branch, swap(branch, 1))
    joined_pair = (joined, swap(joined, 1))

    stream_in, sent, normed_one = front(
        inputs, skip_rows, info, modulation, early, skip_each, qkv_each, cos, sin, utts,
        (group_cos, group_sin, branch_pair[1], joined_pair[1]),
    )
    per_device = width // seq
    groups = width // LANES
    if per_device < LANES:
        sent = sent.reshape(groups, 3, rows, 2, per_device).transpose(0, 3, 1, 2, 4)
        sent = sent.reshape(seq, 3, rows, per_device)
        sent = jnp.pad(sent, ((0, 0), (0, 0), (0, 0), (0, LANES - per_device)))
    held = lax.all_to_all(sent, "seq", 0, 0, tiled=True)
    normed_one_pair = (normed_one, swap(normed_one, 1))
    head_out, log_sums = attend(held, ends, heads, 1024, 512)
    att = lax.all_to_all(
        head_out.reshape(seq, rows, LANES)[:, :, :per_device], "seq", 0, 0, tiled=True
    )
    if per_device < LANES:
        att = att.reshape(groups, 2, rows, per_device).transpose(0, 2, 1, 3).reshape(groups, rows, LANES)

    result, attended, normed_two, activated, grad_pre, grad_mid, grad_low, back, mod_two, bup_terms = middle(
        att, stream_in, info, modulation, branch, late, down_each, out_each, up_each, full_bup, utts
    )
    if per_device < LANES:
        back = back.reshape(groups, rows, 2, per_device).transpose(0, 2, 1, 3).reshape(seq, rows, per_device)
        back = jnp.pad(back, ((0, 0), (0, 0), (0, LANES - per_device)))
    back = lax.all_to_all(back, "seq", 0, 0, tiled=True).reshape(frames, LANES)
    high = [seq >> (i + 1) for i in range(seq.bit_length() - 2)]
    low = high[::-1]

    def pairs(first, second):
        return (first[0], first[1], second[0], second[1])

    def pair(value):
        return (value, swap(value, 1))

    first_weights = [
        pairs(pair(activated), branch_pair),
        pairs(pair(normed_two), pair(grad_pre)),
        pairs(pair(attended), pair(grad_low)),
    ]
    sums = Sums(first_weights, (low, high))
    waits = sums.send()

    grad_held = attend_back(
        held, back, head_out, log_sums, group_cos, group_sin, ends, heads, waits, 1024, 512
    )
    mark = (grad_held,)
    grad_held = tie(grad_held, sums.came())
    grad_held = lax.all_to_all(grad_held[..., :per_device], "seq", 0, 0, tiled=True)
    if per_device < LANES:
        grad_held = grad_held.reshape(groups, 2, 3, rows, per_device).transpose(0, 2, 3, 1, 4)
        grad_held = grad_held.reshape(groups, 3, rows, LANES)
    waits = sums.keep(mark)

    grad_projected, grad_stream, row_sums = tail(
        grad_held, stream_in, info, modulation, grad_mid, early, skip_each, qkv_each,
        mod_two, bup_terms, utts, waits,
    )
    row_sums = lax.all_gather(row_sums, BOTH, axis=0, tiled=False)
    last_weights = [
        pairs(joined_pair, pair(grad_stream)),
        pairs(normed_one_pair, pair(grad_projected)),
    ]
    last_sums = Sums(last_weights, (low, high))
    waits = last_sums.send()
    waits = sums.spread(waits)
    grad_inputs, grad_skip_rows = unjoin(grad_stream, early, skip_each, waits)
    waits = last_sums.keep((grad_inputs,))
    grad_down, grad_up, grad_out_w = sums.result(waits)
    last_sums.spread((grad_down,))
    grad_skip_w, grad_qkv_w = last_sums.result()

    row_sums = jnp.sum(row_sums.reshape(seq, batch, utts + 1, 4 * width), axis=0)
    grad_modulation = row_sums[:, :utts].reshape(batch * utts, 4 * width)
    grad_bup = lax.dynamic_slice_in_dim(
        jnp.sum(row_sums[:, utts], axis=0), device * up_bias.shape[0], up_bias.shape[0]
    )
    grad_bmod = lax.dynamic_slice_in_dim(
        jnp.sum(grad_modulation, axis=0), device * mod_bias.shape[0], mod_bias.shape[0]
    )
    grad_mod_w = jnp.dot(time_vec.astype(jnp.float32).T, grad_modulation, precision=highest)
    grad_time_vec = jnp.dot(grad_modulation, mod_proj.astype(jnp.float32).T, precision=highest)
    grad_table = jnp.dot(step_pick.T, silu_pull(grad_time_vec)[0], precision=highest)
    return (
        result[None],
        grad_inputs[None],
        grad_skip_rows[None],
        grad_table,
        grad_skip_w,
        grad_mod_w,
        grad_bmod,
        grad_qkv_w,
        grad_out_w,
        grad_up,
        grad_bup,
        grad_down,
    )


def solution(mesh):
    return jax.shard_map(
        shards,
        mesh=mesh,
        in_specs=(
            P("batch", "seq", None),
            P("batch", "seq", None),
            P(None, BOTH),
            P("batch", None),
            P("batch", None),
            P("batch", None),
            P("batch", None),
            P(BOTH, None),
            P(BOTH, None),
            P(BOTH),
            P(BOTH, None),
            P(BOTH, None),
            P(BOTH, None),
            P(BOTH),
            P(BOTH, None),
            P("batch", "seq", None),
        ),
        out_specs=(
            P("batch", "seq", None),
            P("batch", "seq", None),
            P("batch", "seq", None),
            P(None, BOTH),
            P(BOTH, None),
            P(BOTH, None),
            P(BOTH),
            P(BOTH, None),
            P(BOTH, None),
            P(BOTH, None),
            P(BOTH),
            P(BOTH, None),
        ),
        check_vma=False,
    )
```

```python
import functools
import math

import jax
import jax.numpy as jnp
from jax import lax
from jax.experimental import pallas as pl
from jax.experimental.pallas import tpu as pltpu
from jax.sharding import PartitionSpec as P

HEADS = 16
HD = 64
LANES = 128
MASKED = -(2.0 ** 100)
NORM_EPS = 1e-06
SMALL = pl.CostEstimate(flops=1024, bytes_accessed=1024, transcendentals=0)
VMEM = 60 * 1024 * 1024
BOTH = ("seq", "batch")
NT = (((1,), (1,)), ((), ()))
NN = (((1,), (0,)), ((), ()))
TN = (((0,), (0,)), ((), ()))
highest = lax.Precision.HIGHEST


def mm(a, b, dims):
    return lax.dot_general(a, b, dims, preferred_element_type=jnp.float32)


def utt_of(ends_ref, rows, utts):
    found = jnp.zeros_like(rows)
    for u in range(utts - 1):
        found = found + (rows >= ends_ref[u]).astype(jnp.int32)
    return found


def key_range(ends_ref, first, last, utts, frames):
    low = 0
    high = frames
    for u in range(utts - 1):
        low = jnp.where(first >= ends_ref[u], ends_ref[u], low)
    for u in reversed(range(utts - 1)):
        high = jnp.where(last < ends_ref[u], ends_ref[u], high)
    return low, high


def split3(x):
    a = x.astype(jnp.bfloat16).astype(jnp.float32)
    b = (x - a).astype(jnp.bfloat16).astype(jnp.float32)
    return a, b, x - a - b


def fwd_kernel(ends_ref, qkv_ref, out_ref, lse_ref, q_s, k_s, v_s, m_s, acc_s, *, heads, utts, bq, bk):
    sources, _, rows, _ = qkv_ref.shape
    frames = sources * rows

    def build(src, carry):
        at = pl.multiple_of(src * rows, rows)
        lane = lax.broadcasted_iota(jnp.int32, (rows, LANES), 1)
        row = lax.broadcasted_iota(jnp.int32, (rows, LANES), 0) + at
        utt = utt_of(ends_ref, row, utts)
        for h in range(heads):
            spare = (1 - h) * HD
            mine = (lane >= HD) if h else (lane < HD)
            slot = lane - spare
            is_slot = (slot >= 0) & (slot < utts)
            qf = jnp.where(is_slot & (slot != utt), MASKED, 0.0)
            kf = jnp.where(slot == utt, 1.0, 0.0)
            vf = jnp.where(slot == 0, 1.0, 0.0)
            for part, feat, dst in ((0, qf, q_s), (1, kf, k_s), (2, vf, v_s)):
                x = qkv_ref[src, part].astype(jnp.float32)
                dst[h, pl.ds(at, rows), :] = jnp.where(mine, x, feat).astype(jnp.bfloat16)
        return carry

    lax.fori_loop(0, sources, build, 0)

    def q_block(i, carry):
        at = pl.multiple_of(i * bq, bq)
        low, high = key_range(ends_ref, at, at + bq - 1, utts, frames)
        m_s[...] = jnp.full(m_s.shape, -3.0e38, jnp.float32)
        acc_s[...] = jnp.zeros(acc_s.shape, jnp.float32)

        def k_block(j, inner):
            kat = pl.multiple_of(j * bk, bk)
            for h in range(heads):
                s = mm(q_s[h, pl.ds(at, bq), :], k_s[h, pl.ds(kat, bk), :], NT)
                old = m_s[h]
                top = jnp.maximum(old, jnp.max(s, axis=1, keepdims=True))
                alpha = jnp.exp(old - top)
                p = jnp.exp(s - top[:, :1]).astype(jnp.bfloat16)
                acc_s[h] = acc_s[h] * alpha + mm(p, v_s[h, pl.ds(kat, bk), :], NN)
                m_s[h] = top
            return inner

        lax.fori_loop(low // bk, (high + bk - 1) // bk, k_block, 0)
        lane = lax.broadcasted_iota(jnp.int32, (bq, LANES), 1)
        out = None
        lse = None
        for h in range(heads):
            spare = (1 - h) * HD
            acc = acc_s[h]
            total = acc[:, spare : spare + 1]
            o = acc / total
            l = m_s[h] + jnp.log(total)
            out = o if out is None else jnp.where(lane < HD, out, o)
            lse = l if lse is None else jnp.where(lane < HD, lse, l)
        out_ref[pl.ds(at, bq), :] = out.astype(jnp.bfloat16)
        lse_ref[pl.ds(at, bq), :] = lse
        return carry

    lax.fori_loop(0, frames // bq, q_block, 0)


def attend(qkv, ends, heads, bq, bk):
    sources, _, rows, _ = qkv.shape
    frames = sources * rows
    utts = ends.shape[0]
    return pl.pallas_call(
        functools.partial(fwd_kernel, heads=heads, utts=utts, bq=bq, bk=bk),
        out_shape=(
            jax.ShapeDtypeStruct((frames, LANES), jnp.bfloat16),
            jax.ShapeDtypeStruct((frames, LANES), jnp.float32),
        ),
        in_specs=[pl.BlockSpec(memory_space=pltpu.SMEM), pl.BlockSpec(memory_space=pltpu.VMEM)],
        out_specs=(pl.BlockSpec(memory_space=pltpu.VMEM), pl.BlockSpec(memory_space=pltpu.VMEM)),
        scratch_shapes=[pltpu.VMEM((heads, frames, LANES), jnp.bfloat16)] * 3
        + [pltpu.VMEM((heads, bq, LANES), jnp.float32)] * 2,
        compiler_params=pltpu.CompilerParams(vmem_limit_bytes=VMEM),
        cost_estimate=pl.CostEstimate(
            flops=40 * heads * frames * frames * HD, bytes_accessed=frames * LANES * 12,
            transcendentals=heads * frames * frames,
        ),
        name="attend",
    )(ends, qkv)


def bwd_kernel(
    ends_ref, qkv_ref, da_ref, out_ref, lse_ref, cos_ref, sin_ref, *rest, heads, utts, bq, bk
):
    grad_ref, q_s, k_s, v_s, d_s, gq_s, gk_s, gv_s = rest[-8:]
    sources, _, rows, _ = qkv_ref.shape
    frames = sources * rows

    def build(src, carry):
        at = pl.multiple_of(src * rows, rows)
        lane = lax.broadcasted_iota(jnp.int32, (rows, LANES), 1)
        row = lax.broadcasted_iota(jnp.int32, (rows, LANES), 0) + at
        utt = utt_of(ends_ref, row, utts)
        da = da_ref[pl.ds(at, rows), :].astype(jnp.float32)
        prod = da * out_ref[pl.ds(at, rows), :].astype(jnp.float32)
        lse = lse_ref[pl.ds(at, rows), :]
        for h in range(heads):
            spare = (1 - h) * HD
            mine = (lane >= HD) if h else (lane < HD)
            slot = lane - spare
            is_slot = (slot >= 0) & (slot < utts)
            delta = jnp.sum(jnp.where(mine, prod, 0.0), axis=1, keepdims=True)
            l3 = split3(-lse[:, h * HD : h * HD + 1])
            d3 = split3(-delta)
            qf = jnp.where(is_slot & (slot != utt), MASKED, 0.0)
            df = jnp.zeros_like(qf)
            for n in range(3):
                qf = jnp.where(slot == utts + n, l3[n], qf)
                df = jnp.where(slot == n, d3[n], df)
            kf = jnp.where((slot == utt) | ((slot >= utts) & (slot < utts + 3)), 1.0, 0.0)
            vf = jnp.where((slot >= 0) & (slot < 3), 1.0, 0.0)
            for x, feat, dst in (
                (qkv_ref[src, 0], qf, q_s), (qkv_ref[src, 1], kf, k_s), (qkv_ref[src, 2], vf, v_s),
            ):
                dst[h, pl.ds(at, rows), :] = jnp.where(mine, x.astype(jnp.float32), feat).astype(jnp.bfloat16)
            d_s[h, pl.ds(at, rows), :] = jnp.where(mine, da, df).astype(jnp.bfloat16)
        gq_s[:, pl.ds(at, rows), :] = jnp.zeros((heads, rows, LANES), jnp.float32)
        return carry

    lax.fori_loop(0, sources, build, 0)

    def k_block(j, carry):
        kat = pl.multiple_of(j * bk, bk)
        low, high = key_range(ends_ref, kat, kat + bk - 1, utts, frames)
        gk_s[:, pl.ds(kat, bk), :] = jnp.zeros((heads, bk, LANES), jnp.float32)
        gv_s[:, pl.ds(kat, bk), :] = jnp.zeros((heads, bk, LANES), jnp.float32)

        def q_block(i, inner):
            at = pl.multiple_of(i * bq, bq)
            for h in range(heads):
                q = q_s[h, pl.ds(at, bq), :]
                d = d_s[h, pl.ds(at, bq), :]
                k = k_s[h, pl.ds(kat, bk), :]
                p = jnp.exp(mm(k, q, NT))
                ds = (p * mm(v_s[h, pl.ds(kat, bk), :], d, NT)).astype(jnp.bfloat16)
                gv_s[h, pl.ds(kat, bk), :] += mm(p.astype(jnp.bfloat16), d, NN)
                gk_s[h, pl.ds(kat, bk), :] += mm(ds, q, NN)
                gq_s[h, pl.ds(at, bq), :] += mm(ds, k, TN)
            return inner

        lax.fori_loop(low // bq, (high + bq - 1) // bq, q_block, 0)
        return carry

    lax.fori_loop(0, frames // bk, k_block, 0)

    def finish(src, carry):
        at = pl.multiple_of(src * rows, rows)
        lane = lax.broadcasted_iota(jnp.int32, (rows, LANES), 1)
        first = (lane % HD) < HD // 2
        cos = cos_ref[pl.ds(at, rows), :]
        sin = sin_ref[pl.ds(at, rows), :]

        def both(ref):
            x = ref[0, pl.ds(at, rows), :]
            return jnp.where(lane < HD, x, ref[1, pl.ds(at, rows), :]) if heads == 2 else x

        def unturn(x):
            partner = jnp.where(first, pltpu.roll(x, LANES - HD // 2, 1), pltpu.roll(x, HD // 2, 1))
            return x * cos - partner * sin

        grad_ref[src, 0] = (unturn(both(gq_s)) * HD ** -0.5).astype(jnp.bfloat16)
        grad_ref[src, 1] = unturn(both(gk_s)).astype(jnp.bfloat16)
        grad_ref[src, 2] = both(gv_s).astype(jnp.bfloat16)
        return carry

    lax.fori_loop(0, sources, finish, 0)


def attend_back(qkv, grad_out, out, lse, cos, sin, ends, heads, after, bq, bk):
    sources, _, rows, _ = qkv.shape
    frames = sources * rows
    utts = ends.shape[0]
    vmem = pl.BlockSpec(memory_space=pltpu.VMEM)
    return pl.pallas_call(
        functools.partial(bwd_kernel, heads=heads, utts=utts, bq=bq, bk=bk),
        out_shape=jax.ShapeDtypeStruct(qkv.shape, jnp.bfloat16),
        in_specs=[pl.BlockSpec(memory_space=pltpu.SMEM)]
        + [vmem] * 6
        + [pl.BlockSpec(memory_space=pl.ANY)] * len(after),
        out_specs=vmem,
        scratch_shapes=[pltpu.VMEM((heads, frames, LANES), jnp.bfloat16)] * 4
        + [pltpu.VMEM((heads, frames, LANES), jnp.float32)] * 3,
        compiler_params=pltpu.CompilerParams(vmem_limit_bytes=VMEM),
        cost_estimate=pl.CostEstimate(
            flops=64 * heads * frames * frames * HD, bytes_accessed=frames * LANES * 24,
            transcendentals=heads * frames * frames,
        ),
        name="attend_back",
    )(ends, qkv, grad_out, out, lse, cos, sin, *after)


def outgoing_kernel(rel_ref, grad_ref, low_ref, high_ref, *rest):
    out_ref, total_s = rest[-2:]
    src = pl.program_id(0)
    rows = grad_ref.shape[2]
    grads = jnp.concatenate([grad_ref[0, part] for part in range(3)], axis=1)
    normed = jnp.concatenate([low_ref[0], high_ref[0]], axis=1)
    term = mm(normed, grads, TN)
    for part in range(3):
        out_ref[src, part, 0:rows] = grad_ref[0, part]

    @pl.when(src == 0)
    def _():
        total_s[...] = term

    @pl.when(src > 0)
    def _():
        total_s[...] += term

    @pl.when(src == pl.num_programs(0) - 1)
    def _():
        total = total_s[...].astype(jnp.bfloat16)
        each = out_ref.shape[2] - rows
        for dest in range(out_ref.shape[0]):
            for part in range(3):
                out_ref[dest, part, rows:] = total[
                    dest * each : (dest + 1) * each, part * LANES : (part + 1) * LANES
                ]


def outgoing(rel, grads, halves, after):
    sources, _, rows, _ = grads.shape
    half = halves[0].shape[2]
    each = 2 * half // sources
    shape = (sources, 3, rows + each, LANES)
    side = pl.BlockSpec((1, rows, half), lambda i, rel: (rel[i], 0, 0))
    return pl.pallas_call(
        outgoing_kernel,
        grid_spec=pltpu.PrefetchScalarGridSpec(
            num_scalar_prefetch=1,
            grid=(sources,),
            in_specs=[pl.BlockSpec((1, 3, rows, LANES), lambda i, rel: (i, 0, 0, 0)), side, side]
            + [pl.BlockSpec(memory_space=pl.ANY)] * len(after),
            out_specs=pl.BlockSpec(shape, lambda i, rel: (0, 0, 0, 0)),
            scratch_shapes=[pltpu.VMEM((2 * half, 3 * LANES), jnp.float32)],
        ),
        out_shape=jax.ShapeDtypeStruct(shape, jnp.bfloat16),
        cost_estimate=pl.CostEstimate(
            flops=12 * rows * sources * half * LANES, bytes_accessed=16 * half * half, transcendentals=0
        ),
        compiler_params=pltpu.CompilerParams(vmem_limit_bytes=VMEM),
        name="outgoing",
    )(rel, grads, *halves, *after)


def unjoin_kernel(grad_ref, weight_ref, *rest):
    width = grad_ref.shape[1]
    i = pl.program_id(0)
    made = mm(grad_ref[...], weight_ref[...].reshape(-1, width), NT).astype(jnp.bfloat16)

    @pl.when(i < 2)
    def _():
        rest[-2][...] = made

    @pl.when(i >= 2)
    def _():
        rest[-1][...] = made


def unjoin(grad, early, skip_each, after):
    rows, width = grad.shape
    devices = early.shape[0]
    half = width // 2
    return pl.pallas_call(
        unjoin_kernel,
        grid=(4,),
        out_shape=[jax.ShapeDtypeStruct((rows, width), jnp.bfloat16)] * 2,
        in_specs=[
            pl.BlockSpec((rows, width), lambda i: (0, 0)),
            pl.BlockSpec((devices // 4, skip_each, width), lambda i: (i, 0, 0)),
        ]
        + [pl.BlockSpec(memory_space=pl.ANY)] * len(after),
        out_specs=[
            pl.BlockSpec((rows, half), lambda i: (0, jnp.minimum(i, 1))),
            pl.BlockSpec((rows, half), lambda i: (0, jnp.maximum(i - 2, 0))),
        ],
        cost_estimate=pl.CostEstimate(
            flops=4 * rows * width * width, bytes_accessed=6 * width * width, transcendentals=0
        ),
        compiler_params=pltpu.CompilerParams(vmem_limit_bytes=VMEM),
        name="unjoin",
    )(grad, early, *after)


def normalise(hidden):
    centred = hidden - jnp.mean(hidden, axis=-1, keepdims=True)
    inverse = lax.rsqrt(jnp.mean(centred * centred, axis=-1, keepdims=True) + NORM_EPS)
    return centred * inverse, inverse


def normalise_back(grad, normed, inverse):
    return inverse * (
        grad
        - jnp.mean(grad, axis=-1, keepdims=True)
        - normed * jnp.mean(grad * normed, axis=-1, keepdims=True)
    )


def per_row(info, table, utts):
    total = info[:, 0:1] * table[0:1]
    for u in range(1, utts):
        total = total + info[:, u : u + 1] * table[u : u + 1]
    return total


def sums_by_utt(ref, at, info, value, utts):
    width = value.shape[1]
    for u in range(utts):
        ref[u : u + 1, at : at + width] = jnp.sum(info[:, u : u + 1] * value, axis=0, keepdims=True)


def gelu_parts(x):
    rate = math.sqrt(2.0 / math.pi)
    square = x * x
    inner = jnp.tanh(x * (rate + rate * 0.044715 * square))
    half = 0.5 + 0.5 * inner
    value = x * half
    slope = half + 0.5 * x * (1.0 - inner * inner) * (rate + 3 * rate * 0.044715 * square)
    return value, slope


def front_kernel(frames_ref, skip_ref, info_ref, mod_ref, weight_ref, *rest, utts, steps):
    stream_ref, normed_low_ref, normed_high_ref = rest[-3:]
    i = pl.program_id(0)
    width = stream_ref.shape[1]
    half = width // 2
    weight = weight_ref[...].reshape(-1, width)
    depth = weight.shape[0]

    for n in range(steps):
        @pl.when(i == n)
        def _(n=n):
            source = frames_ref if n * depth < width else skip_ref
            at = n * depth % width
            term = mm(source[:, at : at + depth], weight, NN)
            stream_ref[...] = term if n == 0 else stream_ref[...] + term

    @pl.when(i == steps - 1)
    def _():
        info = info_ref[...]
        unit, _unused = normalise(stream_ref[...])
        scale = per_row(info, 1.0 + mod_ref[:, :width], utts)
        shift = per_row(info, mod_ref[:, width : 2 * width], utts)
        normed = (unit * scale + shift).astype(jnp.bfloat16)
        normed_low_ref[...] = normed[:, :half]
        normed_high_ref[...] = normed[:, half:]


def front(frames, skip, info, modulation, weights, utts, after):
    rows, width = frames.shape
    devices, each, _ = weights.shape
    half = width // 2
    steps = 4

    def fixed(*shape):
        return pl.BlockSpec(shape, lambda i: (0,) * len(shape))

    return pl.pallas_call(
        functools.partial(front_kernel, utts=utts, steps=steps),
        grid=(steps,),
        in_specs=[
            fixed(rows, width),
            fixed(rows, width),
            fixed(rows, LANES),
            fixed(utts, 4 * width),
            pl.BlockSpec((devices // steps, each, width), lambda i: (i, 0, 0)),
        ]
        + [pl.BlockSpec(memory_space=pl.ANY)] * len(after),
        out_specs=(fixed(rows, width), fixed(rows, half), fixed(rows, half)),
        out_shape=(
            jax.ShapeDtypeStruct((rows, width), jnp.float32),
            jax.ShapeDtypeStruct((rows, half), jnp.bfloat16),
            jax.ShapeDtypeStruct((rows, half), jnp.bfloat16),
        ),
        compiler_params=pltpu.CompilerParams(vmem_limit_bytes=VMEM),
        cost_estimate=pl.CostEstimate(
            flops=4 * rows * width * width, bytes_accessed=8 * width * width, transcendentals=0
        ),
        name="front",
    )(frames, skip, info, modulation, weights, *after)


def project_kernel(rel_ref, low_ref, high_ref, weight_ref, cos_ref, sin_ref, *rest):
    out_ref = rest[-1]
    normed = jnp.concatenate([low_ref[0], high_ref[0]], axis=1)
    turned = mm(normed, weight_ref[...], NN)
    lane = lax.broadcasted_iota(jnp.int32, (turned.shape[0], LANES), 1)
    first = (lane % HD) < HD // 2
    for part in range(3):
        x = turned[:, part * LANES : (part + 1) * LANES]
        if part < 2:
            partner = jnp.where(first, pltpu.roll(x, LANES - HD // 2, 1), pltpu.roll(x, HD // 2, 1))
            x = x * cos_ref[...] + partner * sin_ref[...]
        if part == 0:
            x = x * HD ** -0.5
        out_ref[0, part] = x.astype(jnp.bfloat16)


def project(rel, halves, weight, cos, sin, after):
    sources, rows, half = halves[0].shape
    side = pl.BlockSpec((1, rows, half), lambda i, rel: (rel[i], 0, 0))
    table = pl.BlockSpec((rows, LANES), lambda i, rel: (i, 0))
    return pl.pallas_call(
        project_kernel,
        grid_spec=pltpu.PrefetchScalarGridSpec(
            num_scalar_prefetch=1,
            grid=(sources,),
            in_specs=[side, side, pl.BlockSpec(weight.shape, lambda i, rel: (0, 0)), table, table]
            + [pl.BlockSpec(memory_space=pl.ANY)] * len(after),
            out_specs=pl.BlockSpec((1, 3, rows, LANES), lambda i, rel: (i, 0, 0, 0)),
        ),
        out_shape=jax.ShapeDtypeStruct((sources, 3, rows, LANES), jnp.bfloat16),
        compiler_params=pltpu.CompilerParams(vmem_limit_bytes=VMEM),
        cost_estimate=pl.CostEstimate(
            flops=12 * rows * sources * half * LANES, bytes_accessed=16 * half * half, transcendentals=0
        ),
        name="project",
    )(rel, *halves, weight, cos, sin, *after)


def middle_kernel(att_ref, stream_ref, info_ref, mod_ref, branch_ref, wout_ref, wup_ref, wdown_ref, bias_ref,
                  result_ref, attended_ref, normed_ref, act_ref, pre_ref, grad_ref, grad_low_ref,
                  back_ref, sums_ref, bup_ref,
                  mid_s, unit_s, inv_s, total_s, gn_s, att_s, normed_s, *, utts, blocks):
    b = pl.program_id(0)
    rows, width = stream_ref.shape
    groups = att_ref.shape[0]

    @pl.when(b == 0)
    def _():
        for s in range(groups):
            att_s[:, s * LANES : (s + 1) * LANES] = att_ref[s]
            attended_ref[s * LANES : (s + 1) * LANES, :] = att_ref[s].T
        mid = stream_ref[...] + mm(att_s[...], wout_ref[...].reshape(width, width), NN)
        mid_s[...] = mid
        unit, inverse = normalise(mid)
        unit_s[...] = unit
        inv_s[...] = jnp.broadcast_to(inverse, inv_s.shape)
        info = info_ref[...]
        scale = per_row(info, 1.0 + mod_ref[:, 2 * width : 3 * width], utts)
        shift = per_row(info, mod_ref[:, 3 * width :], utts)
        normed = (unit * scale + shift).astype(jnp.bfloat16)
        normed_s[...] = normed
        normed_ref[...] = normed.T

    up = wup_ref[...].reshape(width, -1)
    down = wdown_ref[...].reshape(-1, width)
    value, slope = gelu_parts(mm(normed_s[...], up, NN) + bias_ref[...])
    act = value.astype(jnp.bfloat16)
    act_ref[...] = act.T
    term = mm(act, down, NN)
    pre = (mm(branch_ref[...], down, NT) * slope).astype(jnp.bfloat16)
    pre_ref[...] = pre
    bup_ref[...] = jnp.sum(pre.astype(jnp.float32), axis=0, keepdims=True)
    grad_term = mm(pre, up, NT)

    @pl.when(b == 0)
    def _():
        total_s[...] = mid_s[...] + term
        gn_s[...] = grad_term

    @pl.when(b > 0)
    def _():
        total_s[...] += term
        gn_s[...] += grad_term

    @pl.when(b == blocks - 1)
    def _():
        result_ref[...] = total_s[...].astype(jnp.bfloat16)
        info = info_ref[...]
        scale = per_row(info, 1.0 + mod_ref[:, 2 * width : 3 * width], utts)
        gn = gn_s[...]
        unit = unit_s[...]
        grad = branch_ref[...].astype(jnp.float32) + normalise_back(gn * scale, unit, inv_s[:, :1])
        grad_ref[...] = grad
        low = grad.astype(jnp.bfloat16)
        grad_low_ref[...] = low
        back = mm(low, wout_ref[...].reshape(width, width), NT).astype(jnp.bfloat16)
        for s in range(groups):
            back_ref[s] = back[:, s * LANES : (s + 1) * LANES]
        sums_by_utt(sums_ref, 0, info, gn * unit, utts)
        sums_by_utt(sums_ref, width, info, gn, utts)


def middle(att, stream, info, modulation, cot, late, down_each, out_each, up_each, bias, utts):
    rows, width = stream.shape
    devices = late.shape[0]
    hidden = down_each * devices
    block = 512
    blocks = hidden // block
    halves = width // block
    groups = width // LANES
    out_at = down_each // out_each
    up_at = (down_each + out_each) // up_each

    def fixed(*shape):
        return pl.BlockSpec(shape, lambda b: (0,) * len(shape))

    def whole(*shape, dtype=jnp.bfloat16):
        return jax.ShapeDtypeStruct(shape, dtype)

    f32 = jnp.float32
    return pl.pallas_call(
        functools.partial(middle_kernel, utts=utts, blocks=blocks),
        grid=(blocks,),
        out_shape=(
            whole(rows, width),
            whole(width, rows),
            whole(width, rows),
            whole(hidden, rows),
            whole(rows, hidden),
            whole(rows, width, dtype=f32),
            whole(rows, width),
            whole(groups, rows, LANES),
            whole(utts, 2 * width, dtype=f32),
            whole(1, hidden, dtype=f32),
        ),
        in_specs=[
            fixed(groups, rows, LANES),
            fixed(rows, width),
            fixed(rows, LANES),
            fixed(utts, 4 * width),
            fixed(rows, width),
            pl.BlockSpec((devices, out_each, width), lambda b: (0, out_at, 0)),
            pl.BlockSpec((devices, up_each, block), lambda b: (0, up_at + b // halves, b % halves)),
            pl.BlockSpec((devices // blocks, down_each, width), lambda b: (b, 0, 0)),
            pl.BlockSpec((1, block), lambda b: (0, b)),
        ],
        out_specs=(
            fixed(rows, width),
            fixed(width, rows),
            fixed(width, rows),
            pl.BlockSpec((block, rows), lambda b: (b, 0)),
            pl.BlockSpec((rows, block), lambda b: (0, b)),
            fixed(rows, width),
            fixed(rows, width),
            fixed(groups, rows, LANES),
            fixed(utts, 2 * width),
            pl.BlockSpec((1, block), lambda b: (0, b)),
        ),
        scratch_shapes=[
            pltpu.VMEM((rows, width), f32),
            pltpu.VMEM((rows, width), f32),
            pltpu.VMEM((rows, LANES), f32),
            pltpu.VMEM((rows, width), f32),
            pltpu.VMEM((rows, width), f32),
            pltpu.VMEM((rows, width), jnp.bfloat16),
            pltpu.VMEM((rows, width), jnp.bfloat16),
        ],
        compiler_params=pltpu.CompilerParams(vmem_limit_bytes=VMEM),
        cost_estimate=pl.CostEstimate(
            flops=12 * rows * hidden * width, bytes_accessed=20 * width * width,
            transcendentals=rows * hidden,
        ),
        name="middle",
    )(att, stream, info, modulation, cot, late, late, late, bias)


def tail_kernel(held_ref, stream_ref, info_ref, mod_ref, mid_ref, w_ref, two_ref, bup_ref,
                *rest, utts):
    out_ref, sums_ref, proj_s, gn_s = rest[-4:]
    p = pl.program_id(0)
    rows, width = stream_ref.shape
    groups = held_ref.shape[0]
    for s in range(groups):
        proj_s[:, s * LANES : (s + 1) * LANES] = held_ref[s, 0]
    term = mm(proj_s[...], w_ref[...].reshape(width, width), NT)

    @pl.when(p == 0)
    def _():
        gn_s[...] = term

    @pl.when(p > 0)
    def _():
        gn_s[...] += term

    @pl.when(p == 2)
    def _():
        info = info_ref[...]
        unit, inverse = normalise(stream_ref[...])
        scale = per_row(info, 1.0 + mod_ref[:, :width], utts)
        gn = gn_s[...]
        out_ref[...] = (mid_ref[...] + normalise_back(gn * scale, unit, inverse)).astype(jnp.bfloat16)
        sums_ref[0:utts, 2 * width :] = two_ref[...]
        sums_ref[utts : utts + 1, :] = bup_ref[...]
        sums_by_utt(sums_ref, 0, info, gn * unit, utts)
        sums_by_utt(sums_ref, width, info, gn, utts)


def tail(held, stream, info, modulation, mid, early, skip_each, qkv_each, two, bup, utts, after):
    rows, width = stream.shape
    devices = early.shape[0]
    groups = held.shape[0]
    first = skip_each // qkv_each

    def fixed(*shape):
        return pl.BlockSpec(shape, lambda p: (0,) * len(shape))

    return pl.pallas_call(
        functools.partial(tail_kernel, utts=utts),
        grid=(3,),
        out_shape=(
            jax.ShapeDtypeStruct((rows, width), jnp.bfloat16),
            jax.ShapeDtypeStruct((utts + 1, 4 * width), jnp.float32),
        ),
        in_specs=[
            pl.BlockSpec((groups, 1, rows, LANES), lambda p: (0, p, 0, 0)),
            fixed(rows, width),
            fixed(rows, LANES),
            fixed(utts, 4 * width),
            fixed(rows, width),
            pl.BlockSpec((devices, qkv_each, width), lambda p: (0, first + p, 0)),
            fixed(utts, 2 * width),
            fixed(1, 4 * width),
        ]
        + [pl.BlockSpec(memory_space=pl.ANY)] * len(after),
        out_specs=(
            fixed(rows, width),
            fixed(utts + 1, 4 * width),
        ),
        scratch_shapes=[
            pltpu.VMEM((rows, width), jnp.bfloat16),
            pltpu.VMEM((rows, width), jnp.float32),
        ],
        compiler_params=pltpu.CompilerParams(vmem_limit_bytes=VMEM),
        cost_estimate=pl.CostEstimate(
            flops=6 * rows * width * width, bytes_accessed=14 * width * width, transcendentals=0
        ),
        name="tail",
    )(held, stream, info, modulation, mid, early, two, bup, *after)


def outer_kernel(pick_ref, *refs, sizes, counts, batch, chosen, adds, extra):
    u = pl.program_id(0)
    out_refs = refs[len(refs) - chosen :] if adds else [refs[-1].at[n] for n in range(chosen)]
    came = refs[len(refs) - chosen - extra - 1] if adds else None
    at = 0
    start = 0
    row = 0
    for each, count in zip(sizes, counts):
        own = refs[at : at + chosen]
        other = refs[at + chosen : at + 2 * chosen]
        second, second_other = refs[at + 2 * chosen : at + 2 * chosen + 2]
        for j in range(count):
            @pl.when(u == start + j)
            def _(own=own, other=other, second=second, second_other=second_other, each=each, row=row):
                left = jnp.concatenate(
                    [
                        jnp.concatenate([one[...] for one in own], axis=0),
                        jnp.concatenate([one[...] for one in other], axis=0),
                    ],
                    axis=1,
                )
                right = jnp.concatenate([second[...], second_other[...]], axis=0)
                total = mm(left, right, NN)
                for n in range(chosen):
                    for z in range(batch):
                        low = (n * batch + z) * each
                        part = total[low : low + each]
                        if adds:
                            part = part + came[n, z, row : row + each, :].astype(jnp.float32)
                        out_refs[n][z, row : row + each, :] = part.astype(jnp.bfloat16)
            row += each
        start += count
        at += 2 * chosen + 2


def outer_plain(weights, picks, half, batch, wide, add):
    made = []
    for first, first_other, second, second_other in weights:
        block = first.shape[0] // lax.axis_size("seq")
        columns = second.shape[1] // 2
        total = 0.0
        for one, two in ((first, second), (first_other, second_other)):
            chosen = [
                lax.dynamic_slice_in_dim(one, picks[n] * block, block, axis=0)
                for n in range(picks.shape[0])
            ]
            total = total + mm(
                jnp.concatenate(chosen, axis=0), two[:, half * columns : (half + 1) * columns], NN
            )
        total = total.reshape(picks.shape[0], batch, block // batch, columns // wide, wide)
        total = total.transpose(0, 1, 3, 2, 4)
        made.append(total.reshape(picks.shape[0], batch, -1, wide))
    made = jnp.concatenate(made, axis=2)
    if add is None:
        return made.astype(jnp.bfloat16)
    return list((made + add.astype(jnp.float32)).astype(jnp.bfloat16))


def outer(weights, picks, half, batch, wide, add=None, after=()):
    chosen = picks.shape[0]
    seq = lax.axis_size("seq")
    blocks = [first.shape[0] // seq for first, _, _, _ in weights]
    sizes = [block // batch for block in blocks]
    counts = [second.shape[1] // 2 // wide for _, _, second, _ in weights]
    if any(block % LANES for block in blocks):
        return outer_plain(weights, picks, half, batch, wide, add)
    tokens = weights[0][0].shape[1]
    height = sum(e * c for e, c in zip(sizes, counts))
    shape = (batch, height, wide)
    specs = []
    operands = []
    start = 0
    flops = 0
    for (first, first_other, second, second_other), block, count in zip(weights, blocks, counts):
        def rows_at(n, block=block):
            return pl.BlockSpec((block, tokens), lambda u, pick: (pick[n], 0))

        def column_at(u, pick, start=start, count=count):
            return (0, half * count + jnp.clip(u - start, 0, count - 1))

        specs += [rows_at(n) for n in range(chosen)] * 2
        specs += [pl.BlockSpec((tokens, wide), column_at)] * 2
        operands += [first] * chosen + [first_other] * chosen + [second, second_other]
        start += count
        flops += 4 * tokens * chosen * block * count * wide
    whole = pl.BlockSpec(shape, lambda u, pick: (0, 0, 0))
    stacked = pl.BlockSpec((chosen,) + shape, lambda u, pick: (0, 0, 0, 0))
    made = jax.ShapeDtypeStruct((chosen,) + shape, jnp.bfloat16)
    return pl.pallas_call(
        functools.partial(
            outer_kernel, sizes=sizes, counts=counts, batch=batch, chosen=chosen,
            adds=add is not None, extra=len(after),
        ),
        grid_spec=pltpu.PrefetchScalarGridSpec(
            num_scalar_prefetch=1,
            grid=(sum(counts),),
            in_specs=specs
            + ([] if add is None else [stacked])
            + [pl.BlockSpec(memory_space=pl.ANY)] * len(after),
            out_specs=stacked if add is None else [whole] * chosen,
        ),
        out_shape=made if add is None else [jax.ShapeDtypeStruct(shape, jnp.bfloat16)] * chosen,
        compiler_params=pltpu.CompilerParams(vmem_limit_bytes=VMEM),
        cost_estimate=pl.CostEstimate(flops=2 * flops, bytes_accessed=flops // 300, transcendentals=0),
        name="outer",
    )(picks, *operands, *(() if add is None else (add,)), *after)


def merge_kernel(*refs, sums, held):
    out = refs[-1]
    batch, height, wide = refs[0].shape
    for z in range(batch):
        for h in range(sums):
            total = refs[2 * h][z].astype(jnp.float32) + refs[2 * h + 1][z].astype(jnp.float32)
            out[z, h, 0:height] = total.astype(jnp.bfloat16)
    if held:
        held_ref = refs[2 * sums]
        groups, _, rows, _ = held_ref.shape
        each = rows // batch
        blocks = 3 * groups * LANES // wide // sums
        for z in range(batch):
            for part in range(3):
                for g in range(groups):
                    low = (part * groups + g) * LANES
                    h, j = divmod(low // wide, blocks)
                    at = height + j * each
                    out[z, h, at : at + each, low % wide : low % wide + LANES] = held_ref[
                        g, part, z * each : (z + 1) * each
                    ]


def merge(pairs, held, rows, after):
    batch, height, wide = pairs[0][0].shape
    vmem = pl.BlockSpec(memory_space=pltpu.VMEM)
    sums = len(pairs)
    operands = [one for pair in pairs for one in pair]
    specs = [pl.BlockSpec((batch, height, wide), lambda i: (0, 0, 0))] * (2 * sums)
    if held is not None:
        groups, _, total_rows, _ = held.shape
        more = total_rows - rows
        if rows % more:
            held = held[:, :, rows:]
            rows = 0
        at = rows // more
        operands.append(held)
        specs.append(pl.BlockSpec((groups, 3, more, LANES), lambda i: (0, 0, at, 0)))
        height += 3 * groups * LANES // wide // sums * (more // batch)
    shape = (batch, sums, height, wide)
    return pl.pallas_call(
        functools.partial(merge_kernel, sums=sums, held=held is not None),
        grid=(1,),
        out_shape=jax.ShapeDtypeStruct(shape, jnp.bfloat16),
        in_specs=specs + [pl.BlockSpec(memory_space=pl.ANY)] * len(after),
        out_specs=pl.BlockSpec(shape, lambda i: (0, 0, 0, 0)),
        cost_estimate=SMALL,
        compiler_params=pltpu.CompilerParams(vmem_limit_bytes=VMEM),
        name="merge",
    )(*operands, *after)


def finish_kernel(came_ref, *rest, sizes, counts):
    outs = rest[len(rest) - len(sizes) :]
    batch, halves, _, wide = came_ref.shape
    for h in range(halves):
        at = 0
        for out, each, blocks in zip(outs, sizes, counts):
            for j in range(blocks):
                total = came_ref[0, h, at : at + each].astype(jnp.float32)
                for z in range(1, batch):
                    total = total + came_ref[z, h, at : at + each].astype(jnp.float32)
                low = (h * blocks + j) * wide
                out[:, low : low + wide] = total
                at += each


def finish(came, sizes, counts, after):
    vmem = pl.BlockSpec(memory_space=pltpu.VMEM)
    _, halves, _, wide = came.shape
    return pl.pallas_call(
        functools.partial(finish_kernel, sizes=sizes, counts=counts),
        out_shape=[
            jax.ShapeDtypeStruct((each, halves * count * wide), jnp.float32)
            for each, count in zip(sizes, counts)
        ],
        in_specs=[vmem] + [pl.BlockSpec(memory_space=pl.ANY)] * len(after),
        out_specs=[vmem] * len(sizes),
        cost_estimate=SMALL,
        name="finish",
    )(came, *after)


def tie_kernel(*refs):
    pass


def tie(value, after):
    anywhere = pl.BlockSpec(memory_space=pl.ANY)
    return pl.pallas_call(
        tie_kernel,
        out_shape=jax.ShapeDtypeStruct(value.shape, value.dtype),
        in_specs=[anywhere] * (1 + len(after)),
        out_specs=anywhere,
        input_output_aliases={0: 0},
        name="tie",
    )(value, *after)


def times(first_op, second_op):
    return lax.dot_general(first_op, second_op, NN, preferred_element_type=jnp.float32)


def swap(value, bit):
    size = lax.axis_size("seq")
    return lax.ppermute(value, "seq", [(i, i ^ bit) for i in range(size)])


def ahead(value, step):
    size = lax.axis_size("batch")
    return lax.ppermute(value, "batch", [(i, (i + step) % size) for i in range(size)])


class Sum:
    wide = 512

    def __init__(self, weights, half, bits):
        self.weights, self.half, self.bits = weights, half, bits
        self.seq = lax.axis_size("seq")
        self.batch = lax.axis_size("batch")
        self.next = 1

    def picks(self, sent):
        me = lax.axis_index("seq")
        first = me ^ self.bits[0] if sent else me
        found = [0]
        for bit in self.bits[:0:-1]:
            found = found + [f | bit for f in found]
        return (jnp.array(found, jnp.int32) ^ first).astype(jnp.int32)

    def send(self, after=()):
        sent = outer(self.weights, self.picks(True), self.half, self.batch, self.wide, None, after)
        self.came = swap(sent, self.bits[0])
        return [sent]

    def keep(self, after=()):
        self.total = list(
            outer(self.weights, self.picks(False), self.half, self.batch, self.wide, self.came, after)
        )

    def pass_on(self):
        count = len(self.total) // 2
        sent = self.total[count:]
        self.total = self.total[:count]
        self.came = [swap(one, self.bits[self.next]) for one in sent]
        self.next += 1
        return sent

    def take(self):
        self.total = [
            (a.astype(jnp.float32) + b.astype(jnp.float32)).astype(jnp.bfloat16)
            for a, b in zip(self.total, self.came)
        ]


class Sums:
    def __init__(self, weights, orders):
        self.weights = weights
        self.halves = [Sum(weights, half, bits) for half, bits in enumerate(orders)]

    def send(self, after=()):
        return sum([one.send(after) for one in self.halves], [])

    def came(self):
        return jax.tree.leaves([one.came for one in self.halves])

    def keep(self, after=(), after_last=()):
        for one in self.halves:
            one.keep(tuple(after) + (tuple(after_last) if one is self.halves[-1] else ()))
        return sum([one.pass_on() for one in self.halves], [])

    def spread(self, after=(), held=None, rows=0):
        for one in self.halves:
            while one.next < len(one.bits):
                one.take()
                one.pass_on()
        pieces = merge(
            [(one.total[0], one.came[0]) for one in self.halves], held, rows, tuple(after)
        )
        self.spread_out = lax.all_to_all(pieces, "batch", 0, 0, tiled=True)
        self.held = held
        self.rows = rows
        return [pieces]

    def result(self, after=()):
        devices = lax.axis_size("seq") * lax.axis_size("batch")
        sizes = [first.shape[0] // devices for first, _, _, _ in self.weights]
        counts = [second.shape[1] // 2 // Sum.wide for _, _, second, _ in self.weights]
        if self.held is not None:
            groups, _, height, _ = self.held.shape
            sizes.append((height - self.rows) // lax.axis_size("batch"))
            counts.append(3 * groups * LANES // 2 // Sum.wide)
        return finish(self.spread_out, sizes, counts, tuple(after))


def turn_tables(position):
    half = HD // 2
    lane = jnp.arange(LANES, dtype=jnp.int32)
    rates = jnp.exp((lane % half).astype(jnp.float32) * (-math.log(10000.0) / half))
    angles = position.astype(jnp.float32)[:, None] * rates[None, :]
    side = jnp.where((lane % HD) < half, -1.0, 1.0).astype(jnp.float32)
    return jnp.cos(angles), jnp.sin(angles) * side[None, :]


def all_pieces(value):
    batch = lax.axis_size("batch")
    place = lax.axis_index("batch")
    out = jnp.zeros((batch,) + value.shape, value.dtype)
    out = lax.dynamic_update_index_in_dim(out, value, place, 0)
    for step in range(1, batch):
        out = lax.dynamic_update_index_in_dim(
            out, ahead(value, step), (place - step) % batch, 0
        )
    return out


def seq_pieces(value, bits):
    have = []
    for bit in bits:
        came = swap(value, bit)
        value = jnp.stack([value, came], axis=sum(b > bit for b in have))
        have.append(bit)
    return value.reshape((lax.axis_size("seq"),) + value.shape[len(have) :])


def seq_total(value):
    bit = 1
    while bit < lax.axis_size("seq"):
        value = value + swap(value, bit)
        bit *= 2
    return value


def shards(
    frames_in,
    skip_in,
    time_table,
    timestep,
    lengths,
    span_start,
    span_len,
    skip_proj,
    mod_proj,
    mod_bias,
    qkv_proj,
    out_proj,
    up_proj,
    up_bias,
    down_proj,
    cotangent,
):
    seq = lax.axis_size("seq")
    batch = lax.axis_size("batch")
    seq_at = lax.axis_index("seq")
    batch_at = lax.axis_index("batch")
    device = seq_at * batch + batch_at
    devices = seq * batch
    inputs = frames_in[0]
    skip_rows = skip_in[0]
    rows, width = inputs.shape
    hidden = up_proj.shape[1]
    frames = rows * seq
    heads = HEADS // seq
    utts = lengths.shape[1]

    high = [seq >> (i + 1) for i in range(seq.bit_length() - 2)]
    low = high[::-1]
    rel = (jnp.arange(seq, dtype=jnp.int32) ^ seq_at).astype(jnp.int32)
    half = width // 2
    skip_each, qkv_each, out_each, up_each, down_each = (
        skip_proj.shape[0],
        qkv_proj.shape[0],
        out_proj.shape[0],
        up_proj.shape[0],
        down_proj.shape[0],
    )
    per_device = width // seq
    groups = width // LANES
    full_skip = lax.all_gather(skip_proj, BOTH, axis=0, tiled=False)
    own_qkv = all_pieces(qkv_proj).reshape(batch, qkv_each, 3, seq, per_device)
    own_qkv = lax.all_to_all(own_qkv.transpose(3, 2, 0, 1, 4), "seq", 0, 0, tiled=True)
    own_qkv = jnp.pad(own_qkv, ((0, 0),) * 4 + ((0, LANES - per_device),))
    own_qkv = own_qkv.transpose(0, 2, 3, 1, 4).reshape(width, 3 * LANES)
    late = jnp.concatenate(
        [down_proj, out_proj]
        + [up_proj[:, p * width : (p + 1) * width] for p in range(hidden // width)],
        axis=0,
    )
    late = lax.all_gather(late, BOTH, axis=0, tiled=False)
    full_qkv = jnp.concatenate([qkv_proj[:, p * width : (p + 1) * width] for p in range(3)], axis=0)
    full_qkv = lax.all_gather(full_qkv, BOTH, axis=0, tiled=False)

    utt_lengths = lengths[0]
    ends = jnp.cumsum(utt_lengths).astype(jnp.int32)
    starts = ends - utt_lengths
    frame_ids = seq_at * rows + jnp.arange(rows, dtype=jnp.int32)
    group_ids = jnp.arange(frames, dtype=jnp.int32)

    def members(ids):
        return (ids[:, None] >= starts[None, :]) & (ids[:, None] < ends[None, :])

    member = members(frame_ids)
    member_int = member.astype(jnp.int32)
    position = frame_ids - jnp.sum(member_int * starts[None, :], axis=1)
    span_first = jnp.sum(member_int * span_start[0][None, :], axis=1)
    span_after = span_first + jnp.sum(member_int * span_len[0][None, :], axis=1)
    in_span = ((position >= span_first) & (position < span_after)).astype(jnp.float32)
    member_rows = member.astype(jnp.float32)
    group_position = group_ids - jnp.sum(members(group_ids).astype(jnp.int32) * starts[None, :], axis=1)
    group_cos, group_sin = turn_tables(group_position)

    steps = all_pieces(timestep[0]).reshape(-1)
    step_pick = (
        steps[:, None] == jnp.arange(time_table.shape[0], dtype=jnp.int32)[None, :]
    ).astype(jnp.float32)
    time_rows = jnp.dot(step_pick, time_table.astype(jnp.float32), precision=highest)
    silu_value, silu_pull = jax.vjp(jax.nn.silu, time_rows)
    time_vec = silu_value.astype(jnp.bfloat16)
    terms = times(time_vec, mod_proj)
    def placed(bias):
        return lax.dynamic_update_slice(
            jnp.zeros((4 * width,), jnp.float32), bias.astype(jnp.float32), (device * bias.shape[0],)
        )

    terms = (terms + placed(mod_bias)[None, :]).reshape(batch, utts, 4 * width)
    up_terms = jnp.broadcast_to(placed(up_bias), (batch, 1, 4 * width))
    terms = jnp.concatenate([terms, up_terms], axis=1)
    modulation = lax.dynamic_index_in_dim(terms, batch_at, 0, keepdims=False)
    for step in range(1, batch):
        modulation = modulation + ahead(
            lax.dynamic_index_in_dim(terms, (batch_at + step) % batch, 0, keepdims=False), step
        )
    modulation = seq_total(modulation)
    full_bup = modulation[utts:]
    modulation = modulation[:utts]
    info = jnp.pad(member_rows, ((0, 0), (0, LANES - utts)))
    branch = (cotangent[0].astype(jnp.float32) * in_span[:, None]).astype(jnp.bfloat16)
    joined = jnp.concatenate([inputs.T, skip_rows.T], axis=0)
    branch_pair = (branch, swap(branch, 1))
    joined_pair = (joined, swap(joined, 1))

    stream_in, *normed_one = front(
        inputs, skip_rows, info, modulation, full_skip, utts,
        (group_cos, group_sin, own_qkv, branch_pair[1], joined_pair[1]),
    )
    normed_halves = [seq_pieces(normed_one[0], low + [1]), seq_pieces(normed_one[1], high + [1])]
    held = project(rel, normed_halves, own_qkv, group_cos, group_sin, ())
    head_out, log_sums = attend(held, ends, heads, 1024, 512)
    att = lax.all_to_all(
        head_out.reshape(seq, rows, LANES)[:, :, :per_device], "seq", 0, 0, tiled=True
    )
    if per_device < LANES:
        att = att.reshape(groups, 2, rows, per_device).transpose(0, 2, 1, 3).reshape(groups, rows, LANES)

    result, attended, normed_two, activated, grad_pre, grad_mid, grad_low, back, mod_two, bup_terms = middle(
        att, stream_in, info, modulation, branch, late, down_each, out_each, up_each, full_bup, utts
    )
    if per_device < LANES:
        back = back.reshape(groups, rows, 2, per_device).transpose(0, 2, 1, 3).reshape(seq, rows, per_device)
        back = jnp.pad(back, ((0, 0), (0, 0), (0, LANES - per_device)))
    back = lax.all_to_all(back, "seq", 0, 0, tiled=True).reshape(frames, LANES)

    def pairs(first, second):
        return (first[0], first[1], second[0], second[1])

    def pair(value):
        return (value, swap(value, 1))

    first_weights = [
        pairs(pair(activated), branch_pair),
        pairs(pair(normed_two), pair(grad_pre)),
        pairs(pair(attended), pair(grad_low)),
    ]
    sums = Sums(first_weights, (low, high))
    waits = sums.send()

    grad_held = attend_back(
        held, back, head_out, log_sums, group_cos, group_sin, ends, heads, waits, 1024, 512
    )
    grad_held = outgoing(rel, grad_held, normed_halves, tuple(sums.came()))
    mark = (grad_held,)
    grad_held = lax.all_to_all(grad_held[..., :per_device], "seq", 0, 0, tiled=True)
    if per_device < LANES:
        grad_held = grad_held.reshape(groups, 2, 3, -1, per_device).transpose(0, 2, 3, 1, 4)
        grad_held = grad_held.reshape(groups, 3, -1, LANES)
    sums.keep(mark)
    waits = sums.spread((), grad_held, rows)

    grad_stream, row_sums = tail(
        grad_held, stream_in, info, modulation, grad_mid, full_qkv, 0, qkv_each,
        mod_two, bup_terms, utts, waits,
    )
    last_sums = Sums([pairs(joined_pair, pair(grad_stream))], (low, high))
    row_sums = row_sums + swap(row_sums, 1)
    waits = last_sums.send((row_sums,))
    row_sums = tie(row_sums, waits)
    row_sums = row_sums + swap(row_sums, 2)
    grad_inputs, grad_skip_rows = unjoin(grad_stream, full_skip, skip_each, waits)
    waits = last_sums.keep((grad_inputs,), (row_sums,))
    row_sums = tie(row_sums, waits)
    for bit in low[1:]:
        row_sums = row_sums + swap(row_sums, bit)
    waits = last_sums.spread((row_sums, sums.spread_out))
    row_sums = all_pieces(tie(row_sums, waits))
    grad_down, grad_up, grad_out_w, grad_qkv_w = sums.result(waits)
    (grad_skip_w,) = last_sums.result()

    grad_modulation = row_sums[:, :utts].reshape(batch * utts, 4 * width)
    grad_bup = lax.dynamic_slice_in_dim(
        jnp.sum(row_sums[:, utts], axis=0), device * up_bias.shape[0], up_bias.shape[0]
    )
    grad_bmod = lax.dynamic_slice_in_dim(
        jnp.sum(grad_modulation, axis=0), device * mod_bias.shape[0], mod_bias.shape[0]
    )
    grad_mod_w = jnp.dot(time_vec.astype(jnp.float32).T, grad_modulation, precision=highest)
    grad_time_vec = jnp.dot(grad_modulation, mod_proj.astype(jnp.float32).T, precision=highest)
    grad_table = jnp.dot(step_pick.T, silu_pull(grad_time_vec)[0], precision=highest)
    return (
        result[None],
        grad_inputs[None],
        grad_skip_rows[None],
        grad_table,
        grad_skip_w,
        grad_mod_w,
        grad_bmod,
        grad_qkv_w,
        grad_out_w,
        grad_up,
        grad_bup,
        grad_down,
    )


def solution(mesh):
    return jax.shard_map(
        shards,
        mesh=mesh,
        in_specs=(
            P("batch", "seq", None),
            P("batch", "seq", None),
            P(None, BOTH),
            P("batch", None),
            P("batch", None),
            P("batch", None),
            P("batch", None),
            P(BOTH, None),
            P(BOTH, None),
            P(BOTH),
            P(BOTH, None),
            P(BOTH, None),
            P(BOTH, None),
            P(BOTH),
            P(BOTH, None),
            P("batch", "seq", None),
        ),
        out_specs=(
            P("batch", "seq", None),
            P("batch", "seq", None),
            P("batch", "seq", None),
            P(None, BOTH),
            P(BOTH, None),
            P(BOTH, None),
            P(BOTH),
            P(BOTH, None),
            P(BOTH, None),
            P(BOTH, None),
            P(BOTH),
            P(BOTH, None),
        ),
        check_vma=False,
    )
```

```python
import functools
import math

import jax
import jax.numpy as jnp
from jax import lax
from jax.experimental import pallas as pl
from jax.experimental.pallas import tpu as pltpu
from jax.sharding import PartitionSpec as P

HEADS = 16
HD = 64
LANES = 128
MASKED = -(2.0 ** 100)
NORM_EPS = 1e-06
SMALL = pl.CostEstimate(flops=1024, bytes_accessed=1024, transcendentals=0)
VMEM = 60 * 1024 * 1024
BOTH = ("seq", "batch")
NT = (((1,), (1,)), ((), ()))
NN = (((1,), (0,)), ((), ()))
TN = (((0,), (0,)), ((), ()))
highest = lax.Precision.HIGHEST


def mm(a, b, dims):
    return lax.dot_general(a, b, dims, preferred_element_type=jnp.float32)


def utt_of(ends_ref, rows, utts):
    found = jnp.zeros_like(rows)
    for u in range(utts - 1):
        found = found + (rows >= ends_ref[u]).astype(jnp.int32)
    return found


def key_range(ends_ref, first, last, utts, frames):
    low = 0
    high = frames
    for u in range(utts - 1):
        low = jnp.where(first >= ends_ref[u], ends_ref[u], low)
    for u in reversed(range(utts - 1)):
        high = jnp.where(last < ends_ref[u], ends_ref[u], high)
    return low, high


def split3(x):
    a = x.astype(jnp.bfloat16).astype(jnp.float32)
    b = (x - a).astype(jnp.bfloat16).astype(jnp.float32)
    return a, b, x - a - b


def fwd_kernel(ends_ref, qkv_ref, out_ref, lse_ref, q_s, k_s, v_s, m_s, acc_s, *, heads, utts, bq, bk):
    sources, _, rows, _ = qkv_ref.shape
    frames = sources * rows

    def build(src, carry):
        at = pl.multiple_of(src * rows, rows)
        lane = lax.broadcasted_iota(jnp.int32, (rows, LANES), 1)
        row = lax.broadcasted_iota(jnp.int32, (rows, LANES), 0) + at
        utt = utt_of(ends_ref, row, utts)
        for h in range(heads):
            spare = (1 - h) * HD
            mine = (lane >= HD) if h else (lane < HD)
            slot = lane - spare
            is_slot = (slot >= 0) & (slot < utts)
            qf = jnp.where(is_slot & (slot != utt), MASKED, 0.0)
            kf = jnp.where(slot == utt, 1.0, 0.0)
            vf = jnp.where(slot == 0, 1.0, 0.0)
            for part, feat, dst in ((0, qf, q_s), (1, kf, k_s)):
                x = qkv_ref[src, part].astype(jnp.float32)
                dst[h, pl.ds(at, rows), :] = jnp.where(mine, x, feat).astype(jnp.bfloat16)
            x = jnp.where(mine, qkv_ref[src, 2].astype(jnp.float32), vf)
            v_s[h, :, pl.ds(at, rows)] = x.T.astype(jnp.bfloat16)
        return carry

    lax.fori_loop(0, sources, build, 0)

    def q_block(i, carry):
        at = pl.multiple_of(i * bq, bq)
        low, high = key_range(ends_ref, at, at + bq - 1, utts, frames)
        m_s[...] = jnp.full(m_s.shape, -3.0e38, jnp.float32)
        acc_s[...] = jnp.zeros(acc_s.shape, jnp.float32)

        def k_block(j, inner):
            kat = pl.multiple_of(j * bk, bk)
            for h in range(heads):
                s = mm(k_s[h, pl.ds(kat, bk), :], q_s[h, pl.ds(at, bq), :], NT)
                old = m_s[h]
                top = jnp.maximum(old, jnp.max(s, axis=0, keepdims=True))
                alpha = jnp.exp(old - top)
                p = jnp.exp(s - top).astype(jnp.bfloat16)
                acc_s[h] = acc_s[h] * alpha + mm(v_s[h, :, pl.ds(kat, bk)], p, NN)
                m_s[h] = top
            return inner

        lax.fori_loop(low // bk, (high + bk - 1) // bk, k_block, 0)
        lane = lax.broadcasted_iota(jnp.int32, (LANES, bq), 0)
        out = None
        lse = None
        for h in range(heads):
            spare = (1 - h) * HD
            acc = acc_s[h]
            total = acc[spare : spare + 1, :]
            o = acc / total
            l = jnp.broadcast_to(m_s[h] + jnp.log(total), (LANES, bq))
            out = o if out is None else jnp.where(lane < HD, out, o)
            lse = l if lse is None else jnp.where(lane < HD, lse, l)
        out_ref[pl.ds(at, bq), :] = out.T.astype(jnp.bfloat16)
        lse_ref[pl.ds(at, bq), :] = lse.T
        return carry

    lax.fori_loop(0, frames // bq, q_block, 0)


def attend(qkv, ends, heads, bq, bk):
    sources, _, rows, _ = qkv.shape
    frames = sources * rows
    utts = ends.shape[0]
    return pl.pallas_call(
        functools.partial(fwd_kernel, heads=heads, utts=utts, bq=bq, bk=bk),
        out_shape=(
            jax.ShapeDtypeStruct((frames, LANES), jnp.bfloat16),
            jax.ShapeDtypeStruct((frames, LANES), jnp.float32),
        ),
        in_specs=[pl.BlockSpec(memory_space=pltpu.SMEM), pl.BlockSpec(memory_space=pltpu.VMEM)],
        out_specs=(pl.BlockSpec(memory_space=pltpu.VMEM), pl.BlockSpec(memory_space=pltpu.VMEM)),
        scratch_shapes=[pltpu.VMEM((heads, frames, LANES), jnp.bfloat16)] * 2
        + [
            pltpu.VMEM((heads, LANES, frames), jnp.bfloat16),
            pltpu.VMEM((heads, 1, bq), jnp.float32),
            pltpu.VMEM((heads, LANES, bq), jnp.float32),
        ],
        compiler_params=pltpu.CompilerParams(vmem_limit_bytes=VMEM),
        cost_estimate=pl.CostEstimate(
            flops=40 * heads * frames * frames * HD, bytes_accessed=frames * LANES * 12,
            transcendentals=heads * frames * frames,
        ),
        name="attend",
    )(ends, qkv)


def bwd_kernel(
    ends_ref, qkv_ref, da_ref, out_ref, lse_ref, cos_ref, sin_ref, *rest, heads, utts, bq, bk
):
    grad_ref, q_s, k_s, kt_s, v_s, d_s, gq_s, gk_s, gv_s = rest[-9:]
    sources, _, rows, _ = qkv_ref.shape
    frames = sources * rows

    def build(src, carry):
        at = pl.multiple_of(src * rows, rows)
        lane = lax.broadcasted_iota(jnp.int32, (rows, LANES), 1)
        row = lax.broadcasted_iota(jnp.int32, (rows, LANES), 0) + at
        utt = utt_of(ends_ref, row, utts)
        da = da_ref[pl.ds(at, rows), :].astype(jnp.float32)
        prod = da * out_ref[pl.ds(at, rows), :].astype(jnp.float32)
        lse = lse_ref[pl.ds(at, rows), :]
        for h in range(heads):
            spare = (1 - h) * HD
            mine = (lane >= HD) if h else (lane < HD)
            slot = lane - spare
            is_slot = (slot >= 0) & (slot < utts)
            delta = jnp.sum(jnp.where(mine, prod, 0.0), axis=1, keepdims=True)
            l3 = split3(-lse[:, h * HD : h * HD + 1])
            d3 = split3(-delta)
            qf = jnp.where(is_slot & (slot != utt), MASKED, 0.0)
            df = jnp.zeros_like(qf)
            for n in range(3):
                qf = jnp.where(slot == utts + n, l3[n], qf)
                df = jnp.where(slot == n, d3[n], df)
            kf = jnp.where((slot == utt) | ((slot >= utts) & (slot < utts + 3)), 1.0, 0.0)
            vf = jnp.where((slot >= 0) & (slot < 3), 1.0, 0.0)
            for x, feat, dst in (
                (qkv_ref[src, 0], qf, q_s), (qkv_ref[src, 1], kf, k_s), (qkv_ref[src, 2], vf, v_s),
            ):
                dst[h, pl.ds(at, rows), :] = jnp.where(mine, x.astype(jnp.float32), feat).astype(jnp.bfloat16)
            d_s[h, pl.ds(at, rows), :] = jnp.where(mine, da, df).astype(jnp.bfloat16)
            kt_s[h, :, pl.ds(at, rows)] = qkv_ref[src, 1].T
        gq_s[:, :, pl.ds(at, rows)] = jnp.zeros((heads, LANES, rows), jnp.float32)
        return carry

    lax.fori_loop(0, sources, build, 0)

    def k_block(j, carry):
        kat = pl.multiple_of(j * bk, bk)
        low, high = key_range(ends_ref, kat, kat + bk - 1, utts, frames)
        gk_s[:, pl.ds(kat, bk), :] = jnp.zeros((heads, bk, LANES), jnp.float32)
        gv_s[:, pl.ds(kat, bk), :] = jnp.zeros((heads, bk, LANES), jnp.float32)

        def q_block(i, inner):
            at = pl.multiple_of(i * bq, bq)
            for h in range(heads):
                q = q_s[h, pl.ds(at, bq), :]
                d = d_s[h, pl.ds(at, bq), :]
                k = k_s[h, pl.ds(kat, bk), :]
                p = jnp.exp(mm(k, q, NT))
                ds = (p * mm(v_s[h, pl.ds(kat, bk), :], d, NT)).astype(jnp.bfloat16)
                gv_s[h, pl.ds(kat, bk), :] += mm(p.astype(jnp.bfloat16), d, NN)
                gk_s[h, pl.ds(kat, bk), :] += mm(ds, q, NN)
                gq_s[h, :, pl.ds(at, bq)] += mm(kt_s[h, :, pl.ds(kat, bk)], ds, NN)
            return inner

        lax.fori_loop(low // bq, (high + bq - 1) // bq, q_block, 0)
        return carry

    lax.fori_loop(0, frames // bk, k_block, 0)

    def finish(src, carry):
        at = pl.multiple_of(src * rows, rows)
        lane = lax.broadcasted_iota(jnp.int32, (rows, LANES), 1)
        first = (lane % HD) < HD // 2
        cos = cos_ref[pl.ds(at, rows), :]
        sin = sin_ref[pl.ds(at, rows), :]

        def both(ref):
            x = ref[0, pl.ds(at, rows), :]
            return jnp.where(lane < HD, x, ref[1, pl.ds(at, rows), :]) if heads == 2 else x

        def both_flipped(ref):
            x = ref[0, :, pl.ds(at, rows)]
            if heads == 2:
                row = lax.broadcasted_iota(jnp.int32, (LANES, rows), 0)
                x = jnp.where(row < HD, x, ref[1, :, pl.ds(at, rows)])
            return x.T

        def unturn(x):
            partner = jnp.where(first, pltpu.roll(x, LANES - HD // 2, 1), pltpu.roll(x, HD // 2, 1))
            return x * cos - partner * sin

        grad_ref[src, 0] = (unturn(both_flipped(gq_s)) * HD ** -0.5).astype(jnp.bfloat16)
        grad_ref[src, 1] = unturn(both(gk_s)).astype(jnp.bfloat16)
        grad_ref[src, 2] = both(gv_s).astype(jnp.bfloat16)
        return carry

    lax.fori_loop(0, sources, finish, 0)


def attend_back(qkv, grad_out, out, lse, cos, sin, ends, heads, after, bq, bk):
    sources, _, rows, _ = qkv.shape
    frames = sources * rows
    utts = ends.shape[0]
    vmem = pl.BlockSpec(memory_space=pltpu.VMEM)
    return pl.pallas_call(
        functools.partial(bwd_kernel, heads=heads, utts=utts, bq=bq, bk=bk),
        out_shape=jax.ShapeDtypeStruct(qkv.shape, jnp.bfloat16),
        in_specs=[pl.BlockSpec(memory_space=pltpu.SMEM)]
        + [vmem] * 6
        + [pl.BlockSpec(memory_space=pl.ANY)] * len(after),
        out_specs=vmem,
        scratch_shapes=[pltpu.VMEM((heads, frames, LANES), jnp.bfloat16)] * 2
        + [pltpu.VMEM((heads, LANES, frames), jnp.bfloat16)]
        + [pltpu.VMEM((heads, frames, LANES), jnp.bfloat16)] * 2
        + [pltpu.VMEM((heads, LANES, frames), jnp.float32)]
        + [pltpu.VMEM((heads, frames, LANES), jnp.float32)] * 2,
        compiler_params=pltpu.CompilerParams(vmem_limit_bytes=VMEM),
        cost_estimate=pl.CostEstimate(
            flops=64 * heads * frames * frames * HD, bytes_accessed=frames * LANES * 24,
            transcendentals=heads * frames * frames,
        ),
        name="attend_back",
    )(ends, qkv, grad_out, out, lse, cos, sin, *after)


def outgoing_kernel(rel_ref, grad_ref, low_ref, high_ref, *rest):
    out_ref, total_s = rest[-2:]
    src = pl.program_id(0)
    rows = grad_ref.shape[2]
    grads = jnp.concatenate([grad_ref[0, part] for part in range(3)], axis=1)
    normed = jnp.concatenate([low_ref[0], high_ref[0]], axis=1)
    term = mm(normed, grads, TN)
    for part in range(3):
        out_ref[src, part, 0:rows] = grad_ref[0, part]

    @pl.when(src == 0)
    def _():
        total_s[...] = term

    @pl.when(src > 0)
    def _():
        total_s[...] += term

    @pl.when(src == pl.num_programs(0) - 1)
    def _():
        total = total_s[...].astype(jnp.bfloat16)
        each = out_ref.shape[2] - rows
        for dest in range(out_ref.shape[0]):
            for part in range(3):
                out_ref[dest, part, rows:] = total[
                    dest * each : (dest + 1) * each, part * LANES : (part + 1) * LANES
                ]


def outgoing(rel, grads, halves, after):
    sources, _, rows, _ = grads.shape
    half = halves[0].shape[2]
    each = 2 * half // sources
    shape = (sources, 3, rows + each, LANES)
    side = pl.BlockSpec((1, rows, half), lambda i, rel: (rel[i], 0, 0))
    return pl.pallas_call(
        outgoing_kernel,
        grid_spec=pltpu.PrefetchScalarGridSpec(
            num_scalar_prefetch=1,
            grid=(sources,),
            in_specs=[pl.BlockSpec((1, 3, rows, LANES), lambda i, rel: (i, 0, 0, 0)), side, side]
            + [pl.BlockSpec(memory_space=pl.ANY)] * len(after),
            out_specs=pl.BlockSpec(shape, lambda i, rel: (0, 0, 0, 0)),
            scratch_shapes=[pltpu.VMEM((2 * half, 3 * LANES), jnp.float32)],
        ),
        out_shape=jax.ShapeDtypeStruct(shape, jnp.bfloat16),
        cost_estimate=pl.CostEstimate(
            flops=12 * rows * sources * half * LANES, bytes_accessed=16 * half * half, transcendentals=0
        ),
        compiler_params=pltpu.CompilerParams(vmem_limit_bytes=VMEM),
        name="outgoing",
    )(rel, grads, *halves, *after)


def unjoin_kernel(grad_ref, weight_ref, *rest):
    width = grad_ref.shape[1]
    i = pl.program_id(0)
    made = mm(grad_ref[...], weight_ref[...].reshape(-1, width), NT).astype(jnp.bfloat16)

    @pl.when(i < 2)
    def _():
        rest[-2][...] = made

    @pl.when(i >= 2)
    def _():
        rest[-1][...] = made


def unjoin(grad, early, skip_each, after):
    rows, width = grad.shape
    devices = early.shape[0]
    half = width // 2
    return pl.pallas_call(
        unjoin_kernel,
        grid=(4,),
        out_shape=[jax.ShapeDtypeStruct((rows, width), jnp.bfloat16)] * 2,
        in_specs=[
            pl.BlockSpec((rows, width), lambda i: (0, 0)),
            pl.BlockSpec((devices // 4, skip_each, width), lambda i: (i, 0, 0)),
        ]
        + [pl.BlockSpec(memory_space=pl.ANY)] * len(after),
        out_specs=[
            pl.BlockSpec((rows, half), lambda i: (0, jnp.minimum(i, 1))),
            pl.BlockSpec((rows, half), lambda i: (0, jnp.maximum(i - 2, 0))),
        ],
        cost_estimate=pl.CostEstimate(
            flops=4 * rows * width * width, bytes_accessed=6 * width * width, transcendentals=0
        ),
        compiler_params=pltpu.CompilerParams(vmem_limit_bytes=VMEM),
        name="unjoin",
    )(grad, early, *after)


def normalise(hidden):
    centred = hidden - jnp.mean(hidden, axis=-1, keepdims=True)
    inverse = lax.rsqrt(jnp.mean(centred * centred, axis=-1, keepdims=True) + NORM_EPS)
    return centred * inverse, inverse


def normalise_back(grad, normed, inverse):
    return inverse * (
        grad
        - jnp.mean(grad, axis=-1, keepdims=True)
        - normed * jnp.mean(grad * normed, axis=-1, keepdims=True)
    )


def per_row(info, table, utts):
    total = info[:, 0:1] * table[0:1]
    for u in range(1, utts):
        total = total + info[:, u : u + 1] * table[u : u + 1]
    return total


def sums_by_utt(ref, at, info, value, utts):
    width = value.shape[1]
    for u in range(utts):
        ref[u : u + 1, at : at + width] = jnp.sum(info[:, u : u + 1] * value, axis=0, keepdims=True)


def gelu_parts(x):
    rate = math.sqrt(2.0 / math.pi)
    square = x * x
    inner = jnp.tanh(x * (rate + rate * 0.044715 * square))
    half = 0.5 + 0.5 * inner
    value = x * half
    slope = half + 0.5 * x * (1.0 - inner * inner) * (rate + 3 * rate * 0.044715 * square)
    return value, slope


def front_kernel(frames_ref, skip_ref, info_ref, mod_ref, weight_ref, *rest, utts, steps):
    stream_ref, normed_low_ref, normed_high_ref = rest[-3:]
    i = pl.program_id(0)
    width = stream_ref.shape[1]
    half = width // 2
    weight = weight_ref[...].reshape(-1, width)
    depth = weight.shape[0]

    for n in range(steps):
        @pl.when(i == n)
        def _(n=n):
            source = frames_ref if n * depth < width else skip_ref
            at = n * depth % width
            term = mm(source[:, at : at + depth], weight, NN)
            stream_ref[...] = term if n == 0 else stream_ref[...] + term

    @pl.when(i == steps - 1)
    def _():
        info = info_ref[...]
        unit, _unused = normalise(stream_ref[...])
        scale = per_row(info, 1.0 + mod_ref[:, :width], utts)
        shift = per_row(info, mod_ref[:, width : 2 * width], utts)
        normed = (unit * scale + shift).astype(jnp.bfloat16)
        normed_low_ref[...] = normed[:, :half]
        normed_high_ref[...] = normed[:, half:]


def front(frames, skip, info, modulation, weights, utts, after):
    rows, width = frames.shape
    devices, each, _ = weights.shape
    half = width // 2
    steps = 4

    def fixed(*shape):
        return pl.BlockSpec(shape, lambda i: (0,) * len(shape))

    return pl.pallas_call(
        functools.partial(front_kernel, utts=utts, steps=steps),
        grid=(steps,),
        in_specs=[
            fixed(rows, width),
            fixed(rows, width),
            fixed(rows, LANES),
            fixed(utts, 4 * width),
            pl.BlockSpec((devices // steps, each, width), lambda i: (i, 0, 0)),
        ]
        + [pl.BlockSpec(memory_space=pl.ANY)] * len(after),
        out_specs=(fixed(rows, width), fixed(rows, half), fixed(rows, half)),
        out_shape=(
            jax.ShapeDtypeStruct((rows, width), jnp.float32),
            jax.ShapeDtypeStruct((rows, half), jnp.bfloat16),
            jax.ShapeDtypeStruct((rows, half), jnp.bfloat16),
        ),
        compiler_params=pltpu.CompilerParams(vmem_limit_bytes=VMEM),
        cost_estimate=pl.CostEstimate(
            flops=4 * rows * width * width, bytes_accessed=8 * width * width, transcendentals=0
        ),
        name="front",
    )(frames, skip, info, modulation, weights, *after)


def project_kernel(rel_ref, low_ref, high_ref, weight_ref, cos_ref, sin_ref, *rest):
    out_ref = rest[-1]
    normed = jnp.concatenate([low_ref[0], high_ref[0]], axis=1)
    turned = mm(normed, weight_ref[...], NN)
    lane = lax.broadcasted_iota(jnp.int32, (turned.shape[0], LANES), 1)
    first = (lane % HD) < HD // 2
    for part in range(3):
        x = turned[:, part * LANES : (part + 1) * LANES]
        if part < 2:
            partner = jnp.where(first, pltpu.roll(x, LANES - HD // 2, 1), pltpu.roll(x, HD // 2, 1))
            x = x * cos_ref[...] + partner * sin_ref[...]
        if part == 0:
            x = x * HD ** -0.5
        out_ref[0, part] = x.astype(jnp.bfloat16)


def project(rel, halves, weight, cos, sin, after):
    sources, rows, half = halves[0].shape
    side = pl.BlockSpec((1, rows, half), lambda i, rel: (rel[i], 0, 0))
    table = pl.BlockSpec((rows, LANES), lambda i, rel: (i, 0))
    return pl.pallas_call(
        project_kernel,
        grid_spec=pltpu.PrefetchScalarGridSpec(
            num_scalar_prefetch=1,
            grid=(sources,),
            in_specs=[side, side, pl.BlockSpec(weight.shape, lambda i, rel: (0, 0)), table, table]
            + [pl.BlockSpec(memory_space=pl.ANY)] * len(after),
            out_specs=pl.BlockSpec((1, 3, rows, LANES), lambda i, rel: (i, 0, 0, 0)),
        ),
        out_shape=jax.ShapeDtypeStruct((sources, 3, rows, LANES), jnp.bfloat16),
        compiler_params=pltpu.CompilerParams(vmem_limit_bytes=VMEM),
        cost_estimate=pl.CostEstimate(
            flops=12 * rows * sources * half * LANES, bytes_accessed=16 * half * half, transcendentals=0
        ),
        name="project",
    )(rel, *halves, weight, cos, sin, *after)


def middle_kernel(att_ref, stream_ref, info_ref, mod_ref, branch_ref, wout_ref, wup_ref, wdown_ref, bias_ref,
                  result_ref, attended_ref, normed_ref, act_ref, pre_ref, grad_ref, grad_low_ref,
                  back_ref, sums_ref, bup_ref,
                  mid_s, unit_s, inv_s, total_s, gn_s, att_s, normed_s, *, utts, blocks):
    b = pl.program_id(0)
    rows, width = stream_ref.shape
    groups = att_ref.shape[0]

    @pl.when(b == 0)
    def _():
        for s in range(groups):
            att_s[:, s * LANES : (s + 1) * LANES] = att_ref[s]
            attended_ref[s * LANES : (s + 1) * LANES, :] = att_ref[s].T
        mid = stream_ref[...] + mm(att_s[...], wout_ref[...].reshape(width, width), NN)
        mid_s[...] = mid
        unit, inverse = normalise(mid)
        unit_s[...] = unit
        inv_s[...] = jnp.broadcast_to(inverse, inv_s.shape)
        info = info_ref[...]
        scale = per_row(info, 1.0 + mod_ref[:, 2 * width : 3 * width], utts)
        shift = per_row(info, mod_ref[:, 3 * width :], utts)
        normed = (unit * scale + shift).astype(jnp.bfloat16)
        normed_s[...] = normed
        normed_ref[...] = normed.T

    up = wup_ref[...].reshape(width, -1)
    down = wdown_ref[...].reshape(-1, width)
    value, slope = gelu_parts(mm(normed_s[...], up, NN) + bias_ref[...])
    act = value.astype(jnp.bfloat16)
    act_ref[...] = act.T
    term = mm(act, down, NN)
    pre = (mm(branch_ref[...], down, NT) * slope).astype(jnp.bfloat16)
    pre_ref[...] = pre
    bup_ref[...] = jnp.sum(pre.astype(jnp.float32), axis=0, keepdims=True)
    grad_term = mm(pre, up, NT)

    @pl.when(b == 0)
    def _():
        total_s[...] = mid_s[...] + term
        gn_s[...] = grad_term

    @pl.when(b > 0)
    def _():
        total_s[...] += term
        gn_s[...] += grad_term

    @pl.when(b == blocks - 1)
    def _():
        result_ref[...] = total_s[...].astype(jnp.bfloat16)
        info = info_ref[...]
        scale = per_row(info, 1.0 + mod_ref[:, 2 * width : 3 * width], utts)
        gn = gn_s[...]
        unit = unit_s[...]
        grad = branch_ref[...].astype(jnp.float32) + normalise_back(gn * scale, unit, inv_s[:, :1])
        grad_ref[...] = grad
        low = grad.astype(jnp.bfloat16)
        grad_low_ref[...] = low
        back = mm(low, wout_ref[...].reshape(width, width), NT).astype(jnp.bfloat16)
        for s in range(groups):
            back_ref[s] = back[:, s * LANES : (s + 1) * LANES]
        sums_by_utt(sums_ref, 0, info, gn * unit, utts)
        sums_by_utt(sums_ref, width, info, gn, utts)


def middle(att, stream, info, modulation, cot, late, down_each, out_each, up_each, bias, utts):
    rows, width = stream.shape
    devices = late.shape[0]
    hidden = down_each * devices
    block = 1024
    blocks = hidden // block
    halves = width // block
    groups = width // LANES
    out_at = down_each // out_each
    up_at = (down_each + out_each) // up_each

    def fixed(*shape):
        return pl.BlockSpec(shape, lambda b: (0,) * len(shape))

    def whole(*shape, dtype=jnp.bfloat16):
        return jax.ShapeDtypeStruct(shape, dtype)

    f32 = jnp.float32
    return pl.pallas_call(
        functools.partial(middle_kernel, utts=utts, blocks=blocks),
        grid=(blocks,),
        out_shape=(
            whole(rows, width),
            whole(width, rows),
            whole(width, rows),
            whole(hidden, rows),
            whole(rows, hidden),
            whole(rows, width, dtype=f32),
            whole(rows, width),
            whole(groups, rows, LANES),
            whole(utts, 2 * width, dtype=f32),
            whole(1, hidden, dtype=f32),
        ),
        in_specs=[
            fixed(groups, rows, LANES),
            fixed(rows, width),
            fixed(rows, LANES),
            fixed(utts, 4 * width),
            fixed(rows, width),
            pl.BlockSpec((devices, out_each, width), lambda b: (0, out_at, 0)),
            pl.BlockSpec((devices, up_each, block), lambda b: (0, up_at + b // halves, b % halves)),
            pl.BlockSpec((devices // blocks, down_each, width), lambda b: (b, 0, 0)),
            pl.BlockSpec((1, block), lambda b: (0, b)),
        ],
        out_specs=(
            fixed(rows, width),
            fixed(width, rows),
            fixed(width, rows),
            pl.BlockSpec((block, rows), lambda b: (b, 0)),
            pl.BlockSpec((rows, block), lambda b: (0, b)),
            fixed(rows, width),
            fixed(rows, width),
            fixed(groups, rows, LANES),
            fixed(utts, 2 * width),
            pl.BlockSpec((1, block), lambda b: (0, b)),
        ),
        scratch_shapes=[
            pltpu.VMEM((rows, width), f32),
            pltpu.VMEM((rows, width), f32),
            pltpu.VMEM((rows, LANES), f32),
            pltpu.VMEM((rows, width), f32),
            pltpu.VMEM((rows, width), f32),
            pltpu.VMEM((rows, width), jnp.bfloat16),
            pltpu.VMEM((rows, width), jnp.bfloat16),
        ],
        compiler_params=pltpu.CompilerParams(vmem_limit_bytes=VMEM),
        cost_estimate=pl.CostEstimate(
            flops=12 * rows * hidden * width, bytes_accessed=20 * width * width,
            transcendentals=rows * hidden,
        ),
        name="middle",
    )(att, stream, info, modulation, cot, late, late, late, bias)


def tail_kernel(held_ref, stream_ref, info_ref, mod_ref, mid_ref, w_ref, two_ref, bup_ref,
                *rest, utts):
    out_ref, sums_ref, proj_s, gn_s = rest[-4:]
    p = pl.program_id(0)
    rows, width = stream_ref.shape
    groups = held_ref.shape[0]
    for s in range(groups):
        proj_s[:, s * LANES : (s + 1) * LANES] = held_ref[s, 0]
    term = mm(proj_s[...], w_ref[...].reshape(width, width), NT)

    @pl.when(p == 0)
    def _():
        gn_s[...] = term

    @pl.when(p > 0)
    def _():
        gn_s[...] += term

    @pl.when(p == 2)
    def _():
        info = info_ref[...]
        unit, inverse = normalise(stream_ref[...])
        scale = per_row(info, 1.0 + mod_ref[:, :width], utts)
        gn = gn_s[...]
        out_ref[...] = (mid_ref[...] + normalise_back(gn * scale, unit, inverse)).astype(jnp.bfloat16)
        sums_ref[0:utts, 2 * width :] = two_ref[...]
        sums_ref[utts : utts + 1, :] = bup_ref[...]
        sums_by_utt(sums_ref, 0, info, gn * unit, utts)
        sums_by_utt(sums_ref, width, info, gn, utts)


def tail(held, stream, info, modulation, mid, early, qkv_each, two, bup, utts, after):
    rows, width = stream.shape
    devices = early.shape[0]
    groups = held.shape[0]

    def fixed(*shape):
        return pl.BlockSpec(shape, lambda p: (0,) * len(shape))

    return pl.pallas_call(
        functools.partial(tail_kernel, utts=utts),
        grid=(3,),
        out_shape=(
            jax.ShapeDtypeStruct((rows, width), jnp.bfloat16),
            jax.ShapeDtypeStruct((utts + 1, 4 * width), jnp.float32),
        ),
        in_specs=[
            pl.BlockSpec((groups, 1, rows, LANES), lambda p: (0, p, 0, 0)),
            fixed(rows, width),
            fixed(rows, LANES),
            fixed(utts, 4 * width),
            fixed(rows, width),
            pl.BlockSpec((devices, qkv_each, width), lambda p: (0, 0, p)),
            fixed(utts, 2 * width),
            fixed(1, 4 * width),
        ]
        + [pl.BlockSpec(memory_space=pl.ANY)] * len(after),
        out_specs=(
            fixed(rows, width),
            fixed(utts + 1, 4 * width),
        ),
        scratch_shapes=[
            pltpu.VMEM((rows, width), jnp.bfloat16),
            pltpu.VMEM((rows, width), jnp.float32),
        ],
        compiler_params=pltpu.CompilerParams(vmem_limit_bytes=VMEM),
        cost_estimate=pl.CostEstimate(
            flops=6 * rows * width * width, bytes_accessed=14 * width * width, transcendentals=0
        ),
        name="tail",
    )(held, stream, info, modulation, mid, early, two, bup, *after)


def outer_kernel(pick_ref, *refs, sizes, counts, batch, chosen, adds, extra):
    u = pl.program_id(0)
    out_refs = refs[len(refs) - chosen :] if adds else [refs[-1].at[n] for n in range(chosen)]
    came = refs[len(refs) - chosen - extra - 1] if adds else None
    at = 0
    start = 0
    row = 0
    for each, count in zip(sizes, counts):
        own = refs[at : at + chosen]
        other = refs[at + chosen : at + 2 * chosen]
        second, second_other = refs[at + 2 * chosen : at + 2 * chosen + 2]
        for j in range(count):
            @pl.when(u == start + j)
            def _(own=own, other=other, second=second, second_other=second_other, each=each, row=row):
                left = jnp.concatenate(
                    [
                        jnp.concatenate([one[...] for one in own], axis=0),
                        jnp.concatenate([one[...] for one in other], axis=0),
                    ],
                    axis=1,
                )
                right = jnp.concatenate([second[...], second_other[...]], axis=0)
                total = mm(left, right, NN)
                for n in range(chosen):
                    for z in range(batch):
                        low = (n * batch + z) * each
                        part = total[low : low + each]
                        if adds:
                            part = part + came[n, z, row : row + each, :].astype(jnp.float32)
                        out_refs[n][z, row : row + each, :] = part.astype(jnp.bfloat16)
            row += each
        start += count
        at += 2 * chosen + 2


def outer_plain(weights, picks, half, batch, wide, add):
    made = []
    for first, first_other, second, second_other in weights:
        block = first.shape[0] // lax.axis_size("seq")
        columns = second.shape[1] // 2
        total = 0.0
        for one, two in ((first, second), (first_other, second_other)):
            chosen = [
                lax.dynamic_slice_in_dim(one, picks[n] * block, block, axis=0)
                for n in range(picks.shape[0])
            ]
            total = total + mm(
                jnp.concatenate(chosen, axis=0), two[:, half * columns : (half + 1) * columns], NN
            )
        total = total.reshape(picks.shape[0], batch, block // batch, columns // wide, wide)
        total = total.transpose(0, 1, 3, 2, 4)
        made.append(total.reshape(picks.shape[0], batch, -1, wide))
    made = jnp.concatenate(made, axis=2)
    if add is None:
        return made.astype(jnp.bfloat16)
    return list((made + add.astype(jnp.float32)).astype(jnp.bfloat16))


def outer(weights, picks, half, batch, wide, add=None, after=()):
    chosen = picks.shape[0]
    seq = lax.axis_size("seq")
    blocks = [first.shape[0] // seq for first, _, _, _ in weights]
    sizes = [block // batch for block in blocks]
    counts = [second.shape[1] // 2 // wide for _, _, second, _ in weights]
    if any(block % LANES for block in blocks):
        return outer_plain(weights, picks, half, batch, wide, add)
    tokens = weights[0][0].shape[1]
    height = sum(e * c for e, c in zip(sizes, counts))
    shape = (batch, height, wide)
    specs = []
    operands = []
    start = 0
    flops = 0
    for (first, first_other, second, second_other), block, count in zip(weights, blocks, counts):
        def rows_at(n, block=block):
            return pl.BlockSpec((block, tokens), lambda u, pick: (pick[n], 0))

        def column_at(u, pick, start=start, count=count):
            return (0, half * count + jnp.clip(u - start, 0, count - 1))

        specs += [rows_at(n) for n in range(chosen)] * 2
        specs += [pl.BlockSpec((tokens, wide), column_at)] * 2
        operands += [first] * chosen + [first_other] * chosen + [second, second_other]
        start += count
        flops += 4 * tokens * chosen * block * count * wide
    whole = pl.BlockSpec(shape, lambda u, pick: (0, 0, 0))
    stacked = pl.BlockSpec((chosen,) + shape, lambda u, pick: (0, 0, 0, 0))
    made = jax.ShapeDtypeStruct((chosen,) + shape, jnp.bfloat16)
    return pl.pallas_call(
        functools.partial(
            outer_kernel, sizes=sizes, counts=counts, batch=batch, chosen=chosen,
            adds=add is not None, extra=len(after),
        ),
        grid_spec=pltpu.PrefetchScalarGridSpec(
            num_scalar_prefetch=1,
            grid=(sum(counts),),
            in_specs=specs
            + ([] if add is None else [stacked])
            + [pl.BlockSpec(memory_space=pl.ANY)] * len(after),
            out_specs=stacked if add is None else [whole] * chosen,
        ),
        out_shape=made if add is None else [jax.ShapeDtypeStruct(shape, jnp.bfloat16)] * chosen,
        compiler_params=pltpu.CompilerParams(vmem_limit_bytes=VMEM),
        cost_estimate=pl.CostEstimate(flops=2 * flops, bytes_accessed=flops // 300, transcendentals=0),
        name="outer",
    )(picks, *operands, *(() if add is None else (add,)), *after)


def merge_kernel(*refs, sums):
    out = refs[-1]
    for z in range(out.shape[0]):
        for h in range(sums):
            total = refs[2 * h][z].astype(jnp.float32) + refs[2 * h + 1][z].astype(jnp.float32)
            out[z, h] = total.astype(jnp.bfloat16)


def merge(pairs, after):
    batch, height, wide = pairs[0][0].shape
    sums = len(pairs)
    shape = (batch, sums, height, wide)
    return pl.pallas_call(
        functools.partial(merge_kernel, sums=sums),
        grid=(1,),
        out_shape=jax.ShapeDtypeStruct(shape, jnp.bfloat16),
        in_specs=[pl.BlockSpec((batch, height, wide), lambda i: (0, 0, 0))] * (2 * sums)
        + [pl.BlockSpec(memory_space=pl.ANY)] * len(after),
        out_specs=pl.BlockSpec(shape, lambda i: (0, 0, 0, 0)),
        cost_estimate=SMALL,
        compiler_params=pltpu.CompilerParams(vmem_limit_bytes=VMEM),
        name="merge",
    )(*[one for pair in pairs for one in pair], *after)


def cut(held, rows):
    groups, _, height, _ = held.shape
    batch = lax.axis_size("batch")
    each = (height - rows) // batch
    piece = held[:, :, rows:].reshape(groups, 3, batch, each, LANES)
    return piece.transpose(2, 3, 1, 0, 4).reshape(batch, each, 3 * groups * LANES)


def finish_kernel(came_ref, *rest, sizes, counts):
    outs = rest[len(rest) - len(sizes) :]
    batch, halves, _, wide = came_ref.shape
    for h in range(halves):
        at = 0
        for out, each, blocks in zip(outs, sizes, counts):
            for j in range(blocks):
                total = came_ref[0, h, at : at + each].astype(jnp.float32)
                for z in range(1, batch):
                    total = total + came_ref[z, h, at : at + each].astype(jnp.float32)
                low = (h * blocks + j) * wide
                out[:, low : low + wide] = total
                at += each


def finish(came, sizes, counts, after):
    vmem = pl.BlockSpec(memory_space=pltpu.VMEM)
    _, halves, _, wide = came.shape
    return pl.pallas_call(
        functools.partial(finish_kernel, sizes=sizes, counts=counts),
        out_shape=[
            jax.ShapeDtypeStruct((each, halves * count * wide), jnp.float32)
            for each, count in zip(sizes, counts)
        ],
        in_specs=[vmem] + [pl.BlockSpec(memory_space=pl.ANY)] * len(after),
        out_specs=[vmem] * len(sizes),
        cost_estimate=SMALL,
        name="finish",
    )(came, *after)


def total_kernel(*refs, count):
    total = refs[0][...].astype(jnp.float32)
    for n in range(1, count):
        total = total + refs[n][...].astype(jnp.float32)
    refs[-1][...] = total


def totalled(pieces, after):
    vmem = pl.BlockSpec(memory_space=pltpu.VMEM)
    return pl.pallas_call(
        functools.partial(total_kernel, count=len(pieces)),
        out_shape=jax.ShapeDtypeStruct(pieces[0].shape, jnp.float32),
        in_specs=[vmem] * len(pieces) + [pl.BlockSpec(memory_space=pl.ANY)] * len(after),
        out_specs=vmem,
        cost_estimate=SMALL,
        name="total",
    )(*pieces, *after)


def tie_kernel(*refs):
    pass


def tie(value, after):
    anywhere = pl.BlockSpec(memory_space=pl.ANY)
    return pl.pallas_call(
        tie_kernel,
        out_shape=jax.ShapeDtypeStruct(value.shape, value.dtype),
        in_specs=[anywhere] * (1 + len(after)),
        out_specs=anywhere,
        input_output_aliases={0: 0},
        name="tie",
    )(value, *after)


def times(first_op, second_op):
    return lax.dot_general(first_op, second_op, NN, preferred_element_type=jnp.float32)


def swap(value, bit):
    size = lax.axis_size("seq")
    return lax.ppermute(value, "seq", [(i, i ^ bit) for i in range(size)])


def ahead(value, step):
    size = lax.axis_size("batch")
    return lax.ppermute(value, "batch", [(i, (i + step) % size) for i in range(size)])


class Sum:
    wide = 512

    def __init__(self, weights, half, bits):
        self.weights, self.half, self.bits = weights, half, bits
        self.seq = lax.axis_size("seq")
        self.batch = lax.axis_size("batch")
        self.next = 1

    def picks(self, sent):
        me = lax.axis_index("seq")
        first = me ^ self.bits[0] if sent else me
        found = [0]
        for bit in self.bits[:0:-1]:
            found = found + [f | bit for f in found]
        return (jnp.array(found, jnp.int32) ^ first).astype(jnp.int32)

    def send(self, after=()):
        sent = outer(self.weights, self.picks(True), self.half, self.batch, self.wide, None, after)
        self.came = swap(sent, self.bits[0])
        return [sent]

    def keep(self, after=()):
        self.total = list(
            outer(self.weights, self.picks(False), self.half, self.batch, self.wide, self.came, after)
        )

    def pass_on(self):
        count = len(self.total) // 2
        sent = self.total[count:]
        self.total = self.total[:count]
        self.came = [swap(one, self.bits[self.next]) for one in sent]
        self.next += 1
        return sent

    def take(self):
        self.total = [
            (a.astype(jnp.float32) + b.astype(jnp.float32)).astype(jnp.bfloat16)
            for a, b in zip(self.total, self.came)
        ]


class Sums:
    def __init__(self, weights, orders):
        self.weights = weights
        self.halves = [Sum(weights, half, bits) for half, bits in enumerate(orders)]

    def send(self, after=()):
        return sum([one.send(after) for one in self.halves], [])

    def came(self):
        return jax.tree.leaves([one.came for one in self.halves])

    def keep(self, after=(), after_last=()):
        for one in self.halves:
            one.keep(tuple(after) + (tuple(after_last) if one is self.halves[-1] else ()))
        return sum([one.pass_on() for one in self.halves], [])

    def spread(self, after=()):
        for one in self.halves:
            while one.next < len(one.bits):
                one.take()
                one.pass_on()
        pieces = merge([(one.total[0], one.came[0]) for one in self.halves], tuple(after))
        self.spread_out = lax.all_to_all(pieces, "batch", 0, 0, tiled=True)
        return [pieces]

    def result(self, after=()):
        devices = lax.axis_size("seq") * lax.axis_size("batch")
        sizes = [first.shape[0] // devices for first, _, _, _ in self.weights]
        counts = [second.shape[1] // 2 // Sum.wide for _, _, second, _ in self.weights]
        return finish(self.spread_out, sizes, counts, tuple(after))


def turn_tables(position):
    half = HD // 2
    lane = jnp.arange(LANES, dtype=jnp.int32)
    rates = jnp.exp((lane % half).astype(jnp.float32) * (-math.log(10000.0) / half))
    angles = position.astype(jnp.float32)[:, None] * rates[None, :]
    side = jnp.where((lane % HD) < half, -1.0, 1.0).astype(jnp.float32)
    return jnp.cos(angles), jnp.sin(angles) * side[None, :]


def all_pieces(value):
    batch = lax.axis_size("batch")
    place = lax.axis_index("batch")
    out = jnp.zeros((batch,) + value.shape, value.dtype)
    out = lax.dynamic_update_index_in_dim(out, value, place, 0)
    for step in range(1, batch):
        out = lax.dynamic_update_index_in_dim(
            out, ahead(value, step), (place - step) % batch, 0
        )
    return out


def all_pieces_for(value):
    batch = lax.axis_size("batch")
    place = lax.axis_index("batch")
    pieces = [
        lax.dynamic_index_in_dim(value, (place + step) % batch, 0, keepdims=False)
        for step in range(batch)
    ]
    return [ahead(piece, step) if step else piece for step, piece in enumerate(pieces)]


def seq_pieces(value, bits):
    have = []
    for bit in bits:
        came = swap(value, bit)
        value = jnp.stack([value, came], axis=sum(b > bit for b in have))
        have.append(bit)
    return value.reshape((lax.axis_size("seq"),) + value.shape[len(have) :])


def seq_total(value):
    bit = 1
    while bit < lax.axis_size("seq"):
        value = value + swap(value, bit)
        bit *= 2
    return value


def shards(
    frames_in,
    skip_in,
    time_table,
    timestep,
    lengths,
    span_start,
    span_len,
    skip_proj,
    mod_proj,
    mod_bias,
    qkv_proj,
    out_proj,
    up_proj,
    up_bias,
    down_proj,
    cotangent,
):
    seq = lax.axis_size("seq")
    batch = lax.axis_size("batch")
    seq_at = lax.axis_index("seq")
    batch_at = lax.axis_index("batch")
    device = seq_at * batch + batch_at
    devices = seq * batch
    inputs = frames_in[0]
    skip_rows = skip_in[0]
    rows, width = inputs.shape
    hidden = up_proj.shape[1]
    frames = rows * seq
    heads = HEADS // seq
    utts = lengths.shape[1]

    high = [seq >> (i + 1) for i in range(seq.bit_length() - 2)]
    low = high[::-1]
    rel = (jnp.arange(seq, dtype=jnp.int32) ^ seq_at).astype(jnp.int32)
    half = width // 2
    skip_each, qkv_each, out_each, up_each, down_each = (
        skip_proj.shape[0],
        qkv_proj.shape[0],
        out_proj.shape[0],
        up_proj.shape[0],
        down_proj.shape[0],
    )
    per_device = width // seq
    groups = width // LANES
    full_skip = lax.all_gather(all_pieces(skip_proj), "seq", axis=0, tiled=True)
    own_rows = all_pieces(qkv_proj)
    own_qkv = own_rows.reshape(batch, qkv_each, 3, seq, per_device)
    own_qkv = lax.all_to_all(own_qkv.transpose(3, 2, 0, 1, 4), "seq", 0, 0, tiled=True)
    own_qkv = jnp.pad(own_qkv, ((0, 0),) * 4 + ((0, LANES - per_device),))
    own_qkv = own_qkv.transpose(0, 2, 3, 1, 4).reshape(width, 3 * LANES)
    late = jnp.concatenate(
        [down_proj, out_proj]
        + [up_proj[:, p * width : (p + 1) * width] for p in range(hidden // width)],
        axis=0,
    )
    late = lax.all_gather(late, BOTH, axis=0, tiled=False)
    full_qkv = lax.all_gather(own_rows, "seq", axis=0, tiled=True)

    utt_lengths = lengths[0]
    ends = jnp.cumsum(utt_lengths).astype(jnp.int32)
    starts = ends - utt_lengths
    frame_ids = seq_at * rows + jnp.arange(rows, dtype=jnp.int32)
    group_ids = jnp.arange(frames, dtype=jnp.int32)

    def members(ids):
        return (ids[:, None] >= starts[None, :]) & (ids[:, None] < ends[None, :])

    member = members(frame_ids)
    member_int = member.astype(jnp.int32)
    position = frame_ids - jnp.sum(member_int * starts[None, :], axis=1)
    span_first = jnp.sum(member_int * span_start[0][None, :], axis=1)
    span_after = span_first + jnp.sum(member_int * span_len[0][None, :], axis=1)
    in_span = ((position >= span_first) & (position < span_after)).astype(jnp.float32)
    member_rows = member.astype(jnp.float32)
    group_position = group_ids - jnp.sum(members(group_ids).astype(jnp.int32) * starts[None, :], axis=1)
    group_cos, group_sin = turn_tables(group_position)

    steps = all_pieces(timestep[0]).reshape(-1)
    step_pick = (
        steps[:, None] == jnp.arange(time_table.shape[0], dtype=jnp.int32)[None, :]
    ).astype(jnp.float32)
    time_rows = jnp.dot(step_pick, time_table.astype(jnp.float32), precision=highest)
    silu_value, silu_pull = jax.vjp(jax.nn.silu, time_rows)
    time_vec = silu_value.astype(jnp.bfloat16)
    terms = times(time_vec, mod_proj)
    def placed(bias):
        return lax.dynamic_update_slice(
            jnp.zeros((4 * width,), jnp.float32), bias.astype(jnp.float32), (device * bias.shape[0],)
        )

    terms = (terms + placed(mod_bias)[None, :]).reshape(batch, utts, 4 * width)
    up_terms = jnp.broadcast_to(placed(up_bias), (batch, 1, 4 * width))
    terms = jnp.concatenate([terms, up_terms], axis=1)
    modulation = lax.dynamic_index_in_dim(terms, batch_at, 0, keepdims=False)
    for step in range(1, batch):
        modulation = modulation + ahead(
            lax.dynamic_index_in_dim(terms, (batch_at + step) % batch, 0, keepdims=False), step
        )
    modulation = seq_total(modulation)
    full_bup = modulation[utts:]
    modulation = modulation[:utts]
    info = jnp.pad(member_rows, ((0, 0), (0, LANES - utts)))
    branch = (cotangent[0].astype(jnp.float32) * in_span[:, None]).astype(jnp.bfloat16)
    joined = jnp.concatenate([inputs.T, skip_rows.T], axis=0)
    branch_pair = (branch, swap(branch, 1))
    joined_pair = (joined, swap(joined, 1))

    stream_in, *normed_one = front(
        inputs, skip_rows, info, modulation, full_skip, utts,
        (group_cos, group_sin, own_qkv, branch_pair[1], joined_pair[1]),
    )
    normed_halves = [seq_pieces(normed_one[0], low + [1]), seq_pieces(normed_one[1], high + [1])]
    held = project(rel, normed_halves, own_qkv, group_cos, group_sin, ())
    head_out, log_sums = attend(held, ends, heads, 1536, 1536)
    att = lax.all_to_all(
        head_out.reshape(seq, rows, LANES)[:, :, :per_device], "seq", 0, 0, tiled=True
    )
    if per_device < LANES:
        att = att.reshape(groups, 2, rows, per_device).transpose(0, 2, 1, 3).reshape(groups, rows, LANES)

    result, attended, normed_two, activated, grad_pre, grad_mid, grad_low, back, mod_two, bup_terms = middle(
        att, stream_in, info, modulation, branch, late, down_each, out_each, up_each, full_bup, utts
    )
    if per_device < LANES:
        back = back.reshape(groups, rows, 2, per_device).transpose(0, 2, 1, 3).reshape(seq, rows, per_device)
        back = jnp.pad(back, ((0, 0), (0, 0), (0, LANES - per_device)))
    back = lax.all_to_all(back, "seq", 0, 0, tiled=True).reshape(frames, LANES)

    def pairs(first, second):
        return (first[0], first[1], second[0], second[1])

    def pair(value):
        return (value, swap(value, 1))

    first_weights = [
        pairs(pair(activated), branch_pair),
        pairs(pair(normed_two), pair(grad_pre)),
        pairs(pair(attended), pair(grad_low)),
    ]
    sums = Sums(first_weights, (low, high))
    waits = sums.send()

    grad_held = attend_back(
        held, back, head_out, log_sums, group_cos, group_sin, ends, heads, waits + [full_qkv], 1024, 1024
    )
    grad_held = outgoing(rel, grad_held, normed_halves, tuple(sums.came()))
    mark = (grad_held,)
    grad_held = lax.all_to_all(grad_held[..., :per_device], "seq", 0, 0, tiled=True)
    if per_device < LANES:
        grad_held = grad_held.reshape(groups, 2, 3, -1, per_device).transpose(0, 2, 3, 1, 4)
        grad_held = grad_held.reshape(groups, 3, -1, LANES)
    sums.keep(mark)
    waits = sums.spread()

    grad_stream, row_sums = tail(
        grad_held, stream_in, info, modulation, grad_mid, full_qkv, qkv_each,
        mod_two, bup_terms, utts, waits,
    )
    last_sums = Sums([pairs(joined_pair, pair(grad_stream))], (low, high))
    row_sums = row_sums + swap(row_sums, 1)
    waits = last_sums.send((row_sums,))
    grad_inputs, grad_skip_rows = unjoin(grad_stream, full_skip, skip_each, waits)
    waits = last_sums.keep((grad_inputs,))
    row_sums = tie(row_sums, waits)
    for bit in low:
        row_sums = row_sums + swap(row_sums, bit)
    qkv_came = all_pieces_for(cut(tie(grad_held, waits), rows))
    waits = last_sums.spread((row_sums, sums.spread_out))
    row_sums = all_pieces(tie(row_sums, waits))
    grad_down, grad_up, grad_out_w = sums.result(waits)
    grad_qkv_w = totalled(qkv_came, (last_sums.spread_out,))
    (grad_skip_w,) = last_sums.result()

    grad_modulation = row_sums[:, :utts].reshape(batch * utts, 4 * width)
    grad_bup = lax.dynamic_slice_in_dim(
        jnp.sum(row_sums[:, utts], axis=0), device * up_bias.shape[0], up_bias.shape[0]
    )
    grad_bmod = lax.dynamic_slice_in_dim(
        jnp.sum(grad_modulation, axis=0), device * mod_bias.shape[0], mod_bias.shape[0]
    )
    grad_mod_w = jnp.dot(time_vec.astype(jnp.float32).T, grad_modulation, precision=highest)
    grad_time_vec = jnp.dot(grad_modulation, mod_proj.astype(jnp.float32).T, precision=highest)
    grad_table = jnp.dot(step_pick.T, silu_pull(grad_time_vec)[0], precision=highest)
    return (
        result[None],
        grad_inputs[None],
        grad_skip_rows[None],
        grad_table,
        grad_skip_w,
        grad_mod_w,
        grad_bmod,
        grad_qkv_w,
        grad_out_w,
        grad_up,
        grad_bup,
        grad_down,
    )


def solution(mesh):
    return jax.shard_map(
        shards,
        mesh=mesh,
        in_specs=(
            P("batch", "seq", None),
            P("batch", "seq", None),
            P(None, BOTH),
            P("batch", None),
            P("batch", None),
            P("batch", None),
            P("batch", None),
            P(BOTH, None),
            P(BOTH, None),
            P(BOTH),
            P(BOTH, None),
            P(BOTH, None),
            P(BOTH, None),
            P(BOTH),
            P(BOTH, None),
            P("batch", "seq", None),
        ),
        out_specs=(
            P("batch", "seq", None),
            P("batch", "seq", None),
            P("batch", "seq", None),
            P(None, BOTH),
            P(BOTH, None),
            P(BOTH, None),
            P(BOTH),
            P(BOTH, None),
            P(BOTH, None),
            P(BOTH, None),
            P(BOTH),
            P(BOTH, None),
        ),
        check_vma=False,
    )
```

```python
import functools
import math

import jax
import jax.numpy as jnp
from jax import lax
from jax.experimental import pallas as pl
from jax.experimental.pallas import tpu as pltpu
from jax.sharding import PartitionSpec as P

HEADS = 16
HD = 64
LANES = 128
MASKED = -(2.0 ** 100)
NORM_EPS = 1e-06
SMALL = pl.CostEstimate(flops=1024, bytes_accessed=1024, transcendentals=0)
VMEM = 60 * 1024 * 1024
BOTH = ("seq", "batch")
NT = (((1,), (1,)), ((), ()))
NN = (((1,), (0,)), ((), ()))
TN = (((0,), (0,)), ((), ()))
highest = lax.Precision.HIGHEST


def mm(a, b, dims):
    return lax.dot_general(a, b, dims, preferred_element_type=jnp.float32)


def utt_of(ends_ref, rows, utts):
    found = jnp.zeros_like(rows)
    for u in range(utts - 1):
        found = found + (rows >= ends_ref[u]).astype(jnp.int32)
    return found


def key_range(ends_ref, first, last, utts, frames):
    low = 0
    high = frames
    for u in range(utts - 1):
        low = jnp.where(first >= ends_ref[u], ends_ref[u], low)
    for u in reversed(range(utts - 1)):
        high = jnp.where(last < ends_ref[u], ends_ref[u], high)
    return low, high


def split3(x):
    a = x.astype(jnp.bfloat16).astype(jnp.float32)
    b = (x - a).astype(jnp.bfloat16).astype(jnp.float32)
    return a, b, x - a - b


def fwd_kernel(ends_ref, qkv_ref, out_ref, lse_ref, q_s, k_s, v_s, m_s, acc_s, *, heads, utts, bq, bk):
    sources, _, rows, _ = qkv_ref.shape
    frames = sources * rows

    def build(src, carry):
        at = pl.multiple_of(src * rows, rows)
        lane = lax.broadcasted_iota(jnp.int32, (rows, LANES), 1)
        row = lax.broadcasted_iota(jnp.int32, (rows, LANES), 0) + at
        utt = utt_of(ends_ref, row, utts)
        for h in range(heads):
            spare = (1 - h) * HD
            mine = (lane >= HD) if h else (lane < HD)
            slot = lane - spare
            is_slot = (slot >= 0) & (slot < utts)
            qf = jnp.where(is_slot & (slot != utt), MASKED, 0.0)
            kf = jnp.where(slot == utt, 1.0, 0.0)
            vf = jnp.where(slot == 0, 1.0, 0.0)
            for part, feat, dst in ((0, qf, q_s), (1, kf, k_s)):
                x = qkv_ref[src, part].astype(jnp.float32)
                dst[h, pl.ds(at, rows), :] = jnp.where(mine, x, feat).astype(jnp.bfloat16)
            x = jnp.where(mine, qkv_ref[src, 2].astype(jnp.float32), vf)
            v_s[h, :, pl.ds(at, rows)] = x.T.astype(jnp.bfloat16)
        return carry

    lax.fori_loop(0, sources, build, 0)

    def q_block(i, carry):
        at = pl.multiple_of(i * bq, bq)
        low, high = key_range(ends_ref, at, at + bq - 1, utts, frames)
        m_s[...] = jnp.full(m_s.shape, -3.0e38, jnp.float32)
        acc_s[...] = jnp.zeros(acc_s.shape, jnp.float32)

        def k_block(j, inner):
            kat = pl.multiple_of(j * bk, bk)
            for h in range(heads):
                s = mm(k_s[h, pl.ds(kat, bk), :], q_s[h, pl.ds(at, bq), :], NT)
                old = m_s[h]
                top = jnp.maximum(old, jnp.max(s, axis=0, keepdims=True))
                alpha = jnp.exp(old - top)
                p = jnp.exp(s - top).astype(jnp.bfloat16)
                acc_s[h] = acc_s[h] * alpha + mm(v_s[h, :, pl.ds(kat, bk)], p, NN)
                m_s[h] = top
            return inner

        lax.fori_loop(low // bk, (high + bk - 1) // bk, k_block, 0)
        lane = lax.broadcasted_iota(jnp.int32, (LANES, bq), 0)
        out = None
        lse = None
        for h in range(heads):
            spare = (1 - h) * HD
            acc = acc_s[h]
            total = acc[spare : spare + 1, :]
            o = acc / total
            l = jnp.broadcast_to(m_s[h] + jnp.log(total), (LANES, bq))
            out = o if out is None else jnp.where(lane < HD, out, o)
            lse = l if lse is None else jnp.where(lane < HD, lse, l)
        out_ref[pl.ds(at, bq), :] = out.T.astype(jnp.bfloat16)
        lse_ref[pl.ds(at, bq), :] = lse.T
        return carry

    lax.fori_loop(0, frames // bq, q_block, 0)


def attend(qkv, ends, heads, bq, bk):
    sources, _, rows, _ = qkv.shape
    frames = sources * rows
    utts = ends.shape[0]
    return pl.pallas_call(
        functools.partial(fwd_kernel, heads=heads, utts=utts, bq=bq, bk=bk),
        out_shape=(
            jax.ShapeDtypeStruct((frames, LANES), jnp.bfloat16),
            jax.ShapeDtypeStruct((frames, LANES), jnp.float32),
        ),
        in_specs=[pl.BlockSpec(memory_space=pltpu.SMEM), pl.BlockSpec(memory_space=pltpu.VMEM)],
        out_specs=(pl.BlockSpec(memory_space=pltpu.VMEM), pl.BlockSpec(memory_space=pltpu.VMEM)),
        scratch_shapes=[pltpu.VMEM((heads, frames, LANES), jnp.bfloat16)] * 2
        + [
            pltpu.VMEM((heads, LANES, frames), jnp.bfloat16),
            pltpu.VMEM((heads, 1, bq), jnp.float32),
            pltpu.VMEM((heads, LANES, bq), jnp.float32),
        ],
        compiler_params=pltpu.CompilerParams(vmem_limit_bytes=VMEM),
        cost_estimate=pl.CostEstimate(
            flops=40 * heads * frames * frames * HD, bytes_accessed=frames * LANES * 12,
            transcendentals=heads * frames * frames,
        ),
        name="attend",
    )(ends, qkv)


def bwd_kernel(
    ends_ref, qkv_ref, da_ref, out_ref, lse_ref, cos_ref, sin_ref, *rest, heads, utts, bq, bk
):
    grad_ref, q_s, k_s, kt_s, v_s, d_s, gq_s, gk_s, gv_s = rest[-9:]
    sources, _, rows, _ = qkv_ref.shape
    frames = sources * rows

    def build(src, carry):
        at = pl.multiple_of(src * rows, rows)
        lane = lax.broadcasted_iota(jnp.int32, (rows, LANES), 1)
        row = lax.broadcasted_iota(jnp.int32, (rows, LANES), 0) + at
        utt = utt_of(ends_ref, row, utts)
        da = da_ref[pl.ds(at, rows), :].astype(jnp.float32)
        prod = da * out_ref[pl.ds(at, rows), :].astype(jnp.float32)
        lse = lse_ref[pl.ds(at, rows), :]
        for h in range(heads):
            spare = (1 - h) * HD
            mine = (lane >= HD) if h else (lane < HD)
            slot = lane - spare
            is_slot = (slot >= 0) & (slot < utts)
            delta = jnp.sum(jnp.where(mine, prod, 0.0), axis=1, keepdims=True)
            l3 = split3(-lse[:, h * HD : h * HD + 1])
            d3 = split3(-delta)
            qf = jnp.where(is_slot & (slot != utt), MASKED, 0.0)
            df = jnp.zeros_like(qf)
            for n in range(3):
                qf = jnp.where(slot == utts + n, l3[n], qf)
                df = jnp.where(slot == n, d3[n], df)
            kf = jnp.where((slot == utt) | ((slot >= utts) & (slot < utts + 3)), 1.0, 0.0)
            vf = jnp.where((slot >= 0) & (slot < 3), 1.0, 0.0)
            for x, feat, dst in (
                (qkv_ref[src, 0], qf, q_s), (qkv_ref[src, 1], kf, k_s), (qkv_ref[src, 2], vf, v_s),
            ):
                dst[h, pl.ds(at, rows), :] = jnp.where(mine, x.astype(jnp.float32), feat).astype(jnp.bfloat16)
            d_s[h, pl.ds(at, rows), :] = jnp.where(mine, da, df).astype(jnp.bfloat16)
            kt_s[h, :, pl.ds(at, rows)] = qkv_ref[src, 1].T
        gq_s[:, :, pl.ds(at, rows)] = jnp.zeros((heads, LANES, rows), jnp.float32)
        return carry

    lax.fori_loop(0, sources, build, 0)

    def k_block(j, carry):
        kat = pl.multiple_of(j * bk, bk)
        low, high = key_range(ends_ref, kat, kat + bk - 1, utts, frames)
        gk_s[:, pl.ds(kat, bk), :] = jnp.zeros((heads, bk, LANES), jnp.float32)
        gv_s[:, pl.ds(kat, bk), :] = jnp.zeros((heads, bk, LANES), jnp.float32)

        def q_block(i, inner):
            at = pl.multiple_of(i * bq, bq)
            for h in range(heads):
                q = q_s[h, pl.ds(at, bq), :]
                d = d_s[h, pl.ds(at, bq), :]
                k = k_s[h, pl.ds(kat, bk), :]
                p = jnp.exp(mm(k, q, NT))
                ds = (p * mm(v_s[h, pl.ds(kat, bk), :], d, NT)).astype(jnp.bfloat16)
                gv_s[h, pl.ds(kat, bk), :] += mm(p.astype(jnp.bfloat16), d, NN)
                gk_s[h, pl.ds(kat, bk), :] += mm(ds, q, NN)
                gq_s[h, :, pl.ds(at, bq)] += mm(kt_s[h, :, pl.ds(kat, bk)], ds, NN)
            return inner

        lax.fori_loop(low // bq, (high + bq - 1) // bq, q_block, 0)
        return carry

    lax.fori_loop(0, frames // bk, k_block, 0)

    def finish(src, carry):
        at = pl.multiple_of(src * rows, rows)
        lane = lax.broadcasted_iota(jnp.int32, (rows, LANES), 1)
        first = (lane % HD) < HD // 2
        cos = cos_ref[pl.ds(at, rows), :]
        sin = sin_ref[pl.ds(at, rows), :]

        def both(ref):
            x = ref[0, pl.ds(at, rows), :]
            return jnp.where(lane < HD, x, ref[1, pl.ds(at, rows), :]) if heads == 2 else x

        def both_flipped(ref):
            x = ref[0, :, pl.ds(at, rows)]
            if heads == 2:
                row = lax.broadcasted_iota(jnp.int32, (LANES, rows), 0)
                x = jnp.where(row < HD, x, ref[1, :, pl.ds(at, rows)])
            return x.T

        def unturn(x):
            partner = jnp.where(first, pltpu.roll(x, LANES - HD // 2, 1), pltpu.roll(x, HD // 2, 1))
            return x * cos - partner * sin

        grad_ref[src, 0] = (unturn(both_flipped(gq_s)) * HD ** -0.5).astype(jnp.bfloat16)
        grad_ref[src, 1] = unturn(both(gk_s)).astype(jnp.bfloat16)
        grad_ref[src, 2] = both(gv_s).astype(jnp.bfloat16)
        return carry

    lax.fori_loop(0, sources, finish, 0)


def attend_back(qkv, grad_out, out, lse, cos, sin, ends, heads, after, bq, bk):
    sources, _, rows, _ = qkv.shape
    frames = sources * rows
    utts = ends.shape[0]
    vmem = pl.BlockSpec(memory_space=pltpu.VMEM)
    return pl.pallas_call(
        functools.partial(bwd_kernel, heads=heads, utts=utts, bq=bq, bk=bk),
        out_shape=jax.ShapeDtypeStruct(qkv.shape, jnp.bfloat16),
        in_specs=[pl.BlockSpec(memory_space=pltpu.SMEM)]
        + [vmem] * 6
        + [pl.BlockSpec(memory_space=pl.ANY)] * len(after),
        out_specs=vmem,
        scratch_shapes=[pltpu.VMEM((heads, frames, LANES), jnp.bfloat16)] * 2
        + [pltpu.VMEM((heads, LANES, frames), jnp.bfloat16)]
        + [pltpu.VMEM((heads, frames, LANES), jnp.bfloat16)] * 2
        + [pltpu.VMEM((heads, LANES, frames), jnp.float32)]
        + [pltpu.VMEM((heads, frames, LANES), jnp.float32)] * 2,
        compiler_params=pltpu.CompilerParams(vmem_limit_bytes=VMEM),
        cost_estimate=pl.CostEstimate(
            flops=64 * heads * frames * frames * HD, bytes_accessed=frames * LANES * 24,
            transcendentals=heads * frames * frames,
        ),
        name="attend_back",
    )(ends, qkv, grad_out, out, lse, cos, sin, *after)


def outgoing_kernel(rel_ref, grad_ref, low_ref, high_ref, *rest):
    out_ref, total_s = rest[-2:]
    src = pl.program_id(0)
    rows = grad_ref.shape[2]
    grads = jnp.concatenate([grad_ref[0, part] for part in range(3)], axis=1)
    normed = jnp.concatenate([low_ref[0], high_ref[0]], axis=1)
    term = mm(normed, grads, TN)
    for part in range(3):
        out_ref[src, part, 0:rows] = grad_ref[0, part]

    @pl.when(src == 0)
    def _():
        total_s[...] = term

    @pl.when(src > 0)
    def _():
        total_s[...] += term

    @pl.when(src == pl.num_programs(0) - 1)
    def _():
        total = total_s[...].astype(jnp.bfloat16)
        each = out_ref.shape[2] - rows
        for dest in range(out_ref.shape[0]):
            for part in range(3):
                out_ref[dest, part, rows:] = total[
                    dest * each : (dest + 1) * each, part * LANES : (part + 1) * LANES
                ]


def outgoing(rel, grads, halves, after):
    sources, _, rows, _ = grads.shape
    half = halves[0].shape[2]
    each = 2 * half // sources
    shape = (sources, 3, rows + each, LANES)
    side = pl.BlockSpec((1, rows, half), lambda i, rel: (rel[i], 0, 0))
    return pl.pallas_call(
        outgoing_kernel,
        grid_spec=pltpu.PrefetchScalarGridSpec(
            num_scalar_prefetch=1,
            grid=(sources,),
            in_specs=[pl.BlockSpec((1, 3, rows, LANES), lambda i, rel: (i, 0, 0, 0)), side, side]
            + [pl.BlockSpec(memory_space=pl.ANY)] * len(after),
            out_specs=pl.BlockSpec(shape, lambda i, rel: (0, 0, 0, 0)),
            scratch_shapes=[pltpu.VMEM((2 * half, 3 * LANES), jnp.float32)],
        ),
        out_shape=jax.ShapeDtypeStruct(shape, jnp.bfloat16),
        cost_estimate=pl.CostEstimate(
            flops=12 * rows * sources * half * LANES, bytes_accessed=16 * half * half, transcendentals=0
        ),
        compiler_params=pltpu.CompilerParams(vmem_limit_bytes=VMEM),
        name="outgoing",
    )(rel, grads, *halves, *after)


def unjoin_kernel(grad_ref, weight_ref, *rest):
    width = grad_ref.shape[1]
    i = pl.program_id(0)
    made = mm(grad_ref[...], weight_ref[...].reshape(-1, width), NT).astype(jnp.bfloat16)

    @pl.when(i < 2)
    def _():
        rest[-2][...] = made

    @pl.when(i >= 2)
    def _():
        rest[-1][...] = made


def unjoin(grad, early, skip_each, after):
    rows, width = grad.shape
    devices = early.shape[0]
    half = width // 2
    return pl.pallas_call(
        unjoin_kernel,
        grid=(4,),
        out_shape=[jax.ShapeDtypeStruct((rows, width), jnp.bfloat16)] * 2,
        in_specs=[
            pl.BlockSpec((rows, width), lambda i: (0, 0)),
            pl.BlockSpec((devices // 4, skip_each, width), lambda i: (i, 0, 0)),
        ]
        + [pl.BlockSpec(memory_space=pl.ANY)] * len(after),
        out_specs=[
            pl.BlockSpec((rows, half), lambda i: (0, jnp.minimum(i, 1))),
            pl.BlockSpec((rows, half), lambda i: (0, jnp.maximum(i - 2, 0))),
        ],
        cost_estimate=pl.CostEstimate(
            flops=4 * rows * width * width, bytes_accessed=6 * width * width, transcendentals=0
        ),
        compiler_params=pltpu.CompilerParams(vmem_limit_bytes=VMEM),
        name="unjoin",
    )(grad, early, *after)


def normalise(hidden):
    centred = hidden - jnp.mean(hidden, axis=-1, keepdims=True)
    inverse = lax.rsqrt(jnp.mean(centred * centred, axis=-1, keepdims=True) + NORM_EPS)
    return centred * inverse, inverse


def normalise_back(grad, normed, inverse):
    return inverse * (
        grad
        - jnp.mean(grad, axis=-1, keepdims=True)
        - normed * jnp.mean(grad * normed, axis=-1, keepdims=True)
    )


def per_row(info, table, utts):
    total = info[:, 0:1] * table[0:1]
    for u in range(1, utts):
        total = total + info[:, u : u + 1] * table[u : u + 1]
    return total


def sums_by_utt(ref, at, info, value, utts):
    width = value.shape[1]
    for u in range(utts):
        ref[u : u + 1, at : at + width] = jnp.sum(info[:, u : u + 1] * value, axis=0, keepdims=True)


def gelu_parts(x):
    rate = math.sqrt(2.0 / math.pi)
    square = x * x
    inner = jnp.tanh(x * (rate + rate * 0.044715 * square))
    half = 0.5 + 0.5 * inner
    value = x * half
    slope = half + 0.5 * x * (1.0 - inner * inner) * (rate + 3 * rate * 0.044715 * square)
    return value, slope


def front_kernel(frames_ref, skip_ref, info_ref, mod_ref, weight_ref, *rest, utts, steps):
    stream_ref, normed_low_ref, normed_high_ref = rest[-3:]
    i = pl.program_id(0)
    width = stream_ref.shape[1]
    half = width // 2
    weight = weight_ref[...].reshape(-1, width)
    depth = weight.shape[0]

    for n in range(steps):
        @pl.when(i == n)
        def _(n=n):
            source = frames_ref if n * depth < width else skip_ref
            at = n * depth % width
            term = mm(source[:, at : at + depth], weight, NN)
            stream_ref[...] = term if n == 0 else stream_ref[...] + term

    @pl.when(i == steps - 1)
    def _():
        info = info_ref[...]
        unit, _unused = normalise(stream_ref[...])
        scale = per_row(info, 1.0 + mod_ref[:, :width], utts)
        shift = per_row(info, mod_ref[:, width : 2 * width], utts)
        normed = (unit * scale + shift).astype(jnp.bfloat16)
        normed_low_ref[...] = normed[:, :half]
        normed_high_ref[...] = normed[:, half:]


def front(frames, skip, info, modulation, weights, utts, after):
    rows, width = frames.shape
    devices, each, _ = weights.shape
    half = width // 2
    steps = 4

    def fixed(*shape):
        return pl.BlockSpec(shape, lambda i: (0,) * len(shape))

    return pl.pallas_call(
        functools.partial(front_kernel, utts=utts, steps=steps),
        grid=(steps,),
        in_specs=[
            fixed(rows, width),
            fixed(rows, width),
            fixed(rows, LANES),
            fixed(utts, 4 * width),
            pl.BlockSpec((devices // steps, each, width), lambda i: (i, 0, 0)),
        ]
        + [pl.BlockSpec(memory_space=pl.ANY)] * len(after),
        out_specs=(fixed(rows, width), fixed(rows, half), fixed(rows, half)),
        out_shape=(
            jax.ShapeDtypeStruct((rows, width), jnp.float32),
            jax.ShapeDtypeStruct((rows, half), jnp.bfloat16),
            jax.ShapeDtypeStruct((rows, half), jnp.bfloat16),
        ),
        compiler_params=pltpu.CompilerParams(vmem_limit_bytes=VMEM),
        cost_estimate=pl.CostEstimate(
            flops=4 * rows * width * width, bytes_accessed=8 * width * width, transcendentals=0
        ),
        name="front",
    )(frames, skip, info, modulation, weights, *after)


def project_kernel(rel_ref, low_ref, high_ref, weight_ref, cos_ref, sin_ref, *rest):
    out_ref = rest[-1]
    normed = jnp.concatenate([low_ref[0], high_ref[0]], axis=1)
    turned = mm(normed, weight_ref[...], NN)
    lane = lax.broadcasted_iota(jnp.int32, (turned.shape[0], LANES), 1)
    first = (lane % HD) < HD // 2
    for part in range(3):
        x = turned[:, part * LANES : (part + 1) * LANES]
        if part < 2:
            partner = jnp.where(first, pltpu.roll(x, LANES - HD // 2, 1), pltpu.roll(x, HD // 2, 1))
            x = x * cos_ref[...] + partner * sin_ref[...]
        if part == 0:
            x = x * HD ** -0.5
        out_ref[0, part] = x.astype(jnp.bfloat16)


def project(rel, halves, weight, cos, sin, after):
    sources, rows, half = halves[0].shape
    side = pl.BlockSpec((1, rows, half), lambda i, rel: (rel[i], 0, 0))
    table = pl.BlockSpec((rows, LANES), lambda i, rel: (i, 0))
    return pl.pallas_call(
        project_kernel,
        grid_spec=pltpu.PrefetchScalarGridSpec(
            num_scalar_prefetch=1,
            grid=(sources,),
            in_specs=[side, side, pl.BlockSpec(weight.shape, lambda i, rel: (0, 0)), table, table]
            + [pl.BlockSpec(memory_space=pl.ANY)] * len(after),
            out_specs=pl.BlockSpec((1, 3, rows, LANES), lambda i, rel: (i, 0, 0, 0)),
        ),
        out_shape=jax.ShapeDtypeStruct((sources, 3, rows, LANES), jnp.bfloat16),
        compiler_params=pltpu.CompilerParams(vmem_limit_bytes=VMEM),
        cost_estimate=pl.CostEstimate(
            flops=12 * rows * sources * half * LANES, bytes_accessed=16 * half * half, transcendentals=0
        ),
        name="project",
    )(rel, *halves, weight, cos, sin, *after)


def middle_kernel(att_ref, stream_ref, info_ref, mod_ref, branch_ref, wout_ref, wup_ref, wdown_ref, bias_ref,
                  result_ref, attended_ref, normed_ref, act_ref, pre_ref, grad_ref, grad_low_ref,
                  back_ref, sums_ref, bup_ref,
                  mid_s, unit_s, inv_s, total_s, gn_s, att_s, normed_s, *, utts, blocks):
    b = pl.program_id(0)
    rows, width = stream_ref.shape
    groups = att_ref.shape[0]

    @pl.when(b == 0)
    def _():
        for s in range(groups):
            att_s[:, s * LANES : (s + 1) * LANES] = att_ref[s]
            attended_ref[s * LANES : (s + 1) * LANES, :] = att_ref[s].T
        mid = stream_ref[...] + mm(att_s[...], wout_ref[...].reshape(width, width), NN)
        mid_s[...] = mid
        unit, inverse = normalise(mid)
        unit_s[...] = unit
        inv_s[...] = jnp.broadcast_to(inverse, inv_s.shape)
        info = info_ref[...]
        scale = per_row(info, 1.0 + mod_ref[:, 2 * width : 3 * width], utts)
        shift = per_row(info, mod_ref[:, 3 * width :], utts)
        normed = (unit * scale + shift).astype(jnp.bfloat16)
        normed_s[...] = normed
        normed_ref[...] = normed.T

    up = wup_ref[...].reshape(width, -1)
    down = wdown_ref[...].reshape(-1, width)
    value, slope = gelu_parts(mm(normed_s[...], up, NN) + bias_ref[...])
    act = value.astype(jnp.bfloat16)
    act_ref[...] = act.T
    term = mm(act, down, NN)
    pre = (mm(branch_ref[...], down, NT) * slope).astype(jnp.bfloat16)
    pre_ref[...] = pre
    bup_ref[...] = jnp.sum(pre.astype(jnp.float32), axis=0, keepdims=True)
    grad_term = mm(pre, up, NT)

    @pl.when(b == 0)
    def _():
        total_s[...] = mid_s[...] + term
        gn_s[...] = grad_term

    @pl.when(b > 0)
    def _():
        total_s[...] += term
        gn_s[...] += grad_term

    @pl.when(b == blocks - 1)
    def _():
        result_ref[...] = total_s[...].astype(jnp.bfloat16)
        info = info_ref[...]
        scale = per_row(info, 1.0 + mod_ref[:, 2 * width : 3 * width], utts)
        gn = gn_s[...]
        unit = unit_s[...]
        grad = branch_ref[...].astype(jnp.float32) + normalise_back(gn * scale, unit, inv_s[:, :1])
        grad_ref[...] = grad
        low = grad.astype(jnp.bfloat16)
        grad_low_ref[...] = low
        back = mm(low, wout_ref[...].reshape(width, width), NT).astype(jnp.bfloat16)
        for s in range(groups):
            back_ref[s] = back[:, s * LANES : (s + 1) * LANES]
        sums_by_utt(sums_ref, 0, info, gn * unit, utts)
        sums_by_utt(sums_ref, width, info, gn, utts)


def middle(att, stream, info, modulation, cot, late, down_each, out_each, up_each, bias, utts):
    rows, width = stream.shape
    devices = late.shape[0]
    hidden = down_each * devices
    block = 1024
    blocks = hidden // block
    halves = width // block
    groups = width // LANES
    out_at = down_each // out_each
    up_at = (down_each + out_each) // up_each

    def fixed(*shape):
        return pl.BlockSpec(shape, lambda b: (0,) * len(shape))

    def whole(*shape, dtype=jnp.bfloat16):
        return jax.ShapeDtypeStruct(shape, dtype)

    f32 = jnp.float32
    return pl.pallas_call(
        functools.partial(middle_kernel, utts=utts, blocks=blocks),
        grid=(blocks,),
        out_shape=(
            whole(rows, width),
            whole(width, rows),
            whole(width, rows),
            whole(hidden, rows),
            whole(rows, hidden),
            whole(rows, width, dtype=f32),
            whole(rows, width),
            whole(groups, rows, LANES),
            whole(utts, 2 * width, dtype=f32),
            whole(1, hidden, dtype=f32),
        ),
        in_specs=[
            fixed(groups, rows, LANES),
            fixed(rows, width),
            fixed(rows, LANES),
            fixed(utts, 4 * width),
            fixed(rows, width),
            pl.BlockSpec((devices, out_each, width), lambda b: (0, out_at, 0)),
            pl.BlockSpec((devices, up_each, block), lambda b: (0, up_at + b // halves, b % halves)),
            pl.BlockSpec((devices // blocks, down_each, width), lambda b: (b, 0, 0)),
            pl.BlockSpec((1, block), lambda b: (0, b)),
        ],
        out_specs=(
            fixed(rows, width),
            fixed(width, rows),
            fixed(width, rows),
            pl.BlockSpec((block, rows), lambda b: (b, 0)),
            pl.BlockSpec((rows, block), lambda b: (0, b)),
            fixed(rows, width),
            fixed(rows, width),
            fixed(groups, rows, LANES),
            fixed(utts, 2 * width),
            pl.BlockSpec((1, block), lambda b: (0, b)),
        ),
        scratch_shapes=[
            pltpu.VMEM((rows, width), f32),
            pltpu.VMEM((rows, width), f32),
            pltpu.VMEM((rows, LANES), f32),
            pltpu.VMEM((rows, width), f32),
            pltpu.VMEM((rows, width), f32),
            pltpu.VMEM((rows, width), jnp.bfloat16),
            pltpu.VMEM((rows, width), jnp.bfloat16),
        ],
        compiler_params=pltpu.CompilerParams(vmem_limit_bytes=VMEM),
        cost_estimate=pl.CostEstimate(
            flops=12 * rows * hidden * width, bytes_accessed=20 * width * width,
            transcendentals=rows * hidden,
        ),
        name="middle",
    )(att, stream, info, modulation, cot, late, late, late, bias)


def tail_kernel(held_ref, stream_ref, info_ref, mod_ref, mid_ref, w_ref, two_ref, bup_ref,
                *rest, utts):
    out_ref, sums_ref, proj_s, gn_s = rest[-4:]
    p = pl.program_id(0)
    rows, width = stream_ref.shape
    groups = held_ref.shape[0]
    for s in range(groups):
        proj_s[:, s * LANES : (s + 1) * LANES] = held_ref[s, 0]
    term = mm(proj_s[...], w_ref[...].reshape(width, width), NT)

    @pl.when(p == 0)
    def _():
        gn_s[...] = term

    @pl.when(p > 0)
    def _():
        gn_s[...] += term

    @pl.when(p == 2)
    def _():
        info = info_ref[...]
        unit, inverse = normalise(stream_ref[...])
        scale = per_row(info, 1.0 + mod_ref[:, :width], utts)
        gn = gn_s[...]
        out_ref[...] = (mid_ref[...] + normalise_back(gn * scale, unit, inverse)).astype(jnp.bfloat16)
        sums_ref[0:utts, 2 * width :] = two_ref[...]
        sums_ref[utts : utts + 1, :] = bup_ref[...]
        sums_by_utt(sums_ref, 0, info, gn * unit, utts)
        sums_by_utt(sums_ref, width, info, gn, utts)


def tail(held, stream, info, modulation, mid, early, qkv_each, two, bup, utts, after):
    rows, width = stream.shape
    devices = early.shape[0]
    groups = held.shape[0]

    def fixed(*shape):
        return pl.BlockSpec(shape, lambda p: (0,) * len(shape))

    return pl.pallas_call(
        functools.partial(tail_kernel, utts=utts),
        grid=(3,),
        out_shape=(
            jax.ShapeDtypeStruct((rows, width), jnp.bfloat16),
            jax.ShapeDtypeStruct((utts + 1, 4 * width), jnp.float32),
        ),
        in_specs=[
            pl.BlockSpec((groups, 1, rows, LANES), lambda p: (0, p, 0, 0)),
            fixed(rows, width),
            fixed(rows, LANES),
            fixed(utts, 4 * width),
            fixed(rows, width),
            pl.BlockSpec((devices, qkv_each, width), lambda p: (0, 0, p)),
            fixed(utts, 2 * width),
            fixed(1, 4 * width),
        ]
        + [pl.BlockSpec(memory_space=pl.ANY)] * len(after),
        out_specs=(
            fixed(rows, width),
            fixed(utts + 1, 4 * width),
        ),
        scratch_shapes=[
            pltpu.VMEM((rows, width), jnp.bfloat16),
            pltpu.VMEM((rows, width), jnp.float32),
        ],
        compiler_params=pltpu.CompilerParams(vmem_limit_bytes=VMEM),
        cost_estimate=pl.CostEstimate(
            flops=6 * rows * width * width, bytes_accessed=14 * width * width, transcendentals=0
        ),
        name="tail",
    )(held, stream, info, modulation, mid, early, two, bup, *after)


def outer_kernel(pick_ref, *refs, sizes, counts, batch, chosen, adds, extra):
    u = pl.program_id(0)
    out_refs = refs[len(refs) - chosen :] if adds else [refs[-1].at[n] for n in range(chosen)]
    came = refs[len(refs) - chosen - extra - 1] if adds else None
    at = 0
    start = 0
    row = 0
    for each, count in zip(sizes, counts):
        own = refs[at : at + chosen]
        other = refs[at + chosen : at + 2 * chosen]
        second, second_other = refs[at + 2 * chosen : at + 2 * chosen + 2]
        for j in range(count):
            @pl.when(u == start + j)
            def _(own=own, other=other, second=second, second_other=second_other, each=each, row=row):
                left = jnp.concatenate(
                    [
                        jnp.concatenate([one[...] for one in own], axis=0),
                        jnp.concatenate([one[...] for one in other], axis=0),
                    ],
                    axis=1,
                )
                right = jnp.concatenate([second[...], second_other[...]], axis=0)
                total = mm(left, right, NN)
                for n in range(chosen):
                    for z in range(batch):
                        low = (n * batch + z) * each
                        part = total[low : low + each]
                        if adds:
                            part = part + came[n, z, row : row + each, :].astype(jnp.float32)
                        out_refs[n][z, row : row + each, :] = part.astype(jnp.bfloat16)
            row += each
        start += count
        at += 2 * chosen + 2


def outer_plain(weights, picks, half, batch, wide, add):
    made = []
    for first, first_other, second, second_other in weights:
        block = first.shape[0] // lax.axis_size("seq")
        columns = second.shape[1] // 2
        total = 0.0
        for one, two in ((first, second), (first_other, second_other)):
            chosen = [
                lax.dynamic_slice_in_dim(one, picks[n] * block, block, axis=0)
                for n in range(picks.shape[0])
            ]
            total = total + mm(
                jnp.concatenate(chosen, axis=0), two[:, half * columns : (half + 1) * columns], NN
            )
        total = total.reshape(picks.shape[0], batch, block // batch, columns // wide, wide)
        total = total.transpose(0, 1, 3, 2, 4)
        made.append(total.reshape(picks.shape[0], batch, -1, wide))
    made = jnp.concatenate(made, axis=2)
    if add is None:
        return made.astype(jnp.bfloat16)
    return list((made + add.astype(jnp.float32)).astype(jnp.bfloat16))


def outer(weights, picks, half, batch, wide, add=None, after=()):
    chosen = picks.shape[0]
    seq = lax.axis_size("seq")
    blocks = [first.shape[0] // seq for first, _, _, _ in weights]
    sizes = [block // batch for block in blocks]
    counts = [second.shape[1] // 2 // wide for _, _, second, _ in weights]
    if any(block % LANES for block in blocks):
        return outer_plain(weights, picks, half, batch, wide, add)
    tokens = weights[0][0].shape[1]
    height = sum(e * c for e, c in zip(sizes, counts))
    shape = (batch, height, wide)
    specs = []
    operands = []
    start = 0
    flops = 0
    for (first, first_other, second, second_other), block, count in zip(weights, blocks, counts):
        def rows_at(n, block=block):
            return pl.BlockSpec((block, tokens), lambda u, pick: (pick[n], 0))

        def column_at(u, pick, start=start, count=count):
            return (0, half * count + jnp.clip(u - start, 0, count - 1))

        specs += [rows_at(n) for n in range(chosen)] * 2
        specs += [pl.BlockSpec((tokens, wide), column_at)] * 2
        operands += [first] * chosen + [first_other] * chosen + [second, second_other]
        start += count
        flops += 4 * tokens * chosen * block * count * wide
    whole = pl.BlockSpec(shape, lambda u, pick: (0, 0, 0))
    stacked = pl.BlockSpec((chosen,) + shape, lambda u, pick: (0, 0, 0, 0))
    made = jax.ShapeDtypeStruct((chosen,) + shape, jnp.bfloat16)
    return pl.pallas_call(
        functools.partial(
            outer_kernel, sizes=sizes, counts=counts, batch=batch, chosen=chosen,
            adds=add is not None, extra=len(after),
        ),
        grid_spec=pltpu.PrefetchScalarGridSpec(
            num_scalar_prefetch=1,
            grid=(sum(counts),),
            in_specs=specs
            + ([] if add is None else [stacked])
            + [pl.BlockSpec(memory_space=pl.ANY)] * len(after),
            out_specs=stacked if add is None else [whole] * chosen,
        ),
        out_shape=made if add is None else [jax.ShapeDtypeStruct(shape, jnp.bfloat16)] * chosen,
        compiler_params=pltpu.CompilerParams(vmem_limit_bytes=VMEM),
        cost_estimate=pl.CostEstimate(flops=2 * flops, bytes_accessed=flops // 300, transcendentals=0),
        name="outer",
    )(picks, *operands, *(() if add is None else (add,)), *after)


def merge_kernel(*refs, sums):
    out = refs[-1]
    for z in range(out.shape[0]):
        for h in range(sums):
            total = refs[2 * h][z].astype(jnp.float32) + refs[2 * h + 1][z].astype(jnp.float32)
            out[z, h] = total.astype(jnp.bfloat16)


def merge(pairs, after):
    batch, height, wide = pairs[0][0].shape
    sums = len(pairs)
    shape = (batch, sums, height, wide)
    return pl.pallas_call(
        functools.partial(merge_kernel, sums=sums),
        grid=(1,),
        out_shape=jax.ShapeDtypeStruct(shape, jnp.bfloat16),
        in_specs=[pl.BlockSpec((batch, height, wide), lambda i: (0, 0, 0))] * (2 * sums)
        + [pl.BlockSpec(memory_space=pl.ANY)] * len(after),
        out_specs=pl.BlockSpec(shape, lambda i: (0, 0, 0, 0)),
        cost_estimate=SMALL,
        compiler_params=pltpu.CompilerParams(vmem_limit_bytes=VMEM),
        name="merge",
    )(*[one for pair in pairs for one in pair], *after)


def cut(held, rows):
    groups, _, height, _ = held.shape
    batch = lax.axis_size("batch")
    each = (height - rows) // batch
    piece = held[:, :, rows:].reshape(groups, 3, batch, each, LANES)
    return piece.transpose(2, 3, 1, 0, 4).reshape(batch, each, 3 * groups * LANES)


def finish_kernel(came_ref, *rest, sizes, counts):
    outs = rest[len(rest) - len(sizes) :]
    batch, halves, _, wide = came_ref.shape
    for h in range(halves):
        at = 0
        for out, each, blocks in zip(outs, sizes, counts):
            for j in range(blocks):
                total = came_ref[0, h, at : at + each].astype(jnp.float32)
                for z in range(1, batch):
                    total = total + came_ref[z, h, at : at + each].astype(jnp.float32)
                low = (h * blocks + j) * wide
                out[:, low : low + wide] = total
                at += each


def finish(came, sizes, counts, after):
    vmem = pl.BlockSpec(memory_space=pltpu.VMEM)
    _, halves, _, wide = came.shape
    return pl.pallas_call(
        functools.partial(finish_kernel, sizes=sizes, counts=counts),
        out_shape=[
            jax.ShapeDtypeStruct((each, halves * count * wide), jnp.float32)
            for each, count in zip(sizes, counts)
        ],
        in_specs=[vmem] + [pl.BlockSpec(memory_space=pl.ANY)] * len(after),
        out_specs=[vmem] * len(sizes),
        cost_estimate=SMALL,
        name="finish",
    )(came, *after)


def total_kernel(*refs, count):
    total = refs[0][...].astype(jnp.float32)
    for n in range(1, count):
        total = total + refs[n][...].astype(jnp.float32)
    refs[-1][...] = total


def totalled(pieces, after):
    vmem = pl.BlockSpec(memory_space=pltpu.VMEM)
    return pl.pallas_call(
        functools.partial(total_kernel, count=len(pieces)),
        out_shape=jax.ShapeDtypeStruct(pieces[0].shape, jnp.float32),
        in_specs=[vmem] * len(pieces) + [pl.BlockSpec(memory_space=pl.ANY)] * len(after),
        out_specs=vmem,
        cost_estimate=SMALL,
        name="total",
    )(*pieces, *after)


def tie_kernel(*refs):
    pass


def tie(value, after):
    anywhere = pl.BlockSpec(memory_space=pl.ANY)
    return pl.pallas_call(
        tie_kernel,
        out_shape=jax.ShapeDtypeStruct(value.shape, value.dtype),
        in_specs=[anywhere] * (1 + len(after)),
        out_specs=anywhere,
        input_output_aliases={0: 0},
        name="tie",
    )(value, *after)


def times(first_op, second_op):
    return lax.dot_general(first_op, second_op, NN, preferred_element_type=jnp.float32)


def swap(value, bit):
    size = lax.axis_size("seq")
    return lax.ppermute(value, "seq", [(i, i ^ bit) for i in range(size)])


def ahead(value, step):
    size = lax.axis_size("batch")
    return lax.ppermute(value, "batch", [(i, (i + step) % size) for i in range(size)])


class Sum:
    wide = 512

    def __init__(self, weights, half, bits):
        self.weights, self.half, self.bits = weights, half, bits
        self.seq = lax.axis_size("seq")
        self.batch = lax.axis_size("batch")
        self.next = 1

    def picks(self, sent):
        me = lax.axis_index("seq")
        first = me ^ self.bits[0] if sent else me
        found = [0]
        for bit in self.bits[:0:-1]:
            found = found + [f | bit for f in found]
        return (jnp.array(found, jnp.int32) ^ first).astype(jnp.int32)

    def send(self, after=()):
        sent = outer(self.weights, self.picks(True), self.half, self.batch, self.wide, None, after)
        self.came = swap(sent, self.bits[0])
        return [sent]

    def keep(self, after=()):
        self.total = list(
            outer(self.weights, self.picks(False), self.half, self.batch, self.wide, self.came, after)
        )

    def pass_on(self):
        count = len(self.total) // 2
        sent = self.total[count:]
        self.total = self.total[:count]
        self.came = [swap(one, self.bits[self.next]) for one in sent]
        self.next += 1
        return sent

    def take(self):
        self.total = [
            (a.astype(jnp.float32) + b.astype(jnp.float32)).astype(jnp.bfloat16)
            for a, b in zip(self.total, self.came)
        ]


class Sums:
    def __init__(self, weights, orders):
        self.weights = weights
        self.halves = [Sum(weights, half, bits) for half, bits in enumerate(orders)]

    def send(self, after=()):
        return sum([one.send(after) for one in self.halves], [])

    def came(self):
        return jax.tree.leaves([one.came for one in self.halves])

    def keep(self, after=(), after_last=()):
        for one in self.halves:
            one.keep(tuple(after) + (tuple(after_last) if one is self.halves[-1] else ()))
        return sum([one.pass_on() for one in self.halves], [])

    def spread(self, after=()):
        for one in self.halves:
            while one.next < len(one.bits):
                one.take()
                one.pass_on()
        pieces = merge([(one.total[0], one.came[0]) for one in self.halves], tuple(after))
        self.spread_out = lax.all_to_all(pieces, "batch", 0, 0, tiled=True)
        return [pieces]

    def result(self, after=()):
        devices = lax.axis_size("seq") * lax.axis_size("batch")
        sizes = [first.shape[0] // devices for first, _, _, _ in self.weights]
        counts = [second.shape[1] // 2 // Sum.wide for _, _, second, _ in self.weights]
        return finish(self.spread_out, sizes, counts, tuple(after))


def turn_tables(position):
    half = HD // 2
    lane = jnp.arange(LANES, dtype=jnp.int32)
    rates = jnp.exp((lane % half).astype(jnp.float32) * (-math.log(10000.0) / half))
    angles = position.astype(jnp.float32)[:, None] * rates[None, :]
    side = jnp.where((lane % HD) < half, -1.0, 1.0).astype(jnp.float32)
    return jnp.cos(angles), jnp.sin(angles) * side[None, :]


def all_pieces(value):
    batch = lax.axis_size("batch")
    place = lax.axis_index("batch")
    out = jnp.zeros((batch,) + value.shape, value.dtype)
    out = lax.dynamic_update_index_in_dim(out, value, place, 0)
    for step in range(1, batch):
        out = lax.dynamic_update_index_in_dim(
            out, ahead(value, step), (place - step) % batch, 0
        )
    return out


def all_pieces_for(value):
    batch = lax.axis_size("batch")
    place = lax.axis_index("batch")
    pieces = [
        lax.dynamic_index_in_dim(value, (place + step) % batch, 0, keepdims=False)
        for step in range(batch)
    ]
    return [ahead(piece, step) if step else piece for step, piece in enumerate(pieces)]


def seq_pieces(value, bits):
    have = []
    for bit in bits:
        came = swap(value, bit)
        value = jnp.stack([value, came], axis=sum(b > bit for b in have) if bit > 1 else 0)
        have.append(bit)
    return value.reshape((lax.axis_size("seq"),) + value.shape[len(have) :])


def seq_total(value):
    bit = 1
    while bit < lax.axis_size("seq"):
        value = value + swap(value, bit)
        bit *= 2
    return value


def shards(
    frames_in,
    skip_in,
    time_table,
    timestep,
    lengths,
    span_start,
    span_len,
    skip_proj,
    mod_proj,
    mod_bias,
    qkv_proj,
    out_proj,
    up_proj,
    up_bias,
    down_proj,
    cotangent,
):
    seq = lax.axis_size("seq")
    batch = lax.axis_size("batch")
    seq_at = lax.axis_index("seq")
    batch_at = lax.axis_index("batch")
    device = seq_at * batch + batch_at
    devices = seq * batch
    inputs = frames_in[0]
    skip_rows = skip_in[0]
    rows, width = inputs.shape
    hidden = up_proj.shape[1]
    frames = rows * seq
    heads = HEADS // seq
    utts = lengths.shape[1]

    high = [seq >> (i + 1) for i in range(seq.bit_length() - 2)]
    low = high[::-1]
    rel = (jnp.arange(seq, dtype=jnp.int32) ^ seq_at).astype(jnp.int32)
    spot = (rel & 1) * (seq // 2) + (rel >> 1)
    half = width // 2
    skip_each, qkv_each, out_each, up_each, down_each = (
        skip_proj.shape[0],
        qkv_proj.shape[0],
        out_proj.shape[0],
        up_proj.shape[0],
        down_proj.shape[0],
    )
    per_device = width // seq
    groups = width // LANES
    full_skip = lax.all_gather(all_pieces(skip_proj), "seq", axis=0, tiled=True)
    own_rows = all_pieces(qkv_proj)
    own_qkv = own_rows.reshape(batch, qkv_each, 3, seq, per_device)
    own_qkv = lax.all_to_all(own_qkv.transpose(3, 2, 0, 1, 4), "seq", 0, 0, tiled=True)
    own_qkv = jnp.pad(own_qkv, ((0, 0),) * 4 + ((0, LANES - per_device),))
    own_qkv = own_qkv.transpose(0, 2, 3, 1, 4).reshape(width, 3 * LANES)
    late = jnp.concatenate(
        [down_proj, out_proj]
        + [up_proj[:, p * width : (p + 1) * width] for p in range(hidden // width)],
        axis=0,
    )
    late = lax.all_gather(late, BOTH, axis=0, tiled=False)
    full_qkv = lax.all_gather(own_rows, "seq", axis=0, tiled=True)

    utt_lengths = lengths[0]
    ends = jnp.cumsum(utt_lengths).astype(jnp.int32)
    starts = ends - utt_lengths
    frame_ids = seq_at * rows + jnp.arange(rows, dtype=jnp.int32)
    group_ids = jnp.arange(frames, dtype=jnp.int32)

    def members(ids):
        return (ids[:, None] >= starts[None, :]) & (ids[:, None] < ends[None, :])

    member = members(frame_ids)
    member_int = member.astype(jnp.int32)
    position = frame_ids - jnp.sum(member_int * starts[None, :], axis=1)
    span_first = jnp.sum(member_int * span_start[0][None, :], axis=1)
    span_after = span_first + jnp.sum(member_int * span_len[0][None, :], axis=1)
    in_span = ((position >= span_first) & (position < span_after)).astype(jnp.float32)
    member_rows = member.astype(jnp.float32)
    group_position = group_ids - jnp.sum(members(group_ids).astype(jnp.int32) * starts[None, :], axis=1)
    group_cos, group_sin = turn_tables(group_position)

    steps = all_pieces(timestep[0]).reshape(-1)
    step_pick = (
        steps[:, None] == jnp.arange(time_table.shape[0], dtype=jnp.int32)[None, :]
    ).astype(jnp.float32)
    time_rows = jnp.dot(step_pick, time_table.astype(jnp.float32), precision=highest)
    silu_value, silu_pull = jax.vjp(jax.nn.silu, time_rows)
    time_vec = silu_value.astype(jnp.bfloat16)
    terms = times(time_vec, mod_proj)
    def placed(bias):
        return lax.dynamic_update_slice(
            jnp.zeros((4 * width,), jnp.float32), bias.astype(jnp.float32), (device * bias.shape[0],)
        )

    terms = (terms + placed(mod_bias)[None, :]).reshape(batch, utts, 4 * width)
    up_terms = jnp.broadcast_to(placed(up_bias), (batch, 1, 4 * width))
    terms = jnp.concatenate([terms, up_terms], axis=1)
    modulation = lax.dynamic_index_in_dim(terms, batch_at, 0, keepdims=False)
    for step in range(1, batch):
        modulation = modulation + ahead(
            lax.dynamic_index_in_dim(terms, (batch_at + step) % batch, 0, keepdims=False), step
        )
    modulation = seq_total(modulation)
    full_bup = modulation[utts:]
    modulation = modulation[:utts]
    info = jnp.pad(member_rows, ((0, 0), (0, LANES - utts)))
    branch = (cotangent[0].astype(jnp.float32) * in_span[:, None]).astype(jnp.bfloat16)
    joined = jnp.concatenate([inputs.T, skip_rows.T], axis=0)
    branch_pair = (branch, swap(branch, 1))
    joined_pair = (joined, swap(joined, 1))

    stream_in, *normed_one = front(
        inputs, skip_rows, info, modulation, full_skip, utts,
        (group_cos, group_sin, own_qkv, branch_pair[1], joined_pair[1]),
    )
    normed_halves = [seq_pieces(normed_one[0], low + [1]), seq_pieces(normed_one[1], high + [1])]
    held = project(spot, normed_halves, own_qkv, group_cos, group_sin, ())
    head_out, log_sums = attend(held, ends, heads, 1536, 1536)
    att = lax.all_to_all(
        head_out.reshape(seq, rows, LANES)[:, :, :per_device], "seq", 0, 0, tiled=True
    )
    if per_device < LANES:
        att = att.reshape(groups, 2, rows, per_device).transpose(0, 2, 1, 3).reshape(groups, rows, LANES)

    result, attended, normed_two, activated, grad_pre, grad_mid, grad_low, back, mod_two, bup_terms = middle(
        att, stream_in, info, modulation, branch, late, down_each, out_each, up_each, full_bup, utts
    )
    if per_device < LANES:
        back = back.reshape(groups, rows, 2, per_device).transpose(0, 2, 1, 3).reshape(seq, rows, per_device)
        back = jnp.pad(back, ((0, 0), (0, 0), (0, LANES - per_device)))
    back = lax.all_to_all(back, "seq", 0, 0, tiled=True).reshape(frames, LANES)

    def pairs(first, second):
        return (first[0], first[1], second[0], second[1])

    def pair(value):
        return (value, swap(value, 1))

    first_weights = [
        pairs(pair(activated), branch_pair),
        pairs(pair(normed_two), pair(grad_pre)),
        pairs(pair(attended), pair(grad_low)),
    ]
    sums = Sums(first_weights, (low, high))
    waits = sums.send()

    grad_held = attend_back(
        held, back, head_out, log_sums, group_cos, group_sin, ends, heads, waits + [full_qkv], 1024, 1024
    )
    grad_held = outgoing(spot, grad_held, normed_halves, tuple(sums.came()))
    mark = (grad_held,)
    grad_held = lax.all_to_all(grad_held[..., :per_device], "seq", 0, 0, tiled=True)
    if per_device < LANES:
        grad_held = grad_held.reshape(groups, 2, 3, -1, per_device).transpose(0, 2, 3, 1, 4)
        grad_held = grad_held.reshape(groups, 3, -1, LANES)
    sums.keep(mark)
    waits = sums.spread()

    grad_stream, row_sums = tail(
        grad_held, stream_in, info, modulation, grad_mid, full_qkv, qkv_each,
        mod_two, bup_terms, utts, waits,
    )
    last_sums = Sums([pairs(joined_pair, pair(grad_stream))], (low, high))
    row_sums = row_sums + swap(row_sums, 1)
    waits = last_sums.send((row_sums,))
    grad_inputs, grad_skip_rows = unjoin(grad_stream, full_skip, skip_each, waits)
    waits = last_sums.keep((grad_inputs,))
    row_sums = tie(row_sums, waits)
    for bit in low:
        row_sums = row_sums + swap(row_sums, bit)
    qkv_came = all_pieces_for(cut(tie(grad_held, waits), rows))
    waits = last_sums.spread((row_sums, sums.spread_out))
    row_sums = all_pieces(tie(row_sums, waits))
    grad_down, grad_up, grad_out_w = sums.result(waits)
    grad_qkv_w = totalled(qkv_came, (last_sums.spread_out,))
    (grad_skip_w,) = last_sums.result()

    grad_modulation = row_sums[:, :utts].reshape(batch * utts, 4 * width)
    grad_bup = lax.dynamic_slice_in_dim(
        jnp.sum(row_sums[:, utts], axis=0), device * up_bias.shape[0], up_bias.shape[0]
    )
    grad_bmod = lax.dynamic_slice_in_dim(
        jnp.sum(grad_modulation, axis=0), device * mod_bias.shape[0], mod_bias.shape[0]
    )
    grad_mod_w = jnp.dot(time_vec.astype(jnp.float32).T, grad_modulation, precision=highest)
    grad_time_vec = jnp.dot(grad_modulation, mod_proj.astype(jnp.float32).T, precision=highest)
    grad_table = jnp.dot(step_pick.T, silu_pull(grad_time_vec)[0], precision=highest)
    return (
        result[None],
        grad_inputs[None],
        grad_skip_rows[None],
        grad_table,
        grad_skip_w,
        grad_mod_w,
        grad_bmod,
        grad_qkv_w,
        grad_out_w,
        grad_up,
        grad_bup,
        grad_down,
    )


def solution(mesh):
    return jax.shard_map(
        shards,
        mesh=mesh,
        in_specs=(
            P("batch", "seq", None),
            P("batch", "seq", None),
            P(None, BOTH),
            P("batch", None),
            P("batch", None),
            P("batch", None),
            P("batch", None),
            P(BOTH, None),
            P(BOTH, None),
            P(BOTH),
            P(BOTH, None),
            P(BOTH, None),
            P(BOTH, None),
            P(BOTH),
            P(BOTH, None),
            P("batch", "seq", None),
        ),
        out_specs=(
            P("batch", "seq", None),
            P("batch", "seq", None),
            P("batch", "seq", None),
            P(None, BOTH),
            P(BOTH, None),
            P(BOTH, None),
            P(BOTH),
            P(BOTH, None),
            P(BOTH, None),
            P(BOTH, None),
            P(BOTH),
            P(BOTH, None),
        ),
        check_vma=False,
    )
```
